32 devices in a mesh: dp: 8 (over z, x), seq: 4 (over y, core).
Axes of the slice: x: 2, y: 2, z: 4, core: 2. Of those that a mesh axis runs over, the one named last changes fastest.
Arguments:
- src_input: bfloat16 [8, 1024, 512], P('dp', 'seq'), may hold values from -6 to 6
- tgt_input: bfloat16 [8, 1024, 512], P('dp', 'seq'), may hold values from -6 to 6
- out_cotangent: bfloat16 [8, 1024, 512], P('dp', 'seq'), may hold values from -6 to 6
- src_lengths: int32 [8, 4], P('dp'), may hold values from 1 to 769, 1024 in all within a row
- tgt_lengths: int32 [8, 4], P('dp'), may hold values from 1 to 769, 1024 in all within a row
- enc_expert: int32 [8, 1], P('dp'), may hold values from 0 to 3
- dec_expert: int32 [8, 1], P('dp'), may hold values from 0 to 3
- norm_gains: bfloat16 [5, 512], P(None, 'dp'), may hold values from 0.5 to 1.5
- norm_biases: bfloat16 [5, 512], P(None, 'dp'), may hold values from -3 to 3
- qkv_weight: bfloat16 [3, 3, 512, 512], P(None, None, 'dp', 'seq'), may hold values from -0.25 to 0.25
- out_weight: bfloat16 [3, 512, 512], P(None, 'seq', 'dp'), may hold values from -0.5 to 0.5
- expert_up: bfloat16 [2, 4, 512, 2048], P(None, None, 'dp', 'seq'), may hold values from -0.25 to 0.25
- expert_down: bfloat16 [2, 4, 2048, 512], P(None, None, 'seq', 'dp'), may hold values from -0.125 to 0.125
Outputs:
- decoder_output: float32 [8, 1024, 512], P('dp', 'seq')
- src_grad: float32 [8, 1024, 512], P('dp', 'seq')
- tgt_grad: float32 [8, 1024, 512], P('dp', 'seq')
- gain_grad: float32 [5, 512], P(None, 'dp')
- bias_grad: float32 [5, 512], P(None, 'dp')
- qkv_grad: float32 [3, 3, 512, 512], P(None, None, 'dp', 'seq')
- out_grad: float32 [3, 512, 512], P(None, 'seq', 'dp')
- up_grad: float32 [2, 4, 512, 2048], P(None, None, 'dp', 'seq')
- down_grad: float32 [2, 4, 2048, 512], P(None, None, 'seq', 'dp')
- sublayer_rms: float32 [8, 2, 5], P('dp')
The draws below stay inside these ranges and needn't reach their ends.
Inputs may be any that keep to these rules, and one draw needn't show every extreme that they name: `src_lengths`: each row's 4 source lengths sum to 1024; the longest is 769. `tgt_lengths`: each row's 4 target lengths sum to 1024; the longest is 769.
All inputs are finite; a program needn't handle non-finite values.
Results may differ from the reference program's by a relative error of at most 0.024.
Values may be sent and summed in bfloat16 or wider, within the bound.
A program may use at most 192 MiB of HBM per device.

```python
import math
import jax
import jax.numpy as jnp
import numpy as np
from jax import lax

D = 512
HEAD_DIM = 64
FF = 2048
EXPERTS = 4
SEQ_LEN = 1024
DOCS = 4
GROUP = 256
ROWS = 8


def block_levels(own_key, extent, cuts, least, top_value):
    level, own = 1.0, jax.random.fold_in(own_key, 6)
    for dim, shards_of in cuts:
        draws = jnp.exp(jax.random.uniform(jax.random.fold_in(own, dim), (shards_of,), jnp.float32, least / len(cuts), top_value / len(cuts)))
        level = level * jnp.repeat(draws, extent[dim] // shards_of).reshape([-1 if axis == dim else 1 for axis in range(len(extent))])
    return level


def picks_of(rng, rows, number_of, top, lift):
    order = jax.random.permutation(jax.random.fold_in(rng, 1), number_of)
    pull = order
    for power in range(3):
        pull = pull * pull // number_of
    pull = pull * lift // number_of
    chance = jax.random.randint(jax.random.fold_in(rng, 2), (rows, number_of), 0, 4096) + pull
    sure = jax.random.permutation(jax.random.fold_in(rng, 3), rows)[jnp.arange(number_of) % rows]
    chance = jnp.where(jnp.arange(rows)[:, None] == sure[None, :], 1 << 14, chance)
    score = chance * number_of + jnp.arange(number_of)
    return lax.top_k(score.astype(jnp.int32), top)[1].astype(jnp.int32)


def length_profile(number_of, total, bound, slope):
    weights = [(1 << 20) // math.isqrt(rank ** slope) + 1 for rank in range(2, number_of + 1)]
    surplus, counts = total - bound - (number_of - 1), [1] * (number_of - 1)
    while surplus > 0:
        free = [i for i in range(number_of - 1) if counts[i] < bound]
        mass, budget = sum([weights[i] for i in free]), surplus
        for i in free:
            more = min(bound - counts[i], max(1, budget * weights[i] // mass), surplus)
            counts[i] = counts[i] + more
            surplus = surplus - more
    return np.array([bound] + counts)


def uneven(stream_key, amount, total, most, skew):
    if amount == 2:
        one = jax.random.randint(stream_key, (), max(1, total - most), min(most, total - 1) + 1)
        return jnp.stack([one, total - one])
    tallies = jnp.asarray(length_profile(amount, total, most, skew), jnp.int32)
    pairs = (amount - 1) // 2
    giver, receiver = tallies[1:1 + 2 * pairs:2], tallies[2:2 + 2 * pairs:2]
    slack = jnp.minimum(giver - 1, most - receiver)
    shifted = jax.random.randint(jax.random.fold_in(stream_key, 1), (pairs,), 0, 1 << 20) % (slack + 1)
    tallies = tallies.at[1:1 + 2 * pairs:2].set(giver - shifted).at[2:2 + 2 * pairs:2].set(receiver + shifted)
    return tallies[jax.random.permutation(jax.random.fold_in(stream_key, 2), amount)]


def normal_values(stream_key, dims, spread, limit, split=(), held_as=jnp.bfloat16):
    drawn = jax.random.normal(stream_key, dims, jnp.float32) * spread
    if len(split) > 0:
        drawn = block_levels(stream_key, dims, split, -0.22, 0.18) * drawn
    return jnp.clip(drawn, min=-limit, max=limit).astype(held_as)


def setup_inputs(seed: int = 0) -> dict:
    seeds = jax.random.split(jax.random.key(seed), 14)
    return {
        "src_input": normal_values(seeds[0], (ROWS, SEQ_LEN, D), 1.0, 6.0, ((0, 8), (1, 4))),
        "tgt_input": normal_values(seeds[1], (ROWS, SEQ_LEN, D), 1.0, 6.0, ((0, 8), (1, 4))),
        "out_cotangent": normal_values(seeds[2], (ROWS, SEQ_LEN, D), 1.0, 6.0, ((0, 8), (1, 4))),
        "src_lengths": jax.vmap(lambda own: uneven(own, DOCS, SEQ_LEN, 3 * GROUP + 1, 1))(jax.random.split(seeds[3], ROWS)).reshape((ROWS, DOCS)).astype(jnp.int32),
        "tgt_lengths": jax.vmap(lambda own: uneven(own, DOCS, SEQ_LEN, 3 * GROUP + 1, 1))(jax.random.split(seeds[4], ROWS)).reshape((ROWS, DOCS)).astype(jnp.int32),
        "enc_expert": picks_of(seeds[5], ROWS, EXPERTS, 1, 4096),
        "dec_expert": picks_of(seeds[6], ROWS, EXPERTS, 1, 4096),
        "norm_gains": jnp.clip(1.0 + 0.1 * jax.random.normal(seeds[7], (5, D), jnp.float32), 0.5, 1.5).astype(jnp.bfloat16),
        "norm_biases": normal_values(seeds[8], (5, D), 0.2, 3.0, ((1, 8),)),
        "qkv_weight": normal_values(seeds[9], (3, 3, D, D), D ** -0.5, 0.25, ((2, 8), (3, 4))),
        "out_weight": normal_values(seeds[10], (3, D, D), (D // 4) ** -0.5, 0.5, ((1, 4), (2, 8))),
        "expert_up": normal_values(seeds[11], (2, EXPERTS, D, FF), D ** -0.5, 0.25, ((2, 8), (3, 4))),
        "expert_down": normal_values(seeds[12], (2, EXPERTS, FF, D), FF ** -0.5, 0.125, ((2, 4), (3, 8))),
    }


@jax.custom_vjp
def low(v):
    return lax.optimization_barrier(v.astype(jnp.bfloat16)).astype(jnp.float32)

@jax.custom_vjp
def low_back(v):
    return v

def low_keep(v):
    return (low(v), None)

def low_pass(kept, grad):
    return (grad,)

def back_keep(v):
    return (v, None)

def back_low(kept, grad):
    return (low(grad),)
low.defvjp(low_keep, low_pass)
low_back.defvjp(back_keep, back_low)
EPSILON = 1e-05
MASKED = -1e+30

def normalize(values, gain, shift):
    average = lax.optimization_barrier(jnp.mean(values, -1, keepdims=True))
    centered = values - average
    variance = lax.optimization_barrier(jnp.mean(centered * centered, -1, keepdims=True))
    return centered * lax.rsqrt(variance + EPSILON) * gain + shift

def segment_ids(lengths, length):
    bounds = jnp.cumsum(lengths, -1)
    places = jnp.arange(length, dtype=jnp.int32)[:, None]
    return lax.optimization_barrier(jnp.sum((places >= bounds[..., None, :]).astype(jnp.int32), -1))

def attend(query_rows, key_rows, weights, out_w, seg_query, seg_key, causal):
    highest = lax.Precision.HIGHEST
    query = low(low_back(jnp.dot(query_rows, weights[0], precision=highest)))
    keys = low(low_back(jnp.dot(key_rows, weights[1], precision=highest)))
    values = low(low_back(jnp.dot(key_rows, weights[2], precision=highest)))
    length = query.shape[0]
    heads_query = query.reshape(length, -1, HEAD_DIM)
    heads_key = keys.reshape(length, -1, HEAD_DIM)
    heads_value = values.reshape(length, -1, HEAD_DIM)
    scores = low_back(jnp.einsum('qhd,khd->hqk', heads_query, heads_key, precision=highest) * HEAD_DIM ** (-0.5))
    allowed = seg_query[:, None] == seg_key[None, :]
    if causal:
        places = jnp.arange(length)
        allowed = allowed & (places[:, None] >= places[None, :])
    scores = jnp.where(allowed[None], scores, MASKED)
    probs = low(jax.nn.softmax(scores, -1))
    mixed = jnp.einsum('hqk,khd->qhd', probs, heads_value, precision=highest).reshape(length, -1)
    mixed = low(low_back(mixed))
    return low_back(jnp.dot(mixed, out_w, precision=highest))

def expert_ffn(rows, w_up, w_down):
    highest = lax.Precision.HIGHEST
    hidden = low_back(jnp.dot(rows, w_up, precision=highest))
    active = low(jax.nn.gelu(hidden))
    return low_back(jnp.dot(active, w_down, precision=highest))

def root_mean(values):
    return jnp.sqrt(jnp.mean(values * values))

def row_layers(params, row_src, row_tgt, len_src, len_tgt, pick_enc, pick_dec):
    gains, shifts, projections, outputs, ups, downs = params
    length = row_src.shape[0]
    seg_src = segment_ids(len_src, length)
    seg_tgt = segment_ids(len_tgt, length)
    normed = low(normalize(row_src, gains[0], shifts[0]))
    branch_one = attend(normed, normed, projections[0], outputs[0], seg_src, seg_src, False)
    src_mid = row_src + branch_one
    normed = low(normalize(src_mid, gains[1], shifts[1]))
    branch_two = expert_ffn(normed, ups[0, pick_enc], downs[0, pick_enc])
    memory = src_mid + branch_two
    memory_rows = low(memory)
    normed = low(normalize(row_tgt, gains[2], shifts[2]))
    branch_three = attend(normed, normed, projections[1], outputs[1], seg_tgt, seg_tgt, True)
    tgt_one = row_tgt + branch_three
    normed = low(normalize(tgt_one, gains[3], shifts[3]))
    branch_four = attend(normed, memory_rows, projections[2], outputs[2], seg_tgt, seg_src, False)
    tgt_two = tgt_one + branch_four
    normed = low(normalize(tgt_two, gains[4], shifts[4]))
    branch_five = expert_ffn(normed, ups[1, pick_dec], downs[1, pick_dec])
    residuals = jnp.stack([root_mean(row_src), root_mean(src_mid), root_mean(row_tgt), root_mean(tgt_one), root_mean(tgt_two)])
    branches = jnp.stack([root_mean(branch_one), root_mean(branch_two), root_mean(branch_three), root_mean(branch_four), root_mean(branch_five)])
    return (tgt_two + branch_five, jnp.stack([residuals, branches]))

def reference(src_input, tgt_input, out_cotangent, src_lengths, tgt_lengths, enc_expert, dec_expert, norm_gains, norm_biases, qkv_weight, out_weight, expert_up, expert_down):
    params = (norm_gains.astype(jnp.float32), norm_biases.astype(jnp.float32), qkv_weight.astype(jnp.float32), out_weight.astype(jnp.float32), expert_up.astype(jnp.float32), expert_down.astype(jnp.float32))
    source = src_input.astype(jnp.float32)
    target = tgt_input.astype(jnp.float32)

    def forward(weights, sources, targets):

        def per_row(items):
            row_src, row_tgt, len_src, len_tgt, pick_enc, pick_dec = items
            return row_layers(weights, row_src, row_tgt, len_src, len_tgt, pick_enc[0], pick_dec[0])
        return lax.map(jax.checkpoint(per_row), (sources, targets, src_lengths, tgt_lengths, enc_expert, dec_expert))
    output, pullback, stats = jax.vjp(forward, params, source, target, has_aux=True)
    param_grads, source_grad, target_grad = pullback(out_cotangent.astype(jnp.float32))
    return (output, source_grad, target_grad, param_grads[0], param_grads[1], param_grads[2], param_grads[3], param_grads[4], param_grads[5], stats)
```

```python
import functools
import math
from types import SimpleNamespace

import jax
import jax.numpy as jnp
from jax import lax
from jax.experimental import pallas as pl
from jax.experimental.pallas import tpu as pltpu
from jax.sharding import PartitionSpec as P

HEAD_DIM = 64
EPSILON = 1e-05
MASKED = -1e30
LANES = 128
F32 = jnp.float32
BF16 = jnp.bfloat16
MESH = pl.DeviceIdType.MESH
GELU_A = math.sqrt(2.0 / math.pi)
GELU_B = 0.044715


def mm(a, b):
    return lax.dot_general(a, b, (((1,), (0,)), ((), ())), preferred_element_type=F32)


def mm_nt(a, b):
    return lax.dot_general(a, b, (((1,), (1,)), ((), ())), preferred_element_type=F32)


def mm_tn(a, b):
    return lax.dot_general(a, b, (((0,), (0,)), ((), ())), preferred_element_type=F32)


def centre(x):
    mean = jnp.mean(x, -1, keepdims=True)
    xc = x - mean
    var = jnp.mean(xc * xc, -1, keepdims=True)
    scale = lax.rsqrt(var + EPSILON)
    return xc * scale, scale


def norm(x, gain, shift):
    return centre(x)[0] * gain + shift


def norm_back(x, gain, up):
    xh, scale = centre(x)
    dgain = jnp.sum(up * xh, 0, keepdims=True)
    dbias = jnp.sum(up, 0, keepdims=True)
    dxh = up * gain
    m1 = jnp.mean(dxh, -1, keepdims=True)
    m2 = jnp.mean(dxh * xh, -1, keepdims=True)
    return scale * (dxh - m1 - xh * m2), dgain, dbias


def gelu_pair(x):
    square = x * x
    t = jnp.tanh(x * (GELU_A + (GELU_A * GELU_B) * square))
    half = 0.5 + 0.5 * t
    slope = half + (0.5 * x) * (1.0 - t * t) * (GELU_A + (3.0 * GELU_A * GELU_B) * square)
    return x * half, slope


def scratch_list(n, nb, cw, B, D, FQ):
    L, F2, KW = 4 * B, 2 * FQ, 2 * LANES

    def b(*shape):
        return pltpu.VMEM(shape, BF16)

    def f(*shape):
        return pltpu.VMEM(shape, F32)

    return dict(
        xrow=b(L, D),
        oth=b(B, D),
        nrow=b(L, D),
        wself=b(2, 4, D, KW),
        wx=b(4, D, KW),
        we0=b(2, D, F2),
        we1=b(2, D, F2),
        sendA=b(3, 4, cw, LANES),
        gtab=f(16, D),
        smallr=f(nb, 16, LANES),
        q=b(L, KW),
        k=b(L, KW),
        v=b(L, KW),
        o=b(L, KW),
        lseT=f(8, L),
        bias=f(B, L),
        biasT=f(L, B),
        part=f(2, B, D),
        cs=b(2, B, D),
        cr=b(2, B, D),
        mid=f(2, B, D),
        n2row=b(L, D),
        g0=b(L, F2),
        gp0=b(L, F2),
        mrow=b(L, D),
        fs=b(B, D),
        fr=b(B, D),
        t1=f(B, D),
        n4c=b(2 * B, D),
        q2=b(2 * B, KW),
        k2=b(L, KW),
        v2=b(L, KW),
        o2=b(2 * B, KW),
        lse2T=f(8, 2 * B),
        ds=b(B, D),
        dr=b(2, B, D),
        t2=f(B, D),
        n5c=b(2 * B, D),
        g1=b(2 * B, F2),
        gp1=b(2 * B, F2),
        b5c=b(2 * B, D),
        g4=f(B, D),
        b4c=b(2 * B, D),
        dqf=f(B, KW),
        dkf=f(L, KW),
        dvf=f(L, KW),
        dkb=b(L, KW),
        dvb=b(L, KW),
        drow=f(16, B),
        dmr=b(2, B, D),
        g3=f(B, D),
        brow=b(L, D),
        dmem=f(2, B, D),
        be=b(L, D),
        dq=b(L, KW),
        gA=b(4, D, KW),
        gE=b(2, D, F2),
        ylX=b(4, D, LANES),
        ylE1=b(2, D, FQ),
        qA=b(3, 4, D, LANES),
        qE=b(2, 2, D, FQ),
        dpA=b(3, nb, 4, cw, LANES),
        dpE=b(2, nb, 2, cw, FQ),
        acc=f(32, D),
        acc1=f(32, D),
        acc2=f(32, D),
        accc=f(32, D),
        accy=f(32, D),
        accd=f(nb, 16, LANES),
    )


def sem_list(nb):
    counts = dict(
        in_y=1,
        in_c=2,
        cot=1,
        small=nb,
        wself=2 * nb,
        wx=nb,
        we0=nb,
        we1=nb,
        wy_self=nb,
        wy_x=nb,
        wy_e0=nb,
        wy_e1=nb,
        rs1=2,
        n2=2,
        rs2=2,
        br3=1,
        m_y=2,
        m_c=2,
        n4=1,
        rs4=1,
        n5=1,
        rs5=1,
        rs6=1,
        b4=1,
        rs7q=1,
        rs7m=2,
        dm=2,
        g3=1,
        brow=2,
        be=2,
        rs8=2,
        rs9=2,
        fin=1,
        gy_s=1,
        gy_x=1,
        gy_e0=1,
        gy_e1=1,
        gd_a=3 * nb,
        gd_e=2 * nb,
        accc=1,
        accy=1,
        accd=nb,
    )
    base, at = {}, 0
    for name, number in counts.items():
        base[name] = at
        at = at + number
    return SimpleNamespace(**base), at


def step_kernel(cfg, names, *refs):
    n, nb, cw, B, D, FQ, E, inside = cfg
    L, F2, KW = 4 * B, 2 * FQ, 2 * LANES
    R = SimpleNamespace(**dict(zip(names, refs, strict=True)))
    K, _ = sem_list(nb)

    dp = lax.axis_index("dp")
    me = dp if inside else 0
    s = lax.axis_index("seq")
    h = lax.div(s, 2)
    c = lax.rem(s, 2)
    cp = 1 - c
    core = (dp, s + 1 - 2 * c)
    ypeer = (dp, s + 2 - 4 * h)
    is_a, is_b = h == 0, h == 1

    def rows(i, size=B):
        return pl.ds(pl.multiple_of(i * size, size), size)

    def lanes(i, size=LANES):
        return pl.ds(pl.multiple_of(i * size, size), size)

    def send(src, dst, name, to, i=0, j=None):
        return pltpu.make_async_remote_copy(
            src_ref=src,
            dst_ref=dst,
            send_sem=R.ss.at[name + i],
            recv_sem=R.rs.at[name + (i if j is None else j)],
            device_id=to,
            device_id_type=MESH,
        )

    def arrived(dst, name, i=0):
        send(dst, dst, name, core, i).wait_recv()

    def sent(src, name, i=0):
        send(src, src, name, core, i).wait_send()

    def loop(count, body, start=0):
        def step(i, carry):
            body(i)
            return carry

        lax.fori_loop(start, count, step, 0)

    def peer_of(i):
        return lax.rem(me + i, nb)

    barrier = pltpu.get_barrier_semaphore()
    for to in (core, ypeer):
        pl.semaphore_signal(barrier, inc=1, device_id=to, device_id_type=MESH)

    def greet(i):
        pl.semaphore_signal(barrier, inc=1, device_id=(peer_of(i), s), device_id_type=MESH)

    loop(nb, greet, 1)
    pl.semaphore_wait(barrier, nb + 1)

    small = R.small

    def small_copy(to, frm):
        return send(small, R.smallr.at[me], K.small, (to, s), to, me)

    if inside:
        loop(nb, lambda i: small_copy(peer_of(i), me).start(), 1)

    @pl.when(is_a)
    def _():
        R.xrow[rows(s)] = R.src[...]
        R.oth[...] = R.tgt[...]

    @pl.when(is_b)
    def _():
        R.xrow[rows(s)] = R.tgt[...]
        R.oth[...] = R.src[...]

    sy = s + 2 - 4 * h
    send(R.oth, R.xrow.at[rows(s)], K.in_y, ypeer).start()
    send(R.xrow.at[rows(s)], R.xrow.at[rows(s)], K.in_c, core, 0).start()
    R.b5c[rows(c)] = R.cot[...]
    send(R.b5c.at[rows(c)], R.b5c.at[rows(c)], K.cot, core).start()

    def wblock(buf, p, half, width):
        return buf.at[:, rows(p, cw), lanes(half, width)]

    def a_copy(buf, a, name, k, idx):
        p = peer_of(k)
        return send(R.sendA.at[a], wblock(buf, me, h, LANES), name, (p, s), idx + p, idx + me)

    def e_copy(l, name, k):
        p = peer_of(k)
        return send(wblock(R.gE, p, l, FQ), wblock((R.we0, R.we1)[l], me, h, FQ), name, (p, s), p, me)

    for a in range(3):
        if inside:
            for j in range(3):
                R.sendA[a, j] = R.qkv[a, j]
            R.sendA[a, 3] = R.wot[a]
        buf = R.wself.at[a] if a < 2 else R.wx
        piece = R.sendA if inside else R.wa
        for j in range(4):
            buf[j, rows(me, cw), lanes(h)] = piece[a, j]
    if inside:
        for a in range(2):
            loop(nb, lambda i, a=a: a_copy(R.wself.at[a], a, K.wself, i, a * nb).start(), 1)

    arrived(R.xrow.at[rows(sy)], K.in_y)
    send(R.xrow.at[rows(sy)], R.xrow.at[rows(sy)], K.in_c, core, 1).start()

    if inside:
        loop(nb, lambda i: arrived(R.smallr.at[0], K.small, peer_of(i)), 1)
        R.smallr[pl.ds(me, 1)] = small[...][None]
        per = LANES // cw
        for t in range(D // LANES):
            tile = R.smallr[t * per]
            for k in range(1, per):
                tile = tile + R.smallr[t * per + k]
            R.gtab[:, t * LANES:(t + 1) * LANES] = tile

        def chosen(p):
            for l in range(2):
                row = R.smallr[p, pl.ds(10 + l, 1), :]
                for m, held in enumerate((R.up, R.dnt)):
                    total = None
                    for e in range(E):
                        hit = jnp.where(row == float(e), 1.0, 0.0)
                        hit = jnp.concatenate([hit] * (FQ // LANES), axis=1)
                        term = held[l, e].astype(F32) * hit
                        total = term if total is None else total + term
                    R.gE[m, rows(p, cw), lanes(l, FQ)] = total.astype(BF16)

        loop(nb, chosen)
        for l in range(2):
            for m in range(2):
                (R.we0, R.we1)[l][m, rows(me, cw), lanes(h, FQ)] = R.gE[m, rows(me, cw), lanes(l, FQ)]
    else:
        R.gtab[...] = small[...]
        for l in range(2):
            for m in range(2):
                (R.we0, R.we1)[l][m, rows(me, cw), lanes(h, FQ)] = R.we[l, m]

    def forward(buf, name_in, base_in, name_y, width):
        def one(i):
            p = peer_of(i)
            if inside:

                @pl.when(i > 0)
                def _():
                    arrived(wblock(buf, p, h, width), name_in, base_in + p)

            send(wblock(buf, p, h, width), wblock(buf, p, h, width), name_y, ypeer, p).start()

        loop(nb, one)

    def own_arrived(buf, name_in, base_in, width):
        if inside:
            loop(nb, lambda i: arrived(wblock(buf, peer_of(i), h, width), name_in, base_in + peer_of(i)), 1)

    def y_arrived(buf, name_y, width):
        loop(nb, lambda i: arrived(wblock(buf, peer_of(i), 1 - h, width), name_y, peer_of(i)))

    def y_sent(buf, name_y, width):
        loop(nb, lambda i: sent(wblock(buf, peer_of(i), h, width), name_y, peer_of(i)))

    other = R.wself.at[1 - h]
    forward(other, K.wself, (1 - h) * nb, K.wy_self, LANES)
    own_arrived(R.wself.at[h], K.wself, h * nb, LANES)
    if inside:
        loop(nb, lambda i: e_copy(0, K.we0, i).start(), 1)
        loop(nb, lambda i: a_copy(R.wx, 2, K.wx, i, 0).start(), 1)
    y_arrived(R.wself.at[h], K.wy_self, LANES)

    R.acc[...] = jnp.zeros((32, D), F32)

    def tally(row, x):
        R.acc[pl.ds(row, 1), :] += jnp.sum(x, 0, keepdims=True)

    def gain(i):
        return R.gtab[pl.ds(i, 1), :]

    def shift(i):
        return R.gtab[pl.ds(5 + i, 1), :]

    def blk(j):
        return c + 2 * j

    def pblk(j):
        return cp + 2 * j

    def documents(lens, position):
        total = jnp.zeros(position.shape, F32)
        edge = 0
        for k in range(lens.shape[1]):
            edge = edge + lens[0, k]
            total = total + jnp.where(position >= edge, 1.0, 0.0)
        return total

    class Lengths:
        def __init__(self, pick):
            self.pick, self.shape = pick, R.slen.shape

        def __getitem__(self, at):
            return self.pick(at)

    src_lens = Lengths(lambda at: R.slen[at])
    tgt_lens = Lengths(lambda at: R.tlen[at])
    self_lens = Lengths(lambda at: jnp.where(is_a, R.slen[at], R.tlen[at]))

    def set_bias(buf, q_start, q_lens, k_lens, causal, q_axis):
        shape = (B, L) if q_axis == 0 else (L, B)
        thin_q = (B, 1) if q_axis == 0 else (1, B)
        thin_k = (1, L) if q_axis == 0 else (L, 1)
        q_pos = lax.broadcasted_iota(jnp.int32, thin_q, q_axis) + q_start
        k_pos = lax.broadcasted_iota(jnp.int32, thin_k, 1 - q_axis)
        same = documents(q_lens, q_pos) == documents(k_lens, k_pos)
        out = jnp.where(same, 0.0, MASKED)
        if causal is not None:
            limit = q_pos + jnp.where(causal, 0, L)
            out = jnp.where(k_pos <= limit, out, MASKED)
        buf[...] = jnp.broadcast_to(out, shape)

    lane_head = lax.div(lax.broadcasted_iota(jnp.int32, (1, KW), 1), HEAD_DIM)

    def head_row(hd):
        return jnp.where(lane_head == hd, 1.0, 0.0)

    heads = KW // HEAD_DIM

    def attend(q_blk, k_ref, v_ref):
        lane = lax.broadcasted_iota(jnp.int32, (1, LANES), 1)
        out = jnp.zeros((B, KW), F32)
        lse = jnp.zeros((B, LANES), F32)
        for hd in range(heads):
            hrow = head_row(hd)
            scores = mm_nt(q_blk * hrow.astype(BF16), k_ref[...]) + R.bias[...]
            top = jnp.max(scores, -1, keepdims=True)
            expos = jnp.exp(scores - top)
            total = jnp.sum(expos, -1, keepdims=True)
            out = out + mm(expos.astype(BF16), v_ref[...]) * (hrow / total)
            lse = lse + jnp.where(lane == hd, top + jnp.log(total), 0.0)
        return out.astype(BF16), jnp.transpose(lse)[0:8, :]

    def attend_back(q_blk, o_blk, do_blk, lse_ref, at, k_ref, v_ref):
        prod = do_blk.astype(F32) * o_blk.astype(F32)
        high = prod.astype(BF16)
        low = (prod - high.astype(F32)).astype(BF16)
        pick = lax.broadcasted_iota(jnp.int32, (16, KW), 0) == jnp.broadcast_to(lane_head, (16, KW))
        pick = jnp.where(pick, 1.0, 0.0).astype(BF16)
        R.drow[...] = mm_nt(pick, high) + mm_nt(pick, low)
        R.dqf[...] = jnp.zeros((B, KW), F32)

        def head(hd):
            hrow = head_row(hd)
            qm = q_blk * hrow.astype(BF16)
            dom = do_blk * hrow.astype(BF16)
            probs = jnp.exp(mm_nt(k_ref[...], qm) + R.biasT[...] - lse_ref[pl.ds(hd, 1), at])
            R.dvf[...] += mm(probs.astype(BF16), dom)
            change = probs * (mm_nt(v_ref[...], dom) - R.drow[pl.ds(hd, 1), :])
            change = change.astype(BF16)
            R.dkf[...] += mm(change, qm)
            R.dqf[...] += mm_tn(change, k_ref[...]) * hrow

        loop(heads, head)
        return R.dqf[...]

    scale = HEAD_DIM ** (-0.5)

    loop(2, lambda j: arrived(R.xrow.at[rows(pblk(j))], K.in_c, lax.rem(j + h, 2)))

    def self_project(i):
        x = R.xrow[rows(i)].astype(F32)
        y = norm(x, gain(2 * h), shift(2 * h)).astype(BF16)
        R.nrow[rows(i)] = y
        R.q[rows(i)] = mm(y, R.wself[h, 0]).astype(BF16) * jnp.asarray(scale, BF16)
        R.k[rows(i)] = mm(y, R.wself[h, 1]).astype(BF16)
        R.v[rows(i)] = mm(y, R.wself[h, 2]).astype(BF16)

    loop(4, self_project)

    def self_block(i):
        j = lax.rem(i, 2)
        b = jnp.where(i < 2, cp, c) + 2 * j
        set_bias(R.bias, b * B, self_lens, self_lens, is_b, 0)
        o, lse = attend(R.q[rows(b)], R.k, R.v)
        R.o[rows(b)] = o
        R.lseT[:, rows(b)] = lse
        y = mm_nt(o, R.wself[h, 3])

        @pl.when(i < 2)
        def _():
            R.cs[j] = y.astype(BF16)
            send(R.cs.at[j], R.cr.at[j], K.rs1, core, j).start()

        @pl.when(i >= 2)
        def _():
            R.part[j] = y

    loop(4, self_block)

    def self_end(j):
        arrived(R.cr.at[j], K.rs1, j)
        branch = R.part[j] + R.cr[j].astype(F32)
        x = R.xrow[rows(blk(j))].astype(F32)
        y = x + branch
        R.mid[j] = y
        tally(16 + 2 * h, x * x)
        tally(21 + 2 * h, branch * branch)

        @pl.when(is_a)
        def _():
            R.n2row[rows(blk(j))] = norm(y, gain(1), shift(1)).astype(BF16)
            send(R.n2row.at[rows(blk(j))], R.n2row.at[rows(blk(j))], K.n2, core, j).start()
            tally(17, y * y)

        @pl.when(is_b & (j == 0))
        def _():
            R.fs[...] = branch.astype(BF16)
            send(R.fs, R.fr, K.br3, ypeer).start()

    loop(2, self_end)

    @pl.when(is_b)
    def _():
        forward(R.we0, K.we0, 0, K.wy_e0, FQ)
        if inside:
            loop(nb, lambda i: e_copy(1, K.we1, i).start(), 1)
        forward(R.wx, K.wx, 0, K.wy_x, LANES)

    @pl.when(is_a)
    def _():
        own_arrived(R.we0, K.we0, 0, FQ)
        if inside:
            loop(nb, lambda i: e_copy(1, K.we1, i).start(), 1)
        y_arrived(R.we0, K.wy_e0, FQ)

        def block(i):
            j = lax.rem(i, 2)
            b = jnp.where(i < 2, c, cp) + 2 * j

            @pl.when(i >= 2)
            def _():
                arrived(R.n2row.at[rows(b)], K.n2, j)

            hid = mm(R.n2row[rows(b)], R.we0[0])
            act, slope = gelu_pair(hid)
            R.g0[rows(b)] = act.astype(BF16)
            R.gp0[rows(b)] = slope.astype(BF16)
            y = mm_nt(R.g0[rows(b)], R.we0[1])

            @pl.when(i < 2)
            def _():
                R.part[j] = y

            @pl.when(i >= 2)
            def _():
                sent(R.cs.at[j], K.rs1, j)
                R.cs[j] = y.astype(BF16)
                send(R.cs.at[j], R.cr.at[j], K.rs2, core, j).start()

        loop(4, block)
        forward(R.wx, K.wx, 0, K.wy_x, LANES)

        def end(j):
            arrived(R.cr.at[j], K.rs2, j)
            branch = R.part[j] + R.cr[j].astype(F32)
            tally(22, branch * branch)
            at = R.mrow.at[rows(blk(j))]
            R.mrow[rows(blk(j))] = (R.mid[j] + branch).astype(BF16)
            send(at, at, K.m_y, ypeer, j).start()
            send(at, at, K.m_c, core, j).start()

        loop(2, end)

    @pl.when(is_a)
    def _():
        arrived(R.fr, K.br3)
        R.t1[...] = R.tgt[...].astype(F32) + R.fr[...].astype(F32)

    @pl.when(is_b)
    def _():
        R.t1[...] = R.mid[1]

    one = R.t1[...]
    tally(19, one * one)
    R.n4c[rows(c)] = norm(one, gain(3), shift(3)).astype(BF16)
    send(R.n4c.at[rows(c)], R.n4c.at[rows(c)], K.n4, core).start()
    y_arrived(R.wx, K.wy_x, LANES)

    def cross_keys(b):
        y = R.mrow[rows(b)]
        R.k2[rows(b)] = mm(y, R.wx[1]).astype(BF16)
        R.v2[rows(b)] = mm(y, R.wx[2]).astype(BF16)

    arrived(R.n4c.at[rows(cp)], K.n4)

    def cross_query(i):
        R.q2[rows(i)] = mm(R.n4c[rows(i)], R.wx[0]).astype(BF16) * jnp.asarray(scale, BF16)

    loop(2, cross_query)

    def memory_block(i):
        j = lax.rem(i, 2)
        b = jnp.where(i < 2, c, cp) + 2 * j
        at = R.mrow.at[rows(b)]

        @pl.when((i < 2) & is_b)
        def _():
            arrived(at, K.m_y, j)
            send(at, at, K.m_c, core, j).start()

        @pl.when(i >= 2)
        def _():
            arrived(at, K.m_c, j)

        cross_keys(b)

    loop(4, memory_block)

    def cross_block(i):
        b = jnp.where(i < 1, cp, c)
        set_bias(R.bias, (2 * h + b) * B, tgt_lens, src_lens, None, 0)
        o, lse = attend(R.q2[rows(b)], R.k2, R.v2)
        R.o2[rows(b)] = o
        R.lse2T[:, rows(b)] = lse
        y = mm_nt(o, R.wx[3])

        @pl.when(i < 1)
        def _():
            R.ds[...] = y.astype(BF16)
            send(R.ds, R.dr.at[0], K.rs4, core).start()

        @pl.when(i >= 1)
        def _():
            R.part[0] = y

    loop(2, cross_block)
    forward(R.we1, K.we1, 0, K.wy_e1, FQ)
    arrived(R.dr.at[0], K.rs4)
    branch4 = R.part[0] + R.dr[0].astype(F32)
    tally(24, branch4 * branch4)
    two = R.t1[...] + branch4
    R.t2[...] = two
    tally(20, two * two)
    R.n5c[rows(c)] = norm(two, gain(4), shift(4)).astype(BF16)
    send(R.n5c.at[rows(c)], R.n5c.at[rows(c)], K.n5, core).start()
    y_arrived(R.we1, K.wy_e1, FQ)

    def dec_block(i):
        b = jnp.where(i < 1, c, cp)

        @pl.when(i >= 1)
        def _():
            arrived(R.n5c.at[rows(b)], K.n5)

        hid = mm(R.n5c[rows(b)], R.we1[0])
        act, slope = gelu_pair(hid)
        R.g1[rows(b)] = act.astype(BF16)
        R.gp1[rows(b)] = slope.astype(BF16)
        y = mm_nt(R.g1[rows(b)], R.we1[1])

        @pl.when(i < 1)
        def _():
            R.part[0] = y

        @pl.when(i >= 1)
        def _():
            sent(R.ds, K.rs4)
            R.ds[...] = y.astype(BF16)
            send(R.ds, R.dr.at[1], K.rs5, core).start()

    loop(2, dec_block)
    arrived(R.b5c.at[rows(cp)], K.cot)

    def dec_back(i):
        b = jnp.where(i < 1, cp, c)
        dact = mm(R.b5c[rows(b)], R.we1[1])
        R.gp1[rows(b)] = (dact * R.gp1[rows(b)].astype(F32)).astype(BF16)
        y = mm_nt(R.gp1[rows(b)], R.we1[0])

        @pl.when(i < 1)
        def _():
            sent(R.ds, K.rs5)
            R.ds[...] = y.astype(BF16)
            send(R.ds, R.dr.at[0], K.rs6, core).start()

        @pl.when(i >= 1)
        def _():
            R.part[1] = y

    loop(2, dec_back)
    arrived(R.dr.at[1], K.rs5)
    branch5 = R.part[0] + R.dr[1].astype(F32)
    tally(25, branch5 * branch5)
    R.dec[...] = R.t2[...] + branch5

    def add_norm(i, dgain, dbias):
        R.acc[pl.ds(i, 1), :] += dgain
        R.acc[pl.ds(5 + i, 1), :] += dbias

    arrived(R.dr.at[0], K.rs6)
    back, dgain, dbias = norm_back(R.t2[...], gain(4), R.part[1] + R.dr[0].astype(F32))
    add_norm(4, dgain, dbias)
    g4 = R.cot[...].astype(F32) + back
    R.g4[...] = g4
    R.b4c[rows(c)] = g4.astype(BF16)
    send(R.b4c.at[rows(c)], R.b4c.at[rows(c)], K.b4, core).start()

    def expert_grads(buf, x_ref, dh_ref, b_ref, g_ref):
        def part(i):
            at = lanes(i, 2 * LANES)
            buf[0, rows(i, 2 * LANES)] = mm_tn(x_ref[:, at], dh_ref[...]).astype(BF16)
            buf[1, rows(i, 2 * LANES)] = mm_tn(b_ref[:, at], g_ref[...]).astype(BF16)

        loop(D // (2 * LANES), part)

    def y_grad(buf, land, name, width):
        return send(buf.at[:, :, lanes(1 - h, width)], land, name, ypeer)

    def dp_a(a, i):
        p = peer_of(i)
        return send(R.qA.at[a, :, rows(p, cw), :], R.dpA.at[a, me], K.gd_a, (p, s), a * nb + p, a * nb + me)

    def dp_e(l, i):
        p = peer_of(i)
        return send(R.qE.at[l, :, rows(p, cw), :], R.dpE.at[l, me], K.gd_e, (p, s), l * nb + p, l * nb + me)

    if inside:

        def chosen_sent(i):
            for l in range(2):
                sent(wblock(R.gE, 0, l, FQ), (K.we0, K.we1)[l], peer_of(i))

        loop(nb, chosen_sent, 1)
    expert_grads(R.gE, R.n5c, R.gp1, R.b5c, R.g1)
    y_grad(R.gE, R.ylE1, K.gy_e1, FQ).start()

    arrived(R.b4c.at[rows(cp)], K.b4)
    R.dkf[...] = jnp.zeros((L, KW), F32)
    R.dvf[...] = jnp.zeros((L, KW), F32)

    def cross_back(i):
        b = jnp.where(i < 1, cp, c)
        do = mm(R.b4c[rows(b)], R.wx[3]).astype(BF16)
        set_bias(R.biasT, (2 * h + b) * B, tgt_lens, src_lens, None, 1)
        dq = attend_back(R.q2[rows(b)], R.o2[rows(b)], do, R.lse2T, rows(b), R.k2, R.v2)
        dq = (dq * scale).astype(BF16)
        R.dq[rows(b)] = dq
        y = mm_nt(dq, R.wx[0])

        @pl.when(i < 1)
        def _():
            sent(R.ds, K.rs6)
            R.ds[...] = y.astype(BF16)
            send(R.ds, R.dr.at[1], K.rs7q, core).start()

        @pl.when(i >= 1)
        def _():
            R.part[0] = y

    loop(2, cross_back)
    R.dkb[...] = R.dkf[...].astype(BF16)
    R.dvb[...] = R.dvf[...].astype(BF16)

    def memory_back(i):
        j = lax.rem(i, 2)
        b = jnp.where(i < 2, cp, c) + 2 * j
        y = mm_nt(R.dkb[rows(b)], R.wx[1]) + mm_nt(R.dvb[rows(b)], R.wx[2])

        @pl.when((i < 2) & is_a)
        def _():
            sent(R.cs.at[j], K.rs2, j)

        @pl.when((i < 2) & is_b)
        def _():
            sent(R.cs.at[j], K.rs1, j)

        @pl.when(i < 2)
        def _():
            R.cs[j] = y.astype(BF16)
            send(R.cs.at[j], R.cr.at[j], K.rs7m, core, j).start()

        @pl.when(i >= 2)
        def _():
            R.dmem[j] = y

    loop(4, memory_back)

    def memory_sum(j):
        arrived(R.cr.at[j], K.rs7m, j)
        y = R.dmem[j] + R.cr[j].astype(F32)
        R.dmem[j] = y

        @pl.when(is_b)
        def _():
            R.be[rows(j)] = y.astype(BF16)
            send(R.be.at[rows(j)], R.dmr.at[j], K.dm, ypeer, j).start()

    loop(2, memory_sum)

    arrived(R.dr.at[1], K.rs7q)
    back, dgain, dbias = norm_back(R.t1[...], gain(3), R.part[0] + R.dr[1].astype(F32))
    add_norm(3, dgain, dbias)
    g3 = R.g4[...] + back
    R.g3[...] = g3

    @pl.when(is_a)
    def _():
        R.fs[...] = g3.astype(BF16)
        send(R.fs, R.brow.at[rows(c)], K.g3, ypeer).start()

    def attn_grads(buf, xq_ref, xk_ref, dq_ref, o_ref, b_ref):
        def part(i):
            at, to = lanes(i, 2 * LANES), rows(i, 2 * LANES)
            buf[0, to] = mm_tn(xq_ref[:, at], dq_ref[...]).astype(BF16)
            buf[1, to] = mm_tn(xk_ref[:, at], R.dkb[...]).astype(BF16)
            buf[2, to] = mm_tn(xk_ref[:, at], R.dvb[...]).astype(BF16)
            buf[3, to] = mm_tn(b_ref[:, at], o_ref[...]).astype(BF16)

        loop(D // (2 * LANES), part)

    attn_grads(R.gA, R.n4c, R.mrow, R.dq.at[0:2 * B], R.o2, R.b4c)
    y_grad(R.gA, R.ylX, K.gy_x, LANES).start()

    def dp_e_start(l):
        if inside:
            loop(nb, lambda i: dp_e(l, i).start(), 1)

    def dp_a_start(a):
        if inside:
            loop(nb, lambda i: dp_a(a, i).start(), 1)

    def join_e1():
        arrived(R.ylE1, K.gy_e1)
        for m in range(2):
            total = R.gE[m, :, lanes(h, FQ)].astype(F32) + R.ylE1[m].astype(F32)
            R.qE[1, m] = total.astype(BF16)
        dp_e_start(1)

    def join_x():
        arrived(R.ylX, K.gy_x)
        for m in range(4):
            total = R.gA[m, :, lanes(h)].astype(F32) + R.ylX[m].astype(F32)
            R.qA[2, m] = total.astype(BF16)
        dp_a_start(2)

    join_e1()
    join_x()

    @pl.when(is_a)
    def _():
        def begin(j):
            arrived(R.dmr.at[j], K.dm, j)
            y = R.dmem[j] + R.dmr[j].astype(F32)
            R.dmem[j] = y
            at = R.be.at[rows(blk(j))]
            R.be[rows(blk(j))] = y.astype(BF16)
            send(at, at, K.be, core, j).start()

        loop(2, begin)

        def block(i):
            j = lax.rem(i, 2)
            b = jnp.where(i < 2, c, cp) + 2 * j

            @pl.when(i >= 2)
            def _():
                arrived(R.be.at[rows(b)], K.be, j)

            dact = mm(R.be[rows(b)], R.we0[1])
            R.gp0[rows(b)] = (dact * R.gp0[rows(b)].astype(F32)).astype(BF16)
            y = mm_nt(R.gp0[rows(b)], R.we0[0])

            @pl.when(i < 2)
            def _():
                R.part[j] = y

            @pl.when(i >= 2)
            def _():
                sent(R.cs.at[j], K.rs7m, j)
                R.cs[j] = y.astype(BF16)
                send(R.cs.at[j], R.cr.at[j], K.rs8, core, j).start()

        loop(4, block)

        def end(j):
            arrived(R.cr.at[j], K.rs8, j)
            up = R.part[j] + R.cr[j].astype(F32)
            back, dgain, dbias = norm_back(R.mid[j], gain(1), up)
            add_norm(1, dgain, dbias)
            g = R.dmem[j] + back
            R.dmem[j] = g
            at = R.brow.at[rows(blk(j))]
            R.brow[rows(blk(j))] = g.astype(BF16)
            send(at, at, K.brow, core, j).start()

        loop(2, end)
        y_grad(R.gE, R.ylE1, K.gy_e1, FQ).wait_send()
        expert_grads(R.gE, R.n2row, R.gp0, R.be, R.g0)
        y_grad(R.gE, R.qE.at[0], K.gy_e0, FQ).start()
        for m in range(2):
            R.qE[0, m] = R.gE[m, :, lanes(h, FQ)]
        dp_e_start(0)

    @pl.when(is_b)
    def _():
        R.brow[rows(blk(1))] = R.g3[...].astype(BF16)
        arrived(R.brow.at[rows(blk(0))], K.g3)
        for j in range(2):
            at = R.brow.at[rows(blk(j))]
            send(at, at, K.brow, core, j).start()

    R.dkf[...] = jnp.zeros((L, KW), F32)
    R.dvf[...] = jnp.zeros((L, KW), F32)

    def self_back(i):
        j = lax.rem(i, 2)
        b = jnp.where(i < 2, c, cp) + 2 * j

        @pl.when(i >= 2)
        def _():
            arrived(R.brow.at[rows(b)], K.brow, j)

        do = mm(R.brow[rows(b)], R.wself[h, 3]).astype(BF16)
        set_bias(R.biasT, b * B, self_lens, self_lens, is_b, 1)
        dq = attend_back(R.q[rows(b)], R.o[rows(b)], do, R.lseT, rows(b), R.k, R.v)
        R.dq[rows(b)] = (dq * scale).astype(BF16)

    loop(4, self_back)
    R.dkb[...] = R.dkf[...].astype(BF16)
    R.dvb[...] = R.dvf[...].astype(BF16)
    y_grad(R.gA, R.ylX, K.gy_x, LANES).wait_send()
    attn_grads(R.gA, R.nrow, R.nrow, R.dq, R.o, R.brow)
    y_grad(R.gA, R.qA.at[h], K.gy_s, LANES).start()
    for m in range(4):
        R.qA[h, m] = R.gA[m, :, lanes(h)]
    dp_a_start(h)

    def self_dx(i):
        j = lax.rem(i, 2)
        b = jnp.where(i < 2, cp, c) + 2 * j
        y = mm_nt(R.dq[rows(b)], R.wself[h, 0])
        y = y + mm_nt(R.dkb[rows(b)], R.wself[h, 1])
        y = y + mm_nt(R.dvb[rows(b)], R.wself[h, 2])

        @pl.when((i < 2) & is_a)
        def _():
            sent(R.cs.at[j], K.rs8, j)

        @pl.when((i < 2) & is_b)
        def _():
            sent(R.cs.at[j], K.rs7m, j)

        @pl.when(i < 2)
        def _():
            R.cs[j] = y.astype(BF16)
            send(R.cs.at[j], R.cr.at[j], K.rs9, core, j).start()

        @pl.when(i >= 2)
        def _():
            R.part[j] = y

    loop(4, self_dx)

    @pl.when(is_b)
    def _():
        arrived(R.qE.at[0], K.gy_e0)
        dp_e_start(0)

    def self_final(j):
        arrived(R.cr.at[j], K.rs9, j)
        x = R.xrow[rows(blk(j))].astype(F32)
        back, dgain, dbias = norm_back(x, gain(2 * h), R.part[j] + R.cr[j].astype(F32))
        add_norm(2 * h, dgain, dbias)

        @pl.when(is_a & (j == 0))
        def _():
            R.sgrad[...] = R.dmem[0] + back

        @pl.when(is_a & (j == 1))
        def _():
            sent(R.fs, K.g3)
            R.fs[...] = (R.dmem[1] + back).astype(BF16)
            send(R.fs, R.fr, K.fin, ypeer).start()

        @pl.when(is_b & (j == 0))
        def _():
            sent(R.fs, K.br3)
            R.fs[...] = back.astype(BF16)
            send(R.fs, R.fr, K.fin, ypeer).start()

        @pl.when(is_b & (j == 1))
        def _():
            R.tgrad[...] = R.g3[...] + back

    loop(2, self_final)

    send(R.acc, R.accc, K.accc, core).start()
    arrived(R.accc, K.accc)
    R.acc1[...] = R.acc[...] + R.accc[...]
    send(R.acc1, R.accy, K.accy, ypeer).start()

    arrived(R.qA.at[1 - h], K.gy_s)
    dp_a_start(1 - h)

    arrived(R.accy, K.accy)
    R.acc2[...] = R.acc1[...] + R.accy[...]
    R.stats[...] = R.acc2[16:32, :]
    arrived(R.fr, K.fin)

    @pl.when(is_a)
    def _():
        R.tgrad[...] = R.g3[...] + R.fr[...].astype(F32)

    @pl.when(is_b)
    def _():
        R.sgrad[...] = R.fr[...].astype(F32)

    if inside:

        def tile_of(p):
            return lanes(lax.div(p * cw, LANES))

        def acc_copy(i):
            p = peer_of(i)
            return send(R.acc2.at[0:16, tile_of(p)], R.accd.at[me], K.accd, (p, s), p, me)

        loop(nb, lambda i: acc_copy(i).start(), 1)

        for l in range(2):
            loop(nb, lambda i, l=l: arrived(R.dpE.at[l, peer_of(i)], K.gd_e, l * nb + peer_of(i)), 1)
            for m in range(2):
                R.dpE[l, pl.ds(me, 1), m] = R.qE[l, m, rows(me, cw), :][None]
            for m, total_ref in enumerate((R.gup, R.gdn)):

                def one_expert(e, l=l, m=m, total_ref=total_ref):
                    total = jnp.zeros((cw, FQ), F32)
                    for p in range(nb):
                        row = R.smallr[p, 10 + l:11 + l, :]
                        hit = jnp.where(row == e.astype(F32), 1.0, 0.0)
                        hit = jnp.concatenate([hit] * (FQ // LANES), axis=1)
                        total = total + R.dpE[l, p, m].astype(F32) * hit
                    total_ref[l, pl.ds(e, 1)] = total[None]

                loop(E, one_expert)

        def attn_total(a):
            loop(nb, lambda i: arrived(R.dpA.at[a, peer_of(i)], K.gd_a, a * nb + peer_of(i)), 1)
            for m in range(4):
                R.dpA[a, pl.ds(me, 1), m] = R.qA[a, m, rows(me, cw), :][None]
            for m in range(4):
                total = R.dpA[a, 0, m].astype(F32)
                for p in range(1, nb):
                    total = total + R.dpA[a, p, m].astype(F32)
                if m < 3:
                    R.gqkv[a, m] = total
                else:
                    R.gout[a] = total

        for a in (2, 0, 1):
            attn_total(a)

        loop(nb, lambda i: arrived(R.accd.at[peer_of(i)], K.accd, peer_of(i)), 1)
        total = R.acc2[0:16, tile_of(me)]

        def more(i):
            R.ggb[...] += R.accd[peer_of(i)]

        R.ggb[...] = total
        loop(nb, more, 1)
    else:
        R.ga[...] = R.qA[...]
        R.ge[...] = R.qE[...]
        R.gacc[...] = R.acc2[0:16, :]

    sent(R.oth, K.in_y)
    sent(R.oth, K.in_c, 0)
    sent(R.oth, K.in_c, 1)
    sent(R.oth, K.cot)
    y_sent(other, K.wy_self, LANES)
    y_sent(R.wx, K.wy_x, LANES)
    y_sent(R.we1, K.wy_e1, FQ)
    for name in (K.rs9, K.brow, K.m_c):
        for j in range(2):
            sent(R.oth, name, j)
    for name in (K.n4, K.n5, K.b4, K.rs7q, K.fin):
        sent(R.oth, name)
    y_grad(R.gA, R.qA.at[h], K.gy_s, LANES).wait_send()
    send(R.acc, R.accc, K.accc, core).wait_send()
    send(R.acc1, R.accy, K.accy, ypeer).wait_send()

    @pl.when(is_a)
    def _():
        for name in (K.n2, K.m_y, K.be):
            for j in range(2):
                sent(R.oth, name, j)
        y_grad(R.gE, R.qE.at[0], K.gy_e0, FQ).wait_send()

    @pl.when(is_b)
    def _():
        y_grad(R.gE, R.ylE1, K.gy_e1, FQ).wait_send()
        y_sent(R.we0, K.wy_e0, FQ)
        for j in range(2):
            sent(R.oth, K.dm, j)

    if inside:

        def drain(i):
            p = peer_of(i)
            small_copy(p, me).wait_send()
            for a in range(2):
                sent(R.sendA.at[a], K.wself, a * nb + p)
            sent(R.sendA.at[2], K.wx, p)
            for l in range(2):
                sent(R.dpE.at[l, 0], K.gd_e, l * nb + p)
            for a in range(3):
                sent(R.dpA.at[a, 0], K.gd_a, a * nb + p)
            sent(R.accd.at[0], K.accd, p)

        loop(nb, drain, 1)


def on_device(
    src_input,
    tgt_input,
    out_cotangent,
    src_lengths,
    tgt_lengths,
    enc_expert,
    dec_expert,
    norm_gains,
    norm_biases,
    qkv_weight,
    out_weight,
    expert_up,
    expert_down,
):
    n = lax.axis_size("dp")
    dp = lax.axis_index("dp")
    B, D = src_input.shape[1:]
    cw = norm_gains.shape[1]
    FQ = expert_up.shape[3]
    E = expert_up.shape[1]
    inside = cw % 16 == 0 and LANES % cw == 0
    wot = jnp.swapaxes(out_weight, 1, 2)
    dnt = jnp.swapaxes(expert_down, 2, 3)
    gb = jnp.concatenate([norm_gains, norm_biases], 0).astype(F32)
    if inside:
        nb, rowsize = n, cw
        at = lax.rem(dp * cw, LANES)
        small = lax.dynamic_update_slice(jnp.zeros((16, LANES), F32), gb, (0, at))
        picks = jnp.concatenate([enc_expert, dec_expert], 0).astype(F32)
        small = small.at[10:12].set(jnp.broadcast_to(picks, (2, LANES)))
        operands = dict(small=small, qkv=qkv_weight, wot=wot, up=expert_up, dnt=dnt)
        grads = dict(
            gqkv=jax.ShapeDtypeStruct((3, 3, cw, LANES), F32),
            gout=jax.ShapeDtypeStruct((3, cw, LANES), F32),
            gup=jax.ShapeDtypeStruct((2, E, cw, FQ), F32),
            gdn=jax.ShapeDtypeStruct((2, E, cw, FQ), F32),
            ggb=jax.ShapeDtypeStruct((16, LANES), F32),
        )
    else:
        nb, rowsize = 1, D
        small = lax.all_gather(gb, "dp", axis=1, tiled=True)
        small = jnp.concatenate([small, jnp.zeros((6, D), F32)], 0)
        wa = jnp.concatenate([qkv_weight, wot[:, None]], 1)
        wa = lax.all_gather(wa, "dp", axis=2, tiled=True)
        picks = jnp.stack([enc_expert[0, 0], dec_expert[0, 0]])
        we = jnp.stack([expert_up, dnt], 2)
        we = lax.all_gather(we, "dp", axis=3, tiled=True)
        we = jnp.stack([jnp.take(we[l], picks[l], axis=0) for l in range(2)])
        operands = dict(small=small, wa=wa, we=we)
        grads = dict(
            ga=jax.ShapeDtypeStruct((3, 4, D, LANES), BF16),
            ge=jax.ShapeDtypeStruct((2, 2, D, FQ), BF16),
            gacc=jax.ShapeDtypeStruct((16, D), F32),
        )
    cfg = (n, nb, rowsize, B, D, FQ, E, inside)
    scratch = scratch_list(n, nb, rowsize, B, D, FQ)
    count = sem_list(nb)[1]
    scratch.update(ss=pltpu.SemaphoreType.DMA((count,)), rs=pltpu.SemaphoreType.DMA((count,)))
    block = jax.ShapeDtypeStruct((B, D), F32)
    vmem = pl.BlockSpec(memory_space=pltpu.VMEM)
    smem = pl.BlockSpec(memory_space=pltpu.SMEM)
    lengths = dict(slen=src_lengths, tlen=tgt_lengths)
    operands = dict(src=src_input[0], tgt=tgt_input[0], cot=out_cotangent[0], **operands)
    results = dict(dec=block, sgrad=block, tgrad=block, stats=jax.ShapeDtypeStruct((16, D), F32), **grads)
    names = tuple(lengths) + tuple(operands) + tuple(results) + tuple(scratch)
    outs = pl.pallas_call(
        functools.partial(step_kernel, cfg, names),
        name="step",
        out_shape=tuple(results.values()),
        in_specs=[smem] * len(lengths) + [vmem] * len(operands),
        out_specs=[vmem] * len(results),
        scratch_shapes=list(scratch.values()),
        compiler_params=pltpu.CompilerParams(
            collective_id=1, has_side_effects=True, vmem_limit_bytes=62 << 20
        ),
        cost_estimate=pl.CostEstimate(flops=17 << 30, bytes_accessed=8 << 20, transcendentals=16 << 20),
    )(*lengths.values(), *operands.values())
    dec, sgrad, tgrad, stats = outs[:4]
    length = B * lax.axis_size("seq")
    rms = jnp.sqrt(jnp.sum(stats[:10], 1) / (length * D)).reshape(1, 2, 5)
    if inside:
        gqkv, gout, gup, gdn, ggb = outs[4:]
        own = lax.dynamic_slice(ggb, (0, at), (16, cw))
        gains, biases = own[0:5], own[5:10]
    else:
        ga, ge, gacc = outs[4:]

        def total(x, axis):
            return lax.psum_scatter(x, "dp", scatter_dimension=axis, tiled=True)

        gains, biases = total(gacc[0:5], 1), total(gacc[5:10], 1)
        ga = total(ga.astype(F32), 2)
        gqkv, gout = ga[:, :3], ga[:, 3]
        match = (picks[:, None] == jnp.arange(E, dtype=jnp.int32)[None]).astype(F32)
        ge = ge.astype(F32)[:, None] * match[:, :, None, None, None]
        ge = total(ge, 3)
        gup, gdn = ge[:, :, 0], ge[:, :, 1]
    return (
        dec[None],
        sgrad[None],
        tgrad[None],
        gains,
        biases,
        gqkv,
        jnp.swapaxes(gout, 1, 2),
        gup,
        jnp.swapaxes(gdn, 2, 3),
        rms,
    )


def solution(mesh):
    placed = (
        P("dp", "seq", None),
        P("dp", "seq", None),
        P("dp", "seq", None),
        P("dp", None),
        P("dp", None),
        P("dp", None),
        P("dp", None),
        P(None, "dp"),
        P(None, "dp"),
        P(None, None, "dp", "seq"),
        P(None, "seq", "dp"),
        P(None, None, "dp", "seq"),
        P(None, None, "seq", "dp"),
    )
    return jax.shard_map(
        on_device,
        mesh=mesh,
        in_specs=placed,
        out_specs=(
            P("dp", "seq", None),
            P("dp", "seq", None),
            P("dp", "seq", None),
            P(None, "dp"),
            P(None, "dp"),
            P(None, None, "dp", "seq"),
            P(None, "seq", "dp"),
            P(None, None, "dp", "seq"),
            P(None, None, "seq", "dp"),
            P("dp", None, None),
        ),
        check_vma=False,
    )
```

```python
import functools
import math
from types import SimpleNamespace

import jax
import jax.numpy as jnp
from jax import lax
from jax.experimental import pallas as pl
from jax.experimental.pallas import tpu as pltpu
from jax.sharding import PartitionSpec as P

HEAD_DIM = 64
EPSILON = 1e-05
MASKED = -1e30
LANES = 128
F32 = jnp.float32
BF16 = jnp.bfloat16
MESH = pl.DeviceIdType.MESH
GELU_A = math.sqrt(2.0 / math.pi)
GELU_B = 0.044715


def mm(a, b):
    return lax.dot_general(a, b, (((1,), (0,)), ((), ())), preferred_element_type=F32)


def mm_nt(a, b):
    return lax.dot_general(a, b, (((1,), (1,)), ((), ())), preferred_element_type=F32)


def mm_tn(a, b):
    return lax.dot_general(a, b, (((0,), (0,)), ((), ())), preferred_element_type=F32)


def centre(x):
    mean = jnp.mean(x, -1, keepdims=True)
    xc = x - mean
    var = jnp.mean(xc * xc, -1, keepdims=True)
    scale = lax.rsqrt(var + EPSILON)
    return xc * scale, scale


def norm(x, gain, shift):
    return centre(x)[0] * gain + shift


def norm_back(x, gain, up):
    xh, scale = centre(x)
    dgain = jnp.sum(up * xh, 0, keepdims=True)
    dbias = jnp.sum(up, 0, keepdims=True)
    dxh = up * gain
    m1 = jnp.mean(dxh, -1, keepdims=True)
    m2 = jnp.mean(dxh * xh, -1, keepdims=True)
    return scale * (dxh - m1 - xh * m2), dgain, dbias


def gelu_pair(x):
    square = x * x
    t = jnp.tanh(x * (GELU_A + (GELU_A * GELU_B) * square))
    half = 0.5 + 0.5 * t
    slope = half + (0.5 * x) * (1.0 - t * t) * (GELU_A + (3.0 * GELU_A * GELU_B) * square)
    return x * half, slope


def scratch_list(nb, cw, B, D, FQ, inside):
    L, F2, KW = 4 * B, 2 * FQ, 2 * LANES

    def b(*shape):
        return pltpu.VMEM(shape, BF16)

    def f(*shape):
        return pltpu.VMEM(shape, F32)

    out = dict(
        xrow=b(L, D),
        oth=b(B, D),
        nrow=b(L, D),
        wself=b(2, 4, D, KW),
        wx=b(4, D, KW),
        we0=b(2, D, F2),
        we1=b(2, D, FQ),
        gtab=f(16, D),
        q=b(L, KW),
        k=b(L, KW),
        v=b(L, KW),
        o=b(L, KW),
        do=b(L, KW),
        lseT=f(8, L),
        drowT=f(16, L),
        bias=f(B, L),
        biasT=f(L, B),
        part=f(2, B, D),
        cs=b(2, B, D),
        cr=b(2, B, D),
        mid=f(2, B, D),
        n2row=b(L, D),
        g0=b(L, F2),
        gp0=b(L, F2),
        mrow=b(L, D),
        fs=b(B, D),
        fr=b(B, D),
        t1=f(B, D),
        n4c=b(2 * B, D),
        q2=b(2 * B, KW),
        k2=b(L, KW),
        v2=b(L, KW),
        o2=b(2 * B, KW),
        lse2T=f(8, 2 * B),
        ds=b(B, D),
        dr=b(2, B, D),
        t2=f(B, D),
        n5=b(L, D),
        b5=b(L, D),
        g1=b(L, FQ),
        dh1=b(L, FQ),
        es=b(3, B, D),
        er=b(3, B, D),
        es6=b(3, B, D),
        er6=b(3, B, D),
        g4=f(B, D),
        last=f(B, D),
        b4c=b(2 * B, D),
        dkf=f(L, LANES),
        dvf=f(L, LANES),
        dkb=b(L, KW),
        dvb=b(L, KW),
        dmr=b(2, B, D),
        g3=f(B, D),
        brow=b(L, D),
        dmem=f(2, B, D),
        be=b(L, D),
        dq=b(L, KW),
        gA=b(4, D, KW),
        gE=b(2, D, F2),
        ylX=b(4, D, LANES),
        acc=f(32, D),
        acc1=f(32, D),
        acc2=f(32, D),
        accc=f(32, D),
        accy=f(32, D),
    )
    if inside:
        out.update(
            small=f(16, LANES),
            smallr=f(nb, 16, LANES),
            sendA=b(3, 4, cw, LANES),
            qA=b(3, 4, D, LANES),
            pA=b(3, 4, D // 2, LANES),
            qE=b(2, 2, D, FQ),
            accd=f(nb, 16, LANES),
        )
    return out


def sem_list(nb):
    counts = dict(
        in_y=1,
        in_c=2,
        b5=3,
        small=nb,
        wa=3 * nb,
        wr=3 * nb,
        we0=nb,
        we1=nb,
        wy_self=nb,
        wy_x=nb,
        wy_e0=nb,
        rs1=2,
        n2=2,
        rs2=2,
        br3=1,
        m_y=2,
        m_c=2,
        n4=1,
        rs4=1,
        n5=3,
        rs5=3,
        rs6=3,
        b4=1,
        rs7q=1,
        rs7m=2,
        dm=2,
        g3=1,
        brow=2,
        be=2,
        rs8=2,
        rs9=2,
        fin=1,
        gy_s=2,
        gy_x=1,
        gy_e0=2,
        gd_a=3 * nb,
        gd_x=3 * nb,
        gd_e=2 * nb,
        accc=1,
        accy=1,
        accd=nb,
        here=5,
    )
    base, at = {}, 0
    for name, number in counts.items():
        base[name] = at
        at = at + number
    return SimpleNamespace(**base), at


def step_kernel(cfg, names, *refs):
    nb, cw, B, D, FQ, E, inside = cfg
    L, F2, KW = 4 * B, 2 * FQ, 2 * LANES
    R = SimpleNamespace(**dict(zip(names, refs, strict=True)))
    K, _ = sem_list(nb)

    dp = lax.axis_index("dp")
    me = dp if inside else 0
    s = lax.axis_index("seq")
    h = lax.div(s, 2)
    c = lax.rem(s, 2)
    cp = 1 - c
    sc = s + 1 - 2 * c
    sy = s + 2 - 4 * h
    core, ypeer = (dp, sc), (dp, sy)
    is_a, is_b = h == 0, h == 1

    def rows(i, size=B):
        return pl.ds(pl.multiple_of(i * size, size), size)

    def lanes(i, size=LANES):
        return pl.ds(pl.multiple_of(i * size, size), size)

    def send(src, dst, name, to, i=0, j=None):
        return pltpu.make_async_remote_copy(
            src_ref=src,
            dst_ref=dst,
            send_sem=R.ss.at[name + i],
            recv_sem=R.rs.at[name + (i if j is None else j)],
            device_id=to,
            device_id_type=MESH,
        )

    def arrived(dst, name, i=0):
        send(dst, dst, name, core, i).wait_recv()

    def sent(src, name, i=0):
        send(src, src, name, core, i).wait_send()

    def loop(count, body, start=0):
        def step(i, carry):
            body(i)
            return carry

        lax.fori_loop(start, count, step, 0)

    def to_peer(i):
        return lax.rem(me + i, nb)

    def from_peer(i):
        return lax.rem(me + nb - i, nb)

    pair = me + 1 - 2 * lax.rem(me, 2)

    barrier = pltpu.get_barrier_semaphore()
    for to in (core, ypeer):
        pl.semaphore_signal(barrier, inc=1, device_id=to, device_id_type=MESH)

    def greet(i):
        pl.semaphore_signal(barrier, inc=1, device_id=(to_peer(i), s), device_id_type=MESH)

    loop(nb, greet, 1)

    if inside:
        R.small[...] = jnp.zeros((16, LANES), F32)
        for k in range(LANES // cw):

            @pl.when(lax.rem(dp, LANES // cw) == k)
            def _(k=k):
                R.small[0:5, k * cw:(k + 1) * cw] = R.gains[...].astype(F32)
                R.small[5:10, k * cw:(k + 1) * cw] = R.biases[...].astype(F32)

        R.small[10:11, :] = jnp.broadcast_to(R.epick[0, 0].astype(F32), (1, LANES))
        R.small[11:12, :] = jnp.broadcast_to(R.dpick[0, 0].astype(F32), (1, LANES))

    @pl.when(is_a)
    def _():
        R.xrow[rows(s)] = R.src[...]
        R.oth[...] = R.tgt[...]

    @pl.when(is_b)
    def _():
        R.xrow[rows(s)] = R.tgt[...]
        R.oth[...] = R.src[...]

    R.b5[rows(s)] = R.cot[...]
    for a in range(3):
        if inside:
            for j in range(3):
                R.sendA[a, j] = R.qkv[a, j]
            R.sendA[a, 3] = R.wot[a]
        buf = R.wself.at[a] if a < 2 else R.wx
        piece = R.sendA if inside else R.wa
        for j in range(4):
            buf[j, rows(me, cw), lanes(h)] = piece[a, j]
    pl.semaphore_wait(barrier, nb + 1)

    def small_copy(p):
        return send(R.small, R.smallr.at[me], K.small, (p, s), p, me)

    def wblock(buf, p, half, width):
        return buf.at[:, rows(p, cw), lanes(half, width)]

    def held(a):
        return R.wself.at[a] if a < 2 else R.wx

    def a_copy(a, p):
        return send(R.sendA.at[a], wblock(held(a), me, h, LANES), K.wa, (p, s), a * nb + p, a * nb + me)

    def a_relay(a, p):
        at = wblock(held(a), p, h, LANES)
        return send(at, at, K.wr, (pair, s), a * nb + p)

    def y_block(buf, p, name, width):
        at = wblock(buf, p, h, width)
        return send(at, at, name, ypeer, p)

    def same_side(i):
        return lax.rem(me + 2 * i, nb)

    def e_copy(l, p):
        at = wblock(R.we0, me, h, FQ) if l == 0 else R.we1.at[:, rows(me, cw), :]
        return send(wblock(R.gE, p, l, FQ), at, (K.we0, K.we1)[l], (p, s), p, me)

    def row_copy(buf, block, name, to, i=0):
        at = buf.at[rows(block)]
        return send(at, at, name, to, i)

    if inside:
        loop(nb, lambda i: small_copy(to_peer(i)).start(), 1)
    send(R.oth, R.xrow.at[rows(s)], K.in_y, ypeer).start()
    row_copy(R.xrow, s, K.in_c, core, 0).start()
    if inside:

        def spread_self(i):
            for a in range(2):
                a_copy(a, same_side(i)).start()

        loop(nb // 2, spread_self, 1)
        for a in range(2):
            a_copy(a, pair).start()
    other = R.wself.at[1 - h]
    y_block(other, me, K.wy_self, LANES).start()

    if inside:
        loop(nb, lambda i: arrived(R.smallr.at[0], K.small, from_peer(i)), 1)
        R.smallr[pl.ds(me, 1)] = R.small[...][None]
        per = LANES // cw
        for t in range(D // LANES):
            tile = R.smallr[t * per]
            for k in range(1, per):
                tile = tile + R.smallr[t * per + k]
            R.gtab[:, t * LANES:(t + 1) * LANES] = tile

        def chosen(l, p):
            row = R.smallr[p, pl.ds(10 + l, 1), :]
            for m, shard in enumerate((R.up, R.dnt)):
                total = None
                for e in range(E):
                    hit = jnp.where(row == float(e), 1.0, 0.0)
                    hit = jnp.concatenate([hit] * (FQ // LANES), axis=1)
                    term = shard[l, e].astype(F32) * hit
                    total = term if total is None else total + term
                R.gE[m, rows(p, cw), lanes(l, FQ)] = total.astype(BF16)

        loop(nb, lambda p: chosen(0, p))
        for m in range(2):
            R.we0[m, rows(me, cw), lanes(h, FQ)] = R.gE[m, rows(me, cw), lanes(0, FQ)]

    arrived(R.xrow.at[rows(sy)], K.in_y)
    row_copy(R.xrow, sy, K.in_c, core, 1).start()

    if inside:

        def near(i):
            p = same_side(i)
            for a in range(2):
                arrived(wblock(held(a), p, h, LANES), K.wa, a * nb + p)
                a_relay(a, p).start()
            y_block(other, p, K.wy_self, LANES).start()

        def far(i):
            p = lax.rem(pair + 2 * i, nb)
            for a in range(2):
                arrived(wblock(held(a), p, h, LANES), K.wr, a * nb + p)
            y_block(other, p, K.wy_self, LANES).start()

        for a in range(2):
            arrived(wblock(held(a), pair, h, LANES), K.wa, a * nb + pair)
        y_block(other, pair, K.wy_self, LANES).start()
        loop(nb // 2, near, 1)
        e_copy(0, pair).start()
        loop(nb // 2, lambda i: e_copy(0, same_side(i)).start(), 1)
        loop(nb // 2, far, 1)
        loop(nb // 2, lambda i: e_copy(0, lax.rem(pair + 2 * i, nb)).start(), 1)
        loop(nb, lambda p: chosen(1, p))
        for m in range(2):
            R.we1[m, rows(me, cw), :] = R.gE[m, rows(me, cw), lanes(1, FQ)]
    else:
        R.gtab[...] = R.small[...]
        for m in range(2):
            R.we0[m, rows(me, cw), lanes(h, FQ)] = R.we[0, m]
            R.we1[m, rows(me, cw), :] = R.we[1, m]

    def send_x():
        if inside:
            loop(nb // 2, lambda i: a_copy(2, same_side(i)).start(), 1)
            a_copy(2, pair).start()

    def near_x():
        def one(i):
            arrived(wblock(R.wx, 0, h, LANES), K.wa, 2 * nb + same_side(i))
            a_relay(2, same_side(i)).start()

        if inside:
            loop(nb // 2, one, 1)

    def send_e1():
        if inside:
            loop(nb, lambda i: e_copy(1, to_peer(i)).start(), 1)

    def finish_x():
        if inside:
            arrived(wblock(R.wx, pair, h, LANES), K.wa, 2 * nb + pair)
            loop(nb // 2, lambda i: arrived(wblock(R.wx, 0, h, LANES), K.wr, 2 * nb + lax.rem(pair + 2 * i, nb)), 1)
        loop(nb, lambda i: y_block(R.wx, to_peer(i), K.wy_x, LANES).start())

    def pass_e0(p):
        if inside:

            @pl.when(p != me)
            def _():
                arrived(wblock(R.we0, p, h, FQ), K.we0, p)

        y_block(R.we0, p, K.wy_e0, FQ).start()

    def y_arrived(buf, name, width):
        loop(nb, lambda i: arrived(wblock(buf, 0, h, width), name, to_peer(i)))

    def y_sent(buf, name, width):
        loop(nb, lambda i: sent(wblock(buf, 0, h, width), name, to_peer(i)))

    @pl.when(is_b)
    def _():
        pass_e0(me)
        if inside:
            pass_e0(pair)

    y_arrived(R.wself.at[h], K.wy_self, LANES)

    R.acc[...] = jnp.zeros((32, D), F32)

    def tally(row, x):
        R.acc[pl.ds(row, 1), :] += jnp.sum(x, 0, keepdims=True)

    def gain(i):
        return R.gtab[pl.ds(i, 1), :]

    def shift(i):
        return R.gtab[pl.ds(5 + i, 1), :]

    def blk(j):
        return c + 2 * j

    def pblk(j):
        return cp + 2 * j

    def src_len(k):
        return R.slen[0, k]

    def tgt_len(k):
        return R.tlen[0, k]

    def self_len(k):
        return jnp.where(is_a, R.slen[0, k], R.tlen[0, k])

    docs = R.slen.shape[1]

    def set_bias(buf, q_start, q_len, k_len, causal, q_axis):
        shape = (B, L) if q_axis == 0 else (L, B)
        q_pos = lax.broadcasted_iota(jnp.int32, (B, 1) if q_axis == 0 else (1, B), q_axis) + q_start
        k_pos = lax.broadcasted_iota(jnp.int32, shape, 1 - q_axis)
        first = jnp.zeros(q_pos.shape, jnp.int32)
        last = jnp.zeros(q_pos.shape, jnp.int32) + k_len(0)
        edge = 0
        for k in range(docs):
            edge = edge + q_len(k)
            passed = q_pos >= edge
            first = first + jnp.where(passed, k_len(k), 0)
            if k + 1 < docs:
                last = last + jnp.where(passed, k_len(k + 1), 0)
        if causal is not None:
            last = jnp.minimum(last, q_pos + jnp.where(causal, 1, L))
        buf[...] = jnp.where((k_pos >= first) & (k_pos < last), 0.0, MASKED)

    lane_head = lax.div(lax.broadcasted_iota(jnp.int32, (1, KW), 1), HEAD_DIM)
    heads = KW // HEAD_DIM

    def attend(q_blk, k_ref, v_ref):
        lane = lax.broadcasted_iota(jnp.int32, (1, LANES), 1)
        out = jnp.zeros((B, KW), F32)
        lse = jnp.zeros((B, LANES), F32)
        for hd in range(heads):
            hrow = jnp.where(lane_head == hd, 1.0, 0.0)
            scores = mm_nt(q_blk * hrow.astype(BF16), k_ref[...]) + R.bias[...]
            top = jnp.max(scores, -1, keepdims=True)
            expos = jnp.exp(scores - top)
            total = jnp.sum(expos, -1, keepdims=True)
            out = out + mm(expos.astype(BF16), v_ref[...]) * (hrow / total)
            lse = lse + jnp.where(lane == hd, top + jnp.log(total), 0.0)
        return out.astype(BF16), jnp.transpose(lse)[0:8, :]

    scale = HEAD_DIM ** (-0.5)

    def row_sums(o_blk, do_blk):
        prod = do_blk.astype(F32) * o_blk.astype(F32)
        high = prod.astype(BF16)
        low = (prod - high.astype(F32)).astype(BF16)
        pick = lax.broadcasted_iota(jnp.int32, (16, KW), 0) == jnp.broadcast_to(lane_head, (16, KW))
        pick = jnp.where(pick, 1.0, 0.0).astype(BF16)
        return mm_nt(pick, high) + mm_nt(pick, low)

    half_head = lax.div(lax.broadcasted_iota(jnp.int32, (1, LANES), 1), HEAD_DIM)

    def back_half(t, count, block_of, first_pass, q_ref, o_ref, lse_ref, k_ref, v_ref, bias_of):
        lt = lanes(t)
        R.dkf[...] = jnp.zeros((L, LANES), F32)
        R.dvf[...] = jnp.zeros((L, LANES), F32)

        def block(i):
            b = block_of(i)
            if first_pass is not None:
                do = first_pass(i, b)
                R.do[rows(b)] = do
                R.drowT[:, rows(b)] = row_sums(o_ref[rows(b)], do)
            bias_of(b)
            q_blk, do_blk = q_ref[rows(b), lt], R.do[rows(b), lt]
            total = jnp.zeros((B, LANES), F32)
            for u in range(LANES // HEAD_DIM):
                hrow = jnp.where(half_head == u, 1.0, 0.0)
                hlow = hrow.astype(BF16)
                at = pl.ds(2 * t + u, 1)
                qm, dom = q_blk * hlow, do_blk * hlow
                probs = jnp.exp(mm_nt(k_ref[:, lt], qm) + R.biasT[...] - lse_ref[at, rows(b)])
                R.dvf[...] += mm(probs.astype(BF16), dom)
                change = probs * (mm_nt(v_ref[:, lt], dom) - R.drowT[at, rows(b)])
                change = change.astype(BF16)
                R.dkf[...] += mm(change, qm)
                total = total + mm_tn(change, k_ref[:, lt]) * hrow
            R.dq[rows(b), lt] = (total * scale).astype(BF16)

        loop(count, block)
        R.dkb[:, lt] = R.dkf[...].astype(BF16)
        R.dvb[:, lt] = R.dvf[...].astype(BF16)

    def half_grads(t, xq_ref, xk_ref, dq_ref, o_ref, b_ref, after=None):
        lt = lanes(t)

        def part(i):
            at, to = lanes(i, 2 * LANES), rows(i, 2 * LANES)
            R.gA[0, to, lt] = mm_tn(xq_ref[:, at], dq_ref[:, lt]).astype(BF16)
            R.gA[1, to, lt] = mm_tn(xk_ref[:, at], R.dkb[:, lt]).astype(BF16)
            R.gA[2, to, lt] = mm_tn(xk_ref[:, at], R.dvb[:, lt]).astype(BF16)
            R.gA[3, to, lt] = mm_tn(b_ref[:, at], o_ref[:, lt]).astype(BF16)
            if after is not None:
                after(i)

        loop(D // (2 * LANES), part)

    loop(2, lambda j: arrived(R.xrow.at[rows(pblk(j))], K.in_c, lax.rem(j + h, 2)))

    def self_project(i):
        x = R.xrow[rows(i)].astype(F32)
        y = norm(x, gain(2 * h), shift(2 * h)).astype(BF16)
        R.nrow[rows(i)] = y
        R.q[rows(i)] = mm(y, R.wself[h, 0]).astype(BF16) * jnp.asarray(scale, BF16)
        R.k[rows(i)] = mm(y, R.wself[h, 1]).astype(BF16)
        R.v[rows(i)] = mm(y, R.wself[h, 2]).astype(BF16)

    loop(4, self_project)

    def self_block(i):
        j = lax.rem(i, 2)
        b = jnp.where(i < 2, cp, c) + 2 * j
        set_bias(R.bias, b * B, self_len, self_len, is_b, 0)
        o, lse = attend(R.q[rows(b)], R.k, R.v)
        R.o[rows(b)] = o
        R.lseT[:, rows(b)] = lse
        y = mm_nt(o, R.wself[h, 3])

        @pl.when(i < 2)
        def _():
            R.cs[j] = y.astype(BF16)
            send(R.cs.at[j], R.cr.at[j], K.rs1, core, j).start()

        @pl.when(i >= 2)
        def _():
            R.part[j] = y

        @pl.when(is_b & (i == 0))
        def _():
            loop(nb // 2, lambda k: pass_e0(same_side(k)), 1)

        @pl.when(i == 1)
        def _():
            send_x()

    loop(4, self_block)

    @pl.when(is_b)
    def _():
        loop(nb // 2, lambda k: pass_e0(lax.rem(pair + 2 * k, nb)), 1)

    near_x()

    @pl.when(is_b)
    def _():
        send_e1()
        y_sent(R.we0, K.wy_e0, FQ)

    def self_end(j):
        arrived(R.cr.at[j], K.rs1, j)
        branch = R.part[j] + R.cr[j].astype(F32)
        x = R.xrow[rows(blk(j))].astype(F32)
        y = x + branch
        R.mid[j] = y
        tally(16 + 2 * h, x * x)
        tally(21 + 2 * h, branch * branch)

        @pl.when(is_a)
        def _():
            R.n2row[rows(blk(j))] = norm(y, gain(1), shift(1)).astype(BF16)
            row_copy(R.n2row, blk(j), K.n2, core, j).start()
            tally(17, y * y)

        @pl.when(is_b & (j == 0))
        def _():
            R.fs[...] = branch.astype(BF16)
            send(R.fs, R.fr, K.br3, ypeer).start()

    loop(2, self_end)

    @pl.when(is_b)
    def _():
        finish_x()

    @pl.when(is_a)
    def _():
        if inside:
            loop(nb, lambda i: arrived(wblock(R.we0, 0, h, FQ), K.we0, from_peer(i)), 1)
        send_e1()
        finish_x()
        y_arrived(R.we0, K.wy_e0, FQ)

        def block(i):
            j = lax.rem(i, 2)
            b = jnp.where(i < 2, c, cp) + 2 * j

            @pl.when(i >= 2)
            def _():
                arrived(R.n2row.at[rows(b)], K.n2, j)

            hid = mm(R.n2row[rows(b)], R.we0[0])
            act, slope = gelu_pair(hid)
            R.g0[rows(b)] = act.astype(BF16)
            R.gp0[rows(b)] = slope.astype(BF16)
            y = mm_nt(R.g0[rows(b)], R.we0[1])

            @pl.when(i < 2)
            def _():
                R.part[j] = y

            @pl.when(i >= 2)
            def _():
                sent(R.cs.at[j], K.rs1, j)
                R.cs[j] = y.astype(BF16)
                send(R.cs.at[j], R.cr.at[j], K.rs2, core, j).start()

        loop(4, block)

        def end(j):
            arrived(R.cr.at[j], K.rs2, j)
            branch = R.part[j] + R.cr[j].astype(F32)
            tally(22, branch * branch)
            R.mrow[rows(blk(j))] = (R.mid[j] + branch).astype(BF16)
            row_copy(R.mrow, blk(j), K.m_y, ypeer, j).start()
            row_copy(R.mrow, blk(j), K.m_c, core, j).start()

        loop(2, end)

    @pl.when(is_a)
    def _():
        arrived(R.fr, K.br3)
        R.t1[...] = R.tgt[...].astype(F32) + R.fr[...].astype(F32)

    @pl.when(is_b)
    def _():
        R.t1[...] = R.mid[1]

    one = R.t1[...]
    tally(19, one * one)
    R.n4c[rows(c)] = norm(one, gain(3), shift(3)).astype(BF16)
    row_copy(R.n4c, c, K.n4, core).start()
    y_arrived(R.wx, K.wy_x, LANES)

    arrived(R.n4c.at[rows(cp)], K.n4)
    row_copy(R.b5, s, K.b5, core, 0).start()
    row_copy(R.b5, s, K.b5, ypeer, 1).start()

    def cross_query(i):
        R.q2[rows(i)] = mm(R.n4c[rows(i)], R.wx[0]).astype(BF16) * jnp.asarray(scale, BF16)

    loop(2, cross_query)

    def memory_block(i):
        j = lax.rem(i, 2)
        b = jnp.where(i < 2, c, cp) + 2 * j

        @pl.when((i < 2) & is_b)
        def _():
            arrived(R.mrow.at[rows(b)], K.m_y, j)
            row_copy(R.mrow, b, K.m_c, core, j).start()

        @pl.when(i >= 2)
        def _():
            arrived(R.mrow.at[rows(b)], K.m_c, j)

        y = R.mrow[rows(b)]
        R.k2[rows(b)] = mm(y, R.wx[1]).astype(BF16)
        R.v2[rows(b)] = mm(y, R.wx[2]).astype(BF16)

    loop(4, memory_block)

    def cross_block(i):
        b = jnp.where(i < 1, cp, c)
        set_bias(R.bias, (2 * h + b) * B, tgt_len, src_len, None, 0)
        o, lse = attend(R.q2[rows(b)], R.k2, R.v2)
        R.o2[rows(b)] = o
        R.lse2T[:, rows(b)] = lse
        y = mm_nt(o, R.wx[3])

        @pl.when(i < 1)
        def _():
            R.ds[...] = y.astype(BF16)
            send(R.ds, R.dr.at[0], K.rs4, core).start()

        @pl.when(i >= 1)
        def _():
            R.part[0] = y

    loop(2, cross_block)
    arrived(R.dr.at[0], K.rs4)
    branch4 = R.part[0] + R.dr[0].astype(F32)
    two = R.t1[...] + branch4
    R.t2[...] = two
    R.n5[rows(s)] = norm(two, gain(4), shift(4)).astype(BF16)
    row_copy(R.n5, s, K.n5, ypeer, 1).start()
    row_copy(R.n5, s, K.n5, core, 0).start()
    tally(24, branch4 * branch4)
    tally(20, two * two)

    if inside:
        loop(nb, lambda i: arrived(R.we1.at[:, rows(0, cw), :], K.we1, from_peer(i)), 1)
    arrived(R.b5.at[rows(sc)], K.b5, 0)
    arrived(R.b5.at[rows(sy)], K.b5, 1)
    row_copy(R.b5, sy, K.b5, core, 2).start()

    def around(m):
        return 2 * lax.rem(h + lax.div(m, 2), 2) + lax.rem(c + lax.rem(m, 2), 2)

    def dec_block(m):
        b = around(m)
        hid = mm(R.n5[rows(b)], R.we1[0])
        act, slope = gelu_pair(hid)
        R.g1[rows(b)] = act.astype(BF16)
        dact = mm(R.b5[rows(b)], R.we1[1])
        R.dh1[rows(b)] = (dact * slope).astype(BF16)
        return mm_nt(R.dh1[rows(b)], R.we1[0])

    def dec_step(i):
        m = jnp.where(i < 2, i, 5 - i)

        @pl.when(i == 1)
        def _():
            arrived(R.n5.at[rows(sc)], K.n5, 0)

        @pl.when(i == 2)
        def _():
            arrived(R.n5.at[rows(sy)], K.n5, 1)
            row_copy(R.n5, sy, K.n5, core, 2).start()
            arrived(R.n5.at[rows(around(3))], K.n5, 2)
            arrived(R.b5.at[rows(around(3))], K.b5, 2)

        y = dec_block(m)

        @pl.when(i == 0)
        def _():
            R.part[1] = y

        @pl.when((i == 1) | (i == 2))
        def _():
            R.es6[i - 1] = y.astype(BF16)
            send(R.es6.at[i - 1], R.er6.at[i - 1], K.rs6, core, i - 1).start()

        @pl.when(i == 3)
        def _():
            arrived(R.er6.at[1], K.rs6, 1)
            R.es6[2] = (y + R.er6[1].astype(F32)).astype(BF16)
            send(R.es6.at[2], R.er6.at[2], K.rs6, ypeer, 2).start()

    loop(4, dec_step)

    def dec_forward(i):
        m = 3 - i
        y = mm_nt(R.g1[rows(around(m))], R.we1[1])

        @pl.when(m == 0)
        def _():
            R.last[...] = y

        @pl.when((m == 1) | (m == 3))
        def _():
            at = lax.div(m, 2)
            R.es[at] = y.astype(BF16)
            send(R.es.at[at], R.er.at[at], K.rs5, core, at).start()

        @pl.when(m == 2)
        def _():
            arrived(R.er.at[1], K.rs5, 1)
            R.es[2] = (y + R.er[1].astype(F32)).astype(BF16)
            send(R.es.at[2], R.er.at[2], K.rs5, ypeer, 2).start()

    loop(4, dec_forward)

    def dp_x(a, p):
        at = rows(lax.div(p, 2), cw)
        return send(R.qA.at[a, :, rows(p, cw), :], R.pA.at[a, :, at, :], K.gd_x, (pair, s), a * nb + p)

    def dp_a(a, p):
        return send(
            R.qA.at[a, :, rows(p, cw), :], R.dpA.at[a, lax.div(me, 2)], K.gd_a, (p, s), a * nb + p, a * nb + me
        )

    def dp_e(l, p):
        return send(R.qE.at[l, :, rows(p, cw), :], R.dpE.at[l, me], K.gd_e, (p, s), l * nb + p, l * nb + me)

    def here(src, dst, i):
        return pltpu.make_async_copy(src, dst, R.ss.at[K.here + i])

    def here_a(a):
        return here(R.qA.at[a, :, rows(me, cw), :], R.dpA.at[a, lax.div(me, 2)], a)

    def here_e(l):
        return here(R.qE.at[l, :, rows(me, cw), :], R.dpE.at[l, me], 3 + l)

    def owners(piece, start):
        if inside:

            def one(i):
                p = piece * (nb // 2) + lax.rem(me + i, nb // 2)

                @pl.when(p != me)
                def _():
                    start(p)

            loop(nb // 2, one)

    def dp_a_start(a, piece):
        if inside:

            def one(i):
                dp_x(a, piece * (nb // 2) + 2 * i + lax.rem(pair, 2)).start()

            loop(nb // 4, one)

    def dp_a_pass(a, piece):
        if inside:

            def one(i):
                p = piece * (nb // 2) + 2 * i + lax.rem(me, 2)
                at = rows(lax.div(p, 2), cw)
                arrived(R.pA.at[a, :, at, :], K.gd_x, a * nb + p)
                for m in range(4):
                    total = R.qA[a, m, rows(p, cw)].astype(F32) + R.pA[a, m, at].astype(F32)
                    R.qA[a, m, rows(p, cw)] = total.astype(BF16)

                @pl.when(p != me)
                def _():
                    dp_a(a, p).start()

            loop(nb // 4, one)

    def dp_e_start(l, piece):
        owners(piece, lambda p: dp_e(l, p).start())

    def keep_a(a):
        if inside:
            here_a(a).start()

    def keep_e(l):
        if inside:
            here_e(l).start()

    half_d = 2 * LANES

    def dec_grads(i):
        at, to = lanes(i, 2 * LANES), rows(i, 2 * LANES)
        R.qE[1, 0, to] = mm_tn(R.n5[:, at], R.dh1[...]).astype(BF16)
        R.qE[1, 1, to] = mm_tn(R.b5[:, at], R.g1[...]).astype(BF16)
        dp_e_start(1, i)

    loop(D // (2 * LANES), dec_grads)
    keep_e(1)

    def add_norm(i, dgain, dbias):
        R.acc[pl.ds(i, 1), :] += dgain
        R.acc[pl.ds(5 + i, 1), :] += dbias

    arrived(R.er6.at[0], K.rs6, 0)
    arrived(R.er6.at[2], K.rs6, 2)
    up = R.part[1] + R.er6[0].astype(F32) + R.er6[2].astype(F32)
    back, dgain, dbias = norm_back(R.t2[...], gain(4), up)
    g4 = R.cot[...].astype(F32) + back
    R.g4[...] = g4
    R.b4c[rows(c)] = g4.astype(BF16)
    row_copy(R.b4c, c, K.b4, core).start()
    add_norm(4, dgain, dbias)


    arrived(R.b4c.at[rows(cp)], K.b4)

    def cross_first(i, b):
        return mm(R.b4c[rows(b)], R.wx[3]).astype(BF16)

    def cross_bias(b):
        set_bias(R.biasT, (2 * h + b) * B, tgt_len, src_len, None, 1)

    for t in range(2):
        back_half(
            t, 2, lambda i: i, cross_first if t == 0 else None, R.q2, R.o2, R.lse2T, R.k2, R.v2, cross_bias
        )

    def memory_back(i):
        j = lax.rem(i, 2)
        b = jnp.where(i < 2, cp, c) + 2 * j
        y = mm_nt(R.dkb[rows(b)], R.wx[1]) + mm_nt(R.dvb[rows(b)], R.wx[2])

        @pl.when((i < 2) & is_a)
        def _():
            sent(R.cs.at[j], K.rs2, j)

        @pl.when((i < 2) & is_b)
        def _():
            sent(R.cs.at[j], K.rs1, j)

        @pl.when(i < 2)
        def _():
            R.cs[j] = y.astype(BF16)
            send(R.cs.at[j], R.cr.at[j], K.rs7m, core, j).start()

        @pl.when(i >= 2)
        def _():
            R.dmem[j] = y

    loop(4, memory_back)

    def cross_dx(i):
        b = jnp.where(i < 1, cp, c)
        y = mm_nt(R.dq[rows(b)], R.wx[0])

        @pl.when(i < 1)
        def _():
            sent(R.ds, K.rs4)
            R.ds[...] = y.astype(BF16)
            send(R.ds, R.dr.at[1], K.rs7q, core).start()

        @pl.when(i >= 1)
        def _():
            R.part[0] = y

    loop(2, cross_dx)

    def memory_sum(j):
        arrived(R.cr.at[j], K.rs7m, j)
        y = R.dmem[j] + R.cr[j].astype(F32)
        R.dmem[j] = y

        @pl.when(is_b)
        def _():
            R.be[rows(j)] = y.astype(BF16)
            send(R.be.at[rows(j)], R.dmr.at[j], K.dm, ypeer, j).start()

    loop(2, memory_sum)

    arrived(R.dr.at[1], K.rs7q)
    back, dgain, dbias = norm_back(R.t1[...], gain(3), R.part[0] + R.dr[1].astype(F32))
    g3 = R.g4[...] + back
    R.g3[...] = g3

    @pl.when(is_a)
    def _():
        R.fs[...] = g3.astype(BF16)
        send(R.fs, R.brow.at[rows(c)], K.g3, ypeer).start()

    add_norm(3, dgain, dbias)

    arrived(R.er.at[0], K.rs5, 0)
    arrived(R.er.at[2], K.rs5, 2)
    branch5 = R.last[...] + R.er[0].astype(F32) + R.er[2].astype(F32)
    tally(25, branch5 * branch5)
    R.dec[...] = R.t2[...] + branch5

    def cross_grads(t):
        half_grads(t, R.n4c, R.mrow, R.dq.at[0:2 * B], R.o2, R.b4c)

    def y_grad_x():
        return send(R.gA.at[:, :, lanes(1 - h)], R.ylX, K.gy_x, ypeer)

    def y_grad_s(i):
        at = rows(i, half_d)
        return send(R.gA.at[:, at, lanes(1 - h)], R.qA.at[h, :, at, :], K.gy_s, ypeer, i)

    cross_grads(1 - h)

    @pl.when(is_a)
    def _():
        y_grad_x().start()

    cross_grads(h)

    def join_x():
        arrived(R.ylX, K.gy_x)
        for m in range(4):
            total = R.gA[m, :, lanes(h)].astype(F32) + R.ylX[m].astype(F32)
            R.qA[2, m] = total.astype(BF16)
        for piece in range(2):
            dp_a_start(2, piece)

    def pass_a(a):
        for piece in range(2):
            dp_a_pass(a, piece)
        keep_a(a)

    if inside:

        def chosen_sent(i):
            for l in range(2):
                sent(wblock(R.gE, 0, l, FQ), (K.we0, K.we1)[l], to_peer(i))

        loop(nb, chosen_sent, 1)

    def e_grad(i):
        at = rows(i, half_d)
        return send(R.gE.at[:, at, lanes(1 - h, FQ)], R.qE.at[0, :, at, :], K.gy_e0, ypeer, i)

    @pl.when(is_a)
    def _():
        def block(i):
            j = lax.rem(i, 2)
            b = jnp.where(i < 2, c, cp) + 2 * j

            @pl.when(i < 2)
            def _():
                arrived(R.dmr.at[j], K.dm, j)
                x = R.dmem[j] + R.dmr[j].astype(F32)
                R.dmem[j] = x
                R.be[rows(b)] = x.astype(BF16)
                row_copy(R.be, b, K.be, core, j).start()

            @pl.when(i >= 2)
            def _():
                arrived(R.be.at[rows(b)], K.be, j)

            dact = mm(R.be[rows(b)], R.we0[1])
            R.gp0[rows(b)] = (dact * R.gp0[rows(b)].astype(F32)).astype(BF16)
            y = mm_nt(R.gp0[rows(b)], R.we0[0])

            @pl.when(i < 2)
            def _():
                R.part[j] = y

            @pl.when(i >= 2)
            def _():
                sent(R.cs.at[j], K.rs7m, j)
                R.cs[j] = y.astype(BF16)
                send(R.cs.at[j], R.cr.at[j], K.rs8, core, j).start()

        loop(4, block)

        def end(j):
            arrived(R.cr.at[j], K.rs8, j)
            up = R.part[j] + R.cr[j].astype(F32)
            back, dgain, dbias = norm_back(R.mid[j], gain(1), up)
            add_norm(1, dgain, dbias)
            g = R.dmem[j] + back
            R.dmem[j] = g
            R.brow[rows(blk(j))] = g.astype(BF16)
            row_copy(R.brow, blk(j), K.brow, core, j).start()

        loop(2, end)

        for half in (1, 0):

            def part(i, half=half):
                at, to, lf = lanes(i, 2 * LANES), rows(i, 2 * LANES), pl.ds(half * FQ, FQ)
                up_part = mm_tn(R.n2row[:, at], R.gp0[:, lf]).astype(BF16)
                down_part = mm_tn(R.be[:, at], R.g0[:, lf]).astype(BF16)
                if half == 1:
                    R.gE[0, to, lf] = up_part
                    R.gE[1, to, lf] = down_part
                    e_grad(i).start()
                else:
                    R.qE[0, 0, to] = up_part
                    R.qE[0, 1, to] = down_part
                    dp_e_start(0, i)

            loop(D // (2 * LANES), part)
        keep_e(0)

    @pl.when(is_b)
    def _():
        R.brow[rows(blk(1))] = R.g3[...].astype(BF16)
        arrived(R.brow.at[rows(blk(0))], K.g3)
        for j in range(2):
            row_copy(R.brow, blk(j), K.brow, core, j).start()

    def self_block_of(i):
        return jnp.where(i < 2, c, cp) + 2 * lax.rem(i, 2)

    def self_first(i, b):
        @pl.when(i >= 2)
        def _():
            arrived(R.brow.at[rows(b)], K.brow, lax.rem(i, 2))

        return mm(R.brow[rows(b)], R.wself[h, 3]).astype(BF16)

    def self_bias(b):
        set_bias(R.biasT, b * B, self_len, self_len, is_b, 1)

    def self_half(t, first_pass):
        back_half(t, 4, self_block_of, first_pass, R.q, R.o, R.lseT, R.k, R.v, self_bias)

    @pl.when(is_b)
    def _():
        for j in range(2):
            sent(R.be.at[rows(j)], K.dm, j)
        y_grad_x().start()

    self_half(1 - h, self_first)
    join_x()

    y_grad_x().wait_send()
    half_grads(1 - h, R.nrow, R.nrow, R.dq, R.o, R.brow, lambda i: y_grad_s(i).start())

    self_half(h, None)
    pass_a(2)

    def own_piece(i):
        at = rows(i, half_d)
        for m in range(4):
            R.qA[h, m, at] = R.gA[m, at, lanes(h)]
        dp_a_start(h, i)

    half_grads(h, R.nrow, R.nrow, R.dq, R.o, R.brow, own_piece)

    def other_pieces():
        for piece in range(2):
            at = rows(piece, half_d)
            arrived(R.qA.at[1 - h, :, at, :], K.gy_s, piece)
            dp_a_start(1 - h, piece)

    @pl.when(is_a)
    def _():
        other_pieces()

    def self_dx(i):
        j = lax.rem(i, 2)
        b = jnp.where(i < 2, cp, c) + 2 * j
        y = mm_nt(R.dq[rows(b)], R.wself[h, 0])
        y = y + mm_nt(R.dkb[rows(b)], R.wself[h, 1])
        y = y + mm_nt(R.dvb[rows(b)], R.wself[h, 2])

        @pl.when((i < 2) & is_a)
        def _():
            sent(R.cs.at[j], K.rs8, j)

        @pl.when((i < 2) & is_b)
        def _():
            sent(R.cs.at[j], K.rs7m, j)

        @pl.when(i < 2)
        def _():
            R.cs[j] = y.astype(BF16)
            send(R.cs.at[j], R.cr.at[j], K.rs9, core, j).start()

        @pl.when(i >= 2)
        def _():
            R.part[j] = y

    loop(4, self_dx)

    def self_final(i):
        j = jnp.where(is_a, 1 - i, i)
        arrived(R.cr.at[j], K.rs9, j)
        x = R.xrow[rows(blk(j))].astype(F32)
        back, dgain, dbias = norm_back(x, gain(2 * h), R.part[j] + R.cr[j].astype(F32))
        add_norm(2 * h, dgain, dbias)

        @pl.when(is_a & (j == 0))
        def _():
            R.sgrad[...] = R.dmem[0] + back

        @pl.when(is_a & (j == 1))
        def _():
            sent(R.fs, K.g3)
            R.fs[...] = (R.dmem[1] + back).astype(BF16)
            send(R.fs, R.fr, K.fin, ypeer).start()

        @pl.when(is_b & (j == 0))
        def _():
            sent(R.fs, K.br3)
            R.fs[...] = back.astype(BF16)
            send(R.fs, R.fr, K.fin, ypeer).start()

        @pl.when(is_b & (j == 1))
        def _():
            R.tgrad[...] = R.g3[...] + back

    loop(2, self_final)
    pass_a(h)

    @pl.when(is_a)
    def _():
        pass_a(1 - h)

    @pl.when(is_b)
    def _():
        for piece in range(2):
            arrived(R.qE.at[0, :, rows(piece, half_d), :], K.gy_e0, piece)
            dp_e_start(0, piece)
        keep_e(0)
        other_pieces()
        pass_a(1 - h)

    send(R.acc, R.accc, K.accc, core).start()
    arrived(R.accc, K.accc)
    R.acc1[...] = R.acc[...] + R.accc[...]
    send(R.acc1, R.accy, K.accy, ypeer).start()
    arrived(R.accy, K.accy)
    R.acc2[...] = R.acc1[...] + R.accy[...]
    R.stats[...] = R.acc2[16:32, :]

    if inside:

        def tile_of(p):
            return lanes(lax.div(p * cw, LANES))

        def acc_copy(p):
            return send(R.acc2.at[0:16, tile_of(p)], R.accd.at[me], K.accd, (p, s), p, me)

        loop(nb, lambda i: acc_copy(to_peer(i)).start(), 1)
        R.picks[...] = R.smallr[...]
    arrived(R.fr, K.fin)

    @pl.when(is_a)
    def _():
        R.tgrad[...] = R.g3[...] + R.fr[...].astype(F32)

    @pl.when(is_b)
    def _():
        R.sgrad[...] = R.fr[...].astype(F32)

    if inside:
        loop(nb, lambda i: arrived(R.accd.at[0], K.accd, from_peer(i)), 1)
        R.ggb[...] = R.acc2[0:16, tile_of(me)]

        def more(i):
            R.ggb[...] += R.accd[from_peer(i)]

        loop(nb, more, 1)
        for l in range(2):
            loop(nb, lambda i, l=l: arrived(R.dpE.at[l, 0], K.gd_e, l * nb + from_peer(i)), 1)
            here_e(l).wait()
        for a in range(3):
            loop(nb // 2, lambda i, a=a: arrived(R.dpA.at[a, 0], K.gd_a, a * nb + same_side(i)), 1)
            here_a(a).wait()
    else:
        R.gacc[...] = R.acc2[0:16, :]

    for name in (K.in_y, K.n4, K.b4, K.rs7q, K.fin):
        sent(R.oth, name)
    for name in (K.in_c, K.m_c, K.brow, K.rs9):
        for j in range(2):
            sent(R.oth, name, j)
    for name in (K.b5, K.n5, K.rs5, K.rs6):
        for j in range(3):
            sent(R.oth, name, j)
    y_sent(other, K.wy_self, LANES)
    y_sent(R.wx, K.wy_x, LANES)
    for piece in range(2):
        y_grad_s(piece).wait_send()
    sent(R.acc, K.accc)
    sent(R.acc1, K.accy)

    @pl.when(is_a)
    def _():
        for name in (K.n2, K.m_y, K.be):
            for j in range(2):
                sent(R.oth, name, j)
        for piece in range(2):
            e_grad(piece).wait_send()

    if inside:

        def drain_side(i):
            for a in range(3):
                sent(R.sendA.at[0], K.wa, a * nb + same_side(i))
                sent(R.sendA.at[0], K.wr, a * nb + same_side(i))
                sent(R.sendA.at[0], K.gd_a, a * nb + same_side(i))
                sent(R.sendA.at[0], K.gd_x, a * nb + lax.rem(pair + 2 * i, nb))

        for a in range(3):
            sent(R.sendA.at[0], K.wa, a * nb + pair)
            sent(R.sendA.at[0], K.gd_x, a * nb + pair)
        loop(nb // 2, drain_side, 1)

        def drain(i):
            p = to_peer(i)
            sent(R.small, K.small, p)
            for l in range(2):
                sent(R.qE.at[l, :, rows(0, cw), :], K.gd_e, l * nb + p)
            sent(R.accd.at[0], K.accd, p)

        loop(nb, drain, 1)


def close_kernel(cfg, names, *refs):
    nb, cw, B, D, FQ, E, _ = cfg
    R = SimpleNamespace(**dict(zip(names, refs, strict=True)))
    dp = lax.axis_index("dp")

    def copy(src, dst, i):
        return pltpu.make_async_copy(src, dst, R.sem.at[i])

    plain = [(R.dec, R.o_dec), (R.sgrad, R.o_sgrad), (R.tgrad, R.o_tgrad)]
    for i, (src, _) in enumerate(plain):
        copy(src, R.vp.at[i], i).start()
    for l in range(2):
        copy(R.dpE.at[l], R.ve.at[l], 3 + l).start()
    for a in range(3):
        copy(R.dpA.at[a], R.va.at[a], 5 + a).start()

    stats = jnp.sum(R.stats[...], -1, keepdims=True) * (1.0 / (4 * B * D))
    root = jnp.broadcast_to(jnp.sqrt(stats), (16, LANES))
    place = lax.broadcasted_iota(jnp.int32, (16, LANES), 0) - lax.broadcasted_iota(jnp.int32, (16, LANES), 1)
    for k in range(2):
        line = jnp.sum(jnp.where(place == 5 * k, root, 0.0), 0, keepdims=True)
        R.o_rms[0, k:k + 1, :] = line[:, 0:5]
    for k in range(LANES // cw):

        @pl.when(lax.rem(dp, LANES // cw) == k)
        def _(k=k):
            R.o_gain[...] = R.ggb[0:5, k * cw:(k + 1) * cw]
            R.o_bias[...] = R.ggb[5:10, k * cw:(k + 1) * cw]

    for i, (src, dst) in enumerate(plain):
        copy(src, R.vp.at[i], i).wait()
        copy(R.vp.at[i], dst, i).start()
    for l in range(2):
        copy(R.dpE.at[l], R.ve.at[l], 3 + l).wait()
        for e in range(E):
            hits = []
            for p in range(nb):
                hit = jnp.where(R.picks[p, 10 + l:11 + l, :] == float(e), 1.0, 0.0)
                hits.append(jnp.concatenate([hit] * (FQ // LANES), axis=1))
            for m, total_ref in enumerate((R.w_up, R.w_dn)):
                total = R.ve[l, 0, m].astype(F32) * hits[0]
                for p in range(1, nb):
                    total = total + R.ve[l, p, m].astype(F32) * hits[p]
                total_ref[l, e] = total
        copy(R.w_up.at[l], R.o_up.at[l], 8 + l).start()
        copy(R.w_dn.at[l], R.o_dn.at[l], 10 + l).start()
    for a in range(3):
        copy(R.dpA.at[a], R.va.at[a], 5 + a).wait()
        for m in range(4):
            total = R.va[a, 0, m].astype(F32)
            for p in range(1, nb // 2):
                total = total + R.va[a, p, m].astype(F32)
            if m < 3:
                R.w_qkv[a, m] = total
            else:
                R.w_out[a] = total
    copy(R.w_qkv, R.o_qkv, 12).start()
    copy(R.w_out, R.o_out, 13).start()
    for i, (_, dst) in enumerate(plain):
        copy(R.vp.at[i], dst, i).wait()
    for l in range(2):
        copy(R.w_up.at[l], R.o_up.at[l], 8 + l).wait()
        copy(R.w_dn.at[l], R.o_dn.at[l], 10 + l).wait()
    copy(R.w_qkv, R.o_qkv, 12).wait()
    copy(R.w_out, R.o_out, 13).wait()


def on_device(
    src_input,
    tgt_input,
    out_cotangent,
    src_lengths,
    tgt_lengths,
    enc_expert,
    dec_expert,
    norm_gains,
    norm_biases,
    qkv_weight,
    out_weight,
    expert_up,
    expert_down,
):
    n = lax.axis_size("dp")
    B, D = src_input.shape[1:]
    cw = norm_gains.shape[1]
    FQ = expert_up.shape[3]
    E = expert_up.shape[1]
    inside = cw % 16 == 0 and LANES % cw == 0 and n % 4 == 0
    wot = jnp.swapaxes(out_weight, 1, 2)
    dnt = jnp.swapaxes(expert_down, 2, 3)
    vmem = pl.BlockSpec(memory_space=pltpu.VMEM)
    smem = pl.BlockSpec(memory_space=pltpu.SMEM)
    anywhere = pl.BlockSpec(memory_space=pl.ANY)

    def f32(*shape):
        return jax.ShapeDtypeStruct(shape, F32)

    def bf16(*shape):
        return jax.ShapeDtypeStruct(shape, BF16)

    scalars = dict(slen=src_lengths, tlen=tgt_lengths)
    operands = dict(src=src_input[0], tgt=tgt_input[0], cot=out_cotangent[0])
    results = dict(dec=f32(B, D), sgrad=f32(B, D), tgrad=f32(B, D), stats=f32(16, D))
    far = {}
    if inside:
        nb, rowsize = n, cw
        scalars.update(epick=enc_expert, dpick=dec_expert)
        operands.update(gains=norm_gains, biases=norm_biases, qkv=qkv_weight, wot=wot, up=expert_up, dnt=dnt)
        results.update(ggb=f32(16, LANES), picks=f32(n, 16, LANES))
        far = dict(dpA=bf16(3, n // 2, 4, cw, LANES), dpE=bf16(2, n, 2, cw, FQ))
    else:
        nb, rowsize = 1, D
        gb = jnp.concatenate([norm_gains, norm_biases], 0).astype(F32)
        small = lax.all_gather(gb, "dp", axis=1, tiled=True)
        small = jnp.concatenate([small, jnp.zeros((6, D), F32)], 0)
        wa = jnp.concatenate([qkv_weight, wot[:, None]], 1)
        wa = lax.all_gather(wa, "dp", axis=2, tiled=True)
        picks = jnp.stack([enc_expert[0, 0], dec_expert[0, 0]])
        we = jnp.stack([expert_up, dnt], 2)
        we = lax.all_gather(we, "dp", axis=3, tiled=True)
        we = jnp.stack([jnp.take(we[l], picks[l], axis=0) for l in range(2)])
        operands.update(small=small, wa=wa, we=we)
        results.update(qA=bf16(3, 4, D, LANES), qE=bf16(2, 2, D, FQ), gacc=f32(16, D))
    cfg = (nb, rowsize, B, D, FQ, E, inside)
    scratch = scratch_list(nb, rowsize, B, D, FQ, inside)
    count = sem_list(nb)[1]
    scratch.update(ss=pltpu.SemaphoreType.DMA((count,)), rs=pltpu.SemaphoreType.DMA((count,)))
    names = tuple(scalars) + tuple(operands) + tuple(results) + tuple(far) + tuple(scratch)
    outs = pl.pallas_call(
        functools.partial(step_kernel, cfg, names),
        name="step",
        out_shape=tuple(results.values()) + tuple(far.values()),
        in_specs=[smem] * len(scalars) + [vmem] * len(operands),
        out_specs=[vmem] * len(results) + [anywhere] * len(far),
        scratch_shapes=list(scratch.values()),
        compiler_params=pltpu.CompilerParams(
            collective_id=1, has_side_effects=True, vmem_limit_bytes=63 << 20
        ),
        cost_estimate=pl.CostEstimate(flops=17 << 30, bytes_accessed=8 << 20, transcendentals=16 << 20),
    )(*scalars.values(), *operands.values())
    made = dict(zip(tuple(results) + tuple(far), outs, strict=True))
    if inside:
        near = dict(stats=vmem, ggb=vmem, picks=vmem, dec=anywhere, sgrad=anywhere, tgrad=anywhere)
        near.update(dpA=anywhere, dpE=anywhere)
        last = dict(
            o_dec=f32(B, D),
            o_sgrad=f32(B, D),
            o_tgrad=f32(B, D),
            o_gain=f32(5, cw),
            o_bias=f32(5, cw),
            o_qkv=f32(3, 3, cw, LANES),
            o_out=f32(3, cw, LANES),
            o_up=f32(2, E, cw, FQ),
            o_dn=f32(2, E, cw, FQ),
            o_rms=f32(1, 2, 5),
        )
        held = dict(
            vp=pltpu.VMEM((3, B, D), F32),
            ve=pltpu.VMEM((2, n, 2, cw, FQ), BF16),
            va=pltpu.VMEM((3, n // 2, 4, cw, LANES), BF16),
            w_up=pltpu.VMEM((2, E, cw, FQ), F32),
            w_dn=pltpu.VMEM((2, E, cw, FQ), F32),
            w_qkv=pltpu.VMEM((3, 3, cw, LANES), F32),
            w_out=pltpu.VMEM((3, cw, LANES), F32),
            sem=pltpu.SemaphoreType.DMA((14,)),
        )
        small_outs = [k in (3, 4, 9) for k in range(len(last))]
        dec, sgrad, tgrad, gains, biases, gqkv, gout, gup, gdn, rms = pl.pallas_call(
            functools.partial(close_kernel, cfg, tuple(near) + tuple(last) + tuple(held)),
            name="close",
            out_shape=tuple(last.values()),
            in_specs=list(near.values()),
            out_specs=[vmem if near_by else anywhere for near_by in small_outs],
            scratch_shapes=list(held.values()),
            compiler_params=pltpu.CompilerParams(vmem_limit_bytes=63 << 20),
            cost_estimate=pl.CostEstimate(flops=16 << 20, bytes_accessed=10 << 20, transcendentals=0),
        )(*[made[name] for name in near])
    else:
        dec, sgrad, tgrad, stats, ga, ge, gacc = outs

        def total(x, axis):
            return lax.psum_scatter(x, "dp", scatter_dimension=axis, tiled=True)

        gains, biases = total(gacc[0:5], 1), total(gacc[5:10], 1)
        ga = total(ga.astype(F32), 2)
        gqkv, gout = ga[:, :3], ga[:, 3]
        match = (picks[:, None] == jnp.arange(E, dtype=jnp.int32)[None]).astype(F32)
        ge = ge.astype(F32)[:, None] * match[:, :, None, None, None]
        ge = total(ge, 3)
        gup, gdn = ge[:, :, 0], ge[:, :, 1]
        length = B * lax.axis_size("seq")
        rms = jnp.sqrt(jnp.sum(stats[:10], 1) / (length * D)).reshape(1, 2, 5)
    return (
        dec[None],
        sgrad[None],
        tgrad[None],
        gains,
        biases,
        gqkv,
        jnp.swapaxes(gout, 1, 2),
        gup,
        jnp.swapaxes(gdn, 2, 3),
        rms,
    )


def solution(mesh):
    placed = (
        P("dp", "seq", None),
        P("dp", "seq", None),
        P("dp", "seq", None),
        P("dp", None),
        P("dp", None),
        P("dp", None),
        P("dp", None),
        P(None, "dp"),
        P(None, "dp"),
        P(None, None, "dp", "seq"),
        P(None, "seq", "dp"),
        P(None, None, "dp", "seq"),
        P(None, None, "seq", "dp"),
    )
    return jax.shard_map(
        on_device,
        mesh=mesh,
        in_specs=placed,
        out_specs=(
            P("dp", "seq", None),
            P("dp", "seq", None),
            P("dp", "seq", None),
            P(None, "dp"),
            P(None, "dp"),
            P(None, None, "dp", "seq"),
            P(None, "seq", "dp"),
            P(None, None, "dp", "seq"),
            P(None, None, "seq", "dp"),
            P("dp", None, None),
        ),
        check_vma=False,
    )
```

```python
import functools
import math
from types import SimpleNamespace

import jax
import jax.numpy as jnp
from jax import lax
from jax.experimental import pallas as pl
from jax.experimental.pallas import tpu as pltpu
from jax.sharding import PartitionSpec as P

HEAD_DIM = 64
EPSILON = 1e-05
MASKED = -1e30
LANES = 128
F32 = jnp.float32
BF16 = jnp.bfloat16
MESH = pl.DeviceIdType.MESH
GELU_A = math.sqrt(2.0 / math.pi)
GELU_B = 0.044715


def mm(a, b):
    return lax.dot_general(a, b, (((1,), (0,)), ((), ())), preferred_element_type=F32)


def mm_nt(a, b):
    return lax.dot_general(a, b, (((1,), (1,)), ((), ())), preferred_element_type=F32)


def mm_tn(a, b):
    return lax.dot_general(a, b, (((0,), (0,)), ((), ())), preferred_element_type=F32)


def centre(x):
    mean = jnp.mean(x, -1, keepdims=True)
    xc = x - mean
    var = jnp.mean(xc * xc, -1, keepdims=True)
    scale = lax.rsqrt(var + EPSILON)
    return xc * scale, scale


def norm(x, gain, shift):
    return centre(x)[0] * gain + shift


def norm_back(x, gain, up):
    xh, scale = centre(x)
    dgain = jnp.sum(up * xh, 0, keepdims=True)
    dbias = jnp.sum(up, 0, keepdims=True)
    dxh = up * gain
    m1 = jnp.mean(dxh, -1, keepdims=True)
    m2 = jnp.mean(dxh * xh, -1, keepdims=True)
    return scale * (dxh - m1 - xh * m2), dgain, dbias


def gelu_pair(x):
    square = x * x
    t = jnp.tanh(x * (GELU_A + (GELU_A * GELU_B) * square))
    half = 0.5 + 0.5 * t
    slope = half + (0.5 * x) * (1.0 - t * t) * (GELU_A + (3.0 * GELU_A * GELU_B) * square)
    return x * half, slope


def scratch_list(nb, cw, B, D, FQ, inside):
    L, F2, KW = 4 * B, 2 * FQ, 2 * LANES

    def b(*shape):
        return pltpu.VMEM(shape, BF16)

    def f(*shape):
        return pltpu.VMEM(shape, F32)

    out = dict(
        xrow=b(L, D),
        oth=b(B, D),
        nrow=b(L, D),
        wself=b(2, 4, D, KW),
        wx=b(4, D, KW),
        we0=b(2, D, FQ),
        we1=b(2, D, FQ),
        gtab=f(16, D),
        q=b(L, KW),
        k=b(L, KW),
        v=b(L, KW),
        o=b(L, KW),
        do=b(L, KW),
        lseT=f(8, L),
        drowT=f(16, L),
        bias=f(B, L),
        biasT=f(L, B),
        part=f(2, B, D),
        cs=b(2, B, D),
        cr=b(2, B, D),
        mid=f(2, B, D),
        n2row=b(L, D),
        g0=b(L, FQ),
        gp0=b(L, FQ),
        ms=b(2, B, D),
        dxr=b(2, B, D),
        mrow=b(L, D),
        fs=b(B, D),
        fr=b(B, D),
        t1=f(B, D),
        n4c=b(2 * B, D),
        q2=b(2 * B, KW),
        k2=b(L, KW),
        v2=b(L, KW),
        o2=b(2 * B, KW),
        lse2T=f(8, 2 * B),
        ds=b(B, D),
        dr=b(2, B, D),
        t2=f(B, D),
        n5=b(L, D),
        b5=b(L, D),
        g1=b(L, FQ),
        dh1=b(L, FQ),
        es=b(3, B, D),
        er=b(3, B, D),
        es6=b(3, B, D),
        er6=b(3, B, D),
        g4=f(B, D),
        last=f(B, D),
        b4c=b(2 * B, D),
        dkf=f(L, LANES),
        dvf=f(L, LANES),
        dkb=b(L, KW),
        dvb=b(L, KW),
        dmr=b(2, B, D),
        g3=f(B, D),
        brow=b(L, D),
        dmem=f(2, B, D),
        be=b(L, D),
        dq=b(L, KW),
        gA=b(4, D, KW),
        ylX=b(4, D, LANES),
        acc=f(32, D),
        acc1=f(32, D),
        acc2=f(32, D),
        accc=f(32, D),
        accy=f(32, D),
    )
    if inside:
        out.update(
            small=f(16, LANES),
            smallr=f(nb, 16, LANES),
            sendA=b(3, 4, cw, LANES),
            gE=b(2, D, F2),
            qA=b(3, 4, D, LANES),
            pA=b(3, 4, D // 2, LANES),
            qE=b(2, 2, D, FQ),
            accd=f(nb, 16, LANES),
        )
    return out


def sem_list(nb):
    counts = dict(
        in_y=1,
        in_c=2,
        b5=3,
        small=nb,
        wa=3 * nb,
        wr=3 * nb,
        we0=nb,
        we1=nb,
        wy_self=nb,
        wy_x=nb,
        rs1=2,
        n2=2,
        rs2=2,
        br3=1,
        m_y=2,
        m_c=2,
        n4=1,
        rs4=1,
        n5=3,
        rs5=3,
        rs6=3,
        b4=1,
        rs7q=1,
        rs7m=2,
        dm=2,
        g3=1,
        brow=2,
        be=2,
        rs8=2,
        rs9=2,
        fin=1,
        gy_s=2,
        gy_x=1,
        dx=2,
        n2y=2,
        gd_a=3 * nb,
        gd_x=3 * nb,
        gd_e=2 * nb,
        accc=1,
        accy=1,
        accd=nb,
        here=5,
    )
    base, at = {}, 0
    for name, number in counts.items():
        base[name] = at
        at = at + number
    return SimpleNamespace(**base), at


def step_kernel(cfg, names, *refs):
    nb, cw, B, D, FQ, E, inside = cfg
    L, F2, KW = 4 * B, 2 * FQ, 2 * LANES
    R = SimpleNamespace(**dict(zip(names, refs, strict=True)))
    K, _ = sem_list(nb)

    dp = lax.axis_index("dp")
    me = dp if inside else 0
    s = lax.axis_index("seq")
    h = lax.div(s, 2)
    c = lax.rem(s, 2)
    cp = 1 - c
    sc = s + 1 - 2 * c
    sy = s + 2 - 4 * h
    core, ypeer = (dp, sc), (dp, sy)
    is_a, is_b = h == 0, h == 1

    def rows(i, size=B):
        return pl.ds(pl.multiple_of(i * size, size), size)

    def lanes(i, size=LANES):
        return pl.ds(pl.multiple_of(i * size, size), size)

    def send(src, dst, name, to, i=0, j=None):
        return pltpu.make_async_remote_copy(
            src_ref=src,
            dst_ref=dst,
            send_sem=R.ss.at[name + i],
            recv_sem=R.rs.at[name + (i if j is None else j)],
            device_id=to,
            device_id_type=MESH,
        )

    def arrived(dst, name, i=0):
        send(dst, dst, name, core, i).wait_recv()

    def sent(src, name, i=0):
        send(src, src, name, core, i).wait_send()

    def loop(count, body, start=0):
        def step(i, carry):
            body(i)
            return carry

        lax.fori_loop(start, count, step, 0)

    def flip(a, m):
        out, bit = a, 1
        while bit < nb:
            out = out + bit * lax.rem(lax.div(m, bit), 2) * (1 - 2 * lax.rem(lax.div(a, bit), 2))
            bit = 2 * bit
        return out

    def to_peer(i):
        return flip(me, i)

    from_peer = to_peer
    pair = me + 1 - 2 * lax.rem(me, 2)

    barrier = pltpu.get_barrier_semaphore()
    for to in (core, ypeer):
        pl.semaphore_signal(barrier, inc=1, device_id=to, device_id_type=MESH)

    def greet(i):
        pl.semaphore_signal(barrier, inc=1, device_id=(to_peer(i), s), device_id_type=MESH)

    loop(nb, greet, 1)

    if inside:
        R.small[...] = jnp.zeros((16, LANES), F32)
        for k in range(LANES // cw):

            @pl.when(lax.rem(dp, LANES // cw) == k)
            def _(k=k):
                R.small[0:5, k * cw:(k + 1) * cw] = R.gains[...].astype(F32)
                R.small[5:10, k * cw:(k + 1) * cw] = R.biases[...].astype(F32)

        R.small[10:11, :] = jnp.broadcast_to(R.epick[0, 0].astype(F32), (1, LANES))
        R.small[11:12, :] = jnp.broadcast_to(R.dpick[0, 0].astype(F32), (1, LANES))

    @pl.when(is_a)
    def _():
        R.xrow[rows(s)] = R.src[...]
        R.oth[...] = R.tgt[...]

    @pl.when(is_b)
    def _():
        R.xrow[rows(s)] = R.tgt[...]
        R.oth[...] = R.src[...]

    R.b5[rows(s)] = R.cot[...]
    for a in range(3):
        if inside:
            for j in range(3):
                R.sendA[a, j] = R.qkv[a, j]
            R.sendA[a, 3] = R.wot[a]
        buf = R.wself.at[a] if a < 2 else R.wx
        piece = R.sendA if inside else R.wa
        for j in range(4):
            buf[j, rows(me, cw), lanes(h)] = piece[a, j]
    pl.semaphore_wait(barrier, nb + 1)

    def small_copy(p):
        return send(R.small, R.smallr.at[me], K.small, (p, s), p, me)

    def wblock(buf, p, half, width):
        return buf.at[:, rows(p, cw), lanes(half, width)]

    def held(a):
        return R.wself.at[a] if a < 2 else R.wx

    def a_copy(a, p):
        return send(R.sendA.at[a], wblock(held(a), me, h, LANES), K.wa, (p, s), a * nb + p, a * nb + me)

    def a_relay(a, p):
        at = wblock(held(a), p, h, LANES)
        return send(at, at, K.wr, (pair, s), a * nb + p)

    def y_block(buf, p, name, width):
        at = wblock(buf, p, h, width)
        return send(at, at, name, ypeer, p)

    def same_side(i):
        return flip(me, 2 * i)

    def far_side(i):
        return flip(pair, 2 * i)

    def e_copy(l, p):
        at = (R.we0, R.we1)[l].at[:, rows(me, cw), :]
        return send(wblock(R.gE, p, l, FQ), at, (K.we0, K.we1)[l], (p, s), p, me)

    def row_copy(buf, block, name, to, i=0):
        at = buf.at[rows(block)]
        return send(at, at, name, to, i)

    if inside:
        loop(nb, lambda i: small_copy(to_peer(i)).start(), 1)
    send(R.oth, R.xrow.at[rows(s)], K.in_y, ypeer).start()
    row_copy(R.xrow, s, K.in_c, core, 0).start()
    if inside:

        def spread_self(i):
            for a in range(2):
                a_copy(a, same_side(i)).start()

        loop(nb // 2, spread_self, 1)
        for a in range(2):
            a_copy(a, pair).start()
    other = R.wself.at[1 - h]
    y_block(other, me, K.wy_self, LANES).start()

    if inside:
        loop(nb, lambda i: arrived(R.smallr.at[0], K.small, from_peer(i)), 1)
        R.smallr[pl.ds(me, 1)] = R.small[...][None]
        per = LANES // cw
        for t in range(D // LANES):
            tile = R.smallr[t * per]
            for k in range(1, per):
                tile = tile + R.smallr[t * per + k]
            R.gtab[:, t * LANES:(t + 1) * LANES] = tile

        def chosen(l, p):
            row = R.smallr[p, pl.ds(10 + l, 1), :]
            for m, shard in enumerate((R.up, R.dnt)):
                total = None
                for e in range(E):
                    hit = jnp.where(row == float(e), 1.0, 0.0)
                    hit = jnp.concatenate([hit] * (FQ // LANES), axis=1)
                    term = shard[l, e].astype(F32) * hit
                    total = term if total is None else total + term
                R.gE[m, rows(p, cw), lanes(l, FQ)] = total.astype(BF16)

        loop(nb, lambda p: chosen(0, p))
        for m in range(2):
            R.we0[m, rows(me, cw), :] = R.gE[m, rows(me, cw), lanes(0, FQ)]

    arrived(R.xrow.at[rows(sy)], K.in_y)
    row_copy(R.xrow, sy, K.in_c, core, 1).start()

    if inside:

        def near(i):
            p = same_side(i)
            for a in range(2):
                arrived(wblock(held(a), p, h, LANES), K.wa, a * nb + p)
                a_relay(a, p).start()
            y_block(other, p, K.wy_self, LANES).start()

        def far(i):
            p = far_side(i)
            for a in range(2):
                arrived(wblock(held(a), p, h, LANES), K.wr, a * nb + p)
            y_block(other, p, K.wy_self, LANES).start()

        for a in range(2):
            arrived(wblock(held(a), pair, h, LANES), K.wa, a * nb + pair)
        y_block(other, pair, K.wy_self, LANES).start()
        loop(nb // 2, near, 1)
        loop(nb // 2, lambda i: a_copy(2, same_side(i)).start(), 1)
        a_copy(2, pair).start()
        loop(nb // 2, far, 1)
        e_copy(0, pair).start()
        loop(nb // 2, lambda i: e_copy(0, same_side(i)).start(), 1)
        loop(nb, lambda p: chosen(1, p))
        for m in range(2):
            R.we1[m, rows(me, cw), :] = R.gE[m, rows(me, cw), lanes(1, FQ)]
    else:
        R.gtab[...] = R.small[...]
        for m in range(2):
            R.we0[m, rows(me, cw), :] = R.we[0, m]
            R.we1[m, rows(me, cw), :] = R.we[1, m]

    def near_x():
        def one(i):
            arrived(wblock(R.wx, 0, h, LANES), K.wa, 2 * nb + same_side(i))
            a_relay(2, same_side(i)).start()

        if inside:
            loop(nb // 2, one, 1)

    def send_e1():
        if inside:
            loop(nb, lambda i: e_copy(1, to_peer(i)).start(), 1)

    def finish_x():
        if inside:
            arrived(wblock(R.wx, pair, h, LANES), K.wa, 2 * nb + pair)
            loop(nb // 2, lambda i: arrived(wblock(R.wx, 0, h, LANES), K.wr, 2 * nb + far_side(i)), 1)
        loop(nb, lambda i: y_block(R.wx, to_peer(i), K.wy_x, LANES).start())

    def y_arrived(buf, name, width):
        loop(nb, lambda i: arrived(wblock(buf, 0, h, width), name, to_peer(i)))

    def y_sent(buf, name, width):
        loop(nb, lambda i: sent(wblock(buf, 0, h, width), name, to_peer(i)))

    near_x()
    y_arrived(R.wself.at[h], K.wy_self, LANES)

    R.acc[...] = jnp.zeros((32, D), F32)

    def tally(row, x):
        R.acc[pl.ds(row, 1), :] += jnp.sum(x, 0, keepdims=True)

    def gain(i):
        return R.gtab[pl.ds(i, 1), :]

    def shift(i):
        return R.gtab[pl.ds(5 + i, 1), :]

    def blk(j):
        return c + 2 * j

    def pblk(j):
        return cp + 2 * j

    def src_len(k):
        return R.slen[0, k]

    def tgt_len(k):
        return R.tlen[0, k]

    def self_len(k):
        return jnp.where(is_a, R.slen[0, k], R.tlen[0, k])

    docs = R.slen.shape[1]

    def set_bias(buf, q_start, q_len, k_len, causal, q_axis):
        shape = (B, L) if q_axis == 0 else (L, B)
        q_pos = lax.broadcasted_iota(jnp.int32, (B, 1) if q_axis == 0 else (1, B), q_axis) + q_start
        k_pos = lax.broadcasted_iota(jnp.int32, shape, 1 - q_axis)
        first = jnp.zeros(q_pos.shape, jnp.int32)
        last = jnp.zeros(q_pos.shape, jnp.int32) + k_len(0)
        edge = 0
        for k in range(docs):
            edge = edge + q_len(k)
            passed = q_pos >= edge
            first = first + jnp.where(passed, k_len(k), 0)
            if k + 1 < docs:
                last = last + jnp.where(passed, k_len(k + 1), 0)
        if causal is not None:
            last = jnp.minimum(last, q_pos + jnp.where(causal, 1, L))
        buf[...] = jnp.where((k_pos >= first) & (k_pos < last), 0.0, MASKED)

    lane_head = lax.div(lax.broadcasted_iota(jnp.int32, (1, KW), 1), HEAD_DIM)
    heads = KW // HEAD_DIM

    def attend(q_blk, k_ref, v_ref):
        lane = lax.broadcasted_iota(jnp.int32, (1, LANES), 1)
        out = jnp.zeros((B, KW), F32)
        lse = jnp.zeros((B, LANES), F32)
        for hd in range(heads):
            hrow = jnp.where(lane_head == hd, 1.0, 0.0)
            scores = mm_nt(q_blk * hrow.astype(BF16), k_ref[...]) + R.bias[...]
            top = jnp.max(scores, -1, keepdims=True)
            expos = jnp.exp(scores - top)
            total = jnp.sum(expos, -1, keepdims=True)
            out = out + mm(expos.astype(BF16), v_ref[...]) * (hrow / total)
            lse = lse + jnp.where(lane == hd, top + jnp.log(total), 0.0)
        return out.astype(BF16), jnp.transpose(lse)[0:8, :]

    scale = HEAD_DIM ** (-0.5)

    def row_sums(o_blk, do_blk):
        prod = do_blk.astype(F32) * o_blk.astype(F32)
        high = prod.astype(BF16)
        low = (prod - high.astype(F32)).astype(BF16)
        pick = lax.broadcasted_iota(jnp.int32, (16, KW), 0) == jnp.broadcast_to(lane_head, (16, KW))
        pick = jnp.where(pick, 1.0, 0.0).astype(BF16)
        return mm_nt(pick, high) + mm_nt(pick, low)

    half_head = lax.div(lax.broadcasted_iota(jnp.int32, (1, LANES), 1), HEAD_DIM)

    def back_half(t, count, block_of, first_pass, q_ref, o_ref, lse_ref, k_ref, v_ref, bias_of, hook=None):
        lt = lanes(t)
        R.dkf[...] = jnp.zeros((L, LANES), F32)
        R.dvf[...] = jnp.zeros((L, LANES), F32)

        def block(i):
            b = block_of(i)
            if hook is not None:
                hook(i)
            if first_pass is not None:
                do = first_pass(i, b)
                R.do[rows(b)] = do
                R.drowT[:, rows(b)] = row_sums(o_ref[rows(b)], do)
            bias_of(b)
            q_blk, do_blk = q_ref[rows(b), lt], R.do[rows(b), lt]
            pairs = range(LANES // HEAD_DIM)
            masks = [jnp.where(half_head == u, 1.0, 0.0) for u in pairs]
            lse = jnp.concatenate([lse_ref[pl.ds(2 * t + u, 1), rows(b)] for u in pairs], 1)
            inner = jnp.concatenate([R.drowT[pl.ds(2 * t + u, 1), rows(b)] for u in pairs], 1)
            bias = jnp.concatenate([R.biasT[...] for u in pairs], 1)
            qm = jnp.concatenate([q_blk * mask.astype(BF16) for mask in masks], 0)
            dom = jnp.concatenate([do_blk * mask.astype(BF16) for mask in masks], 0)
            probs = jnp.exp(mm_nt(k_ref[:, lt], qm) + bias - lse)
            change = (probs * (mm_nt(v_ref[:, lt], dom) - inner)).astype(BF16)
            R.dvf[...] += mm(probs.astype(BF16), dom)
            R.dkf[...] += mm(change, qm)
            dq = mm_tn(change, k_ref[:, lt])
            total = sum(dq[u * B:(u + 1) * B] * masks[u] for u in pairs)
            R.dq[rows(b), lt] = (total * scale).astype(BF16)

        loop(count, block)
        R.dkb[:, lt] = R.dkf[...].astype(BF16)
        R.dvb[:, lt] = R.dvf[...].astype(BF16)

    def half_grads(t, xq_ref, xk_ref, dq_ref, o_ref, b_ref, after=None):
        lt = lanes(t)

        def part(i):
            at, to = lanes(i, 2 * LANES), rows(i, 2 * LANES)
            R.gA[0, to, lt] = mm_tn(xq_ref[:, at], dq_ref[:, lt]).astype(BF16)
            R.gA[1, to, lt] = mm_tn(xk_ref[:, at], R.dkb[:, lt]).astype(BF16)
            R.gA[2, to, lt] = mm_tn(xk_ref[:, at], R.dvb[:, lt]).astype(BF16)
            R.gA[3, to, lt] = mm_tn(b_ref[:, at], o_ref[:, lt]).astype(BF16)
            if after is not None:
                after(i)

        loop(D // (2 * LANES), part)

    loop(2, lambda j: arrived(R.xrow.at[rows(pblk(j))], K.in_c, lax.rem(j + h, 2)))

    def self_project(i):
        x = R.xrow[rows(i)].astype(F32)
        y = norm(x, gain(2 * h), shift(2 * h)).astype(BF16)
        R.nrow[rows(i)] = y
        R.q[rows(i)] = mm(y, R.wself[h, 0]).astype(BF16) * jnp.asarray(scale, BF16)
        R.k[rows(i)] = mm(y, R.wself[h, 1]).astype(BF16)
        R.v[rows(i)] = mm(y, R.wself[h, 2]).astype(BF16)

    loop(4, self_project)

    def self_block(i):
        j = lax.rem(i, 2)
        b = jnp.where(i < 2, cp, c) + 2 * j
        set_bias(R.bias, b * B, self_len, self_len, is_b, 0)
        o, lse = attend(R.q[rows(b)], R.k, R.v)
        R.o[rows(b)] = o
        R.lseT[:, rows(b)] = lse
        y = mm_nt(o, R.wself[h, 3])

        @pl.when(i < 2)
        def _():
            R.cs[j] = y.astype(BF16)
            send(R.cs.at[j], R.cr.at[j], K.rs1, core, j).start()

        @pl.when(i >= 2)
        def _():
            R.part[j] = y

        @pl.when(i == 0)
        def _():
            if inside:
                loop(nb // 2, lambda i: e_copy(0, far_side(i)).start(), 1)
            finish_x()

    loop(4, self_block)

    def self_end(j):
        arrived(R.cr.at[j], K.rs1, j)
        branch = R.part[j] + R.cr[j].astype(F32)
        x = R.xrow[rows(blk(j))].astype(F32)
        y = x + branch
        R.mid[j] = y
        tally(16 + 2 * h, x * x)
        tally(21 + 2 * h, branch * branch)

        @pl.when(is_a)
        def _():
            R.n2row[rows(blk(j))] = norm(y, gain(1), shift(1)).astype(BF16)
            row_copy(R.n2row, blk(j), K.n2y, ypeer, j).start()
            row_copy(R.n2row, blk(j), K.n2, core, j).start()
            tally(17, y * y)

        @pl.when(is_b & (j == 0))
        def _():
            R.fs[...] = branch.astype(BF16)
            send(R.fs, R.fr, K.br3, ypeer).start()

    loop(2, self_end)

    if inside:
        loop(nb, lambda i: arrived(R.we0.at[:, rows(0, cw), :], K.we0, from_peer(i)), 1)
    send_e1()

    def enc_sum(j):
        arrived(R.cr.at[j], K.rs2, j)
        y = R.part[j] + R.cr[j].astype(F32)
        R.part[j] = y

        @pl.when(is_a)
        def _():
            R.ms[j] = (R.mid[j] + y).astype(BF16)

        @pl.when(is_b)
        def _():
            R.ms[j] = y.astype(BF16)

        send(R.ms.at[j], R.dmr.at[j], K.m_y, ypeer, j).start()

    def enc_block(i):
        j = lax.div(i, 2)
        own = lax.rem(i, 2) == 0
        b = jnp.where(own, c, cp) + 2 * j

        @pl.when(own & is_b)
        def _():
            arrived(R.n2row.at[rows(b)], K.n2y, j)
            row_copy(R.n2row, b, K.n2, core, j).start()

        @pl.when(jnp.logical_not(own))
        def _():
            arrived(R.n2row.at[rows(b)], K.n2, j)

        hid = mm(R.n2row[rows(b)], R.we0[0])
        act, slope = gelu_pair(hid)
        R.g0[rows(b)] = act.astype(BF16)
        R.gp0[rows(b)] = slope.astype(BF16)
        y = mm_nt(R.g0[rows(b)], R.we0[1])

        @pl.when(own)
        def _():
            R.part[j] = y

        @pl.when(jnp.logical_not(own))
        def _():
            sent(R.cs.at[j], K.rs1, j)
            R.cs[j] = y.astype(BF16)
            send(R.cs.at[j], R.cr.at[j], K.rs2, core, j).start()

        @pl.when(i == 2)
        def _():
            enc_sum(0)

    loop(4, enc_block)
    enc_sum(1)

    @pl.when(is_a)
    def _():
        arrived(R.fr, K.br3)
        R.t1[...] = R.tgt[...].astype(F32) + R.fr[...].astype(F32)

    @pl.when(is_b)
    def _():
        R.t1[...] = R.mid[1]

    one = R.t1[...]
    tally(19, one * one)
    R.n4c[rows(c)] = norm(one, gain(3), shift(3)).astype(BF16)
    row_copy(R.n4c, c, K.n4, core).start()
    y_arrived(R.wx, K.wy_x, LANES)

    arrived(R.n4c.at[rows(cp)], K.n4)
    row_copy(R.b5, s, K.b5, core, 0).start()
    row_copy(R.b5, s, K.b5, ypeer, 1).start()

    def cross_query(i):
        R.q2[rows(i)] = mm(R.n4c[rows(i)], R.wx[0]).astype(BF16) * jnp.asarray(scale, BF16)

    loop(2, cross_query)

    def memory_block(i):
        j = lax.rem(i, 2)
        b = jnp.where(i < 2, c, cp) + 2 * j

        @pl.when(i < 2)
        def _():
            arrived(R.dmr.at[j], K.m_y, j)
            branch = R.part[j] + R.dmr[j].astype(F32)

            @pl.when(is_a)
            def _():
                tally(22, branch * branch)
                R.mrow[rows(b)] = (R.mid[j] + branch).astype(BF16)

            @pl.when(is_b)
            def _():
                R.mrow[rows(b)] = branch.astype(BF16)

            row_copy(R.mrow, b, K.m_c, core, j).start()

        @pl.when(i >= 2)
        def _():
            arrived(R.mrow.at[rows(b)], K.m_c, j)

        y = R.mrow[rows(b)]
        R.k2[rows(b)] = mm(y, R.wx[1]).astype(BF16)
        R.v2[rows(b)] = mm(y, R.wx[2]).astype(BF16)

    loop(4, memory_block)

    def cross_block(i):
        b = jnp.where(i < 1, cp, c)
        set_bias(R.bias, (2 * h + b) * B, tgt_len, src_len, None, 0)
        o, lse = attend(R.q2[rows(b)], R.k2, R.v2)
        R.o2[rows(b)] = o
        R.lse2T[:, rows(b)] = lse
        y = mm_nt(o, R.wx[3])

        @pl.when(i < 1)
        def _():
            R.ds[...] = y.astype(BF16)
            send(R.ds, R.dr.at[0], K.rs4, core).start()

        @pl.when(i >= 1)
        def _():
            R.part[0] = y

    loop(2, cross_block)
    arrived(R.dr.at[0], K.rs4)
    branch4 = R.part[0] + R.dr[0].astype(F32)
    two = R.t1[...] + branch4
    R.t2[...] = two
    R.n5[rows(s)] = norm(two, gain(4), shift(4)).astype(BF16)
    row_copy(R.n5, s, K.n5, ypeer, 1).start()
    row_copy(R.n5, s, K.n5, core, 0).start()
    tally(24, branch4 * branch4)
    tally(20, two * two)

    if inside:
        loop(nb, lambda i: arrived(R.we1.at[:, rows(0, cw), :], K.we1, from_peer(i)), 1)
    arrived(R.b5.at[rows(sc)], K.b5, 0)
    arrived(R.b5.at[rows(sy)], K.b5, 1)
    row_copy(R.b5, sy, K.b5, core, 2).start()

    def around(m):
        return 2 * lax.rem(h + lax.div(m, 2), 2) + lax.rem(c + lax.rem(m, 2), 2)

    def dec_block(m):
        b = around(m)
        hid = mm(R.n5[rows(b)], R.we1[0])
        act, slope = gelu_pair(hid)
        R.g1[rows(b)] = act.astype(BF16)
        dact = mm(R.b5[rows(b)], R.we1[1])
        R.dh1[rows(b)] = (dact * slope).astype(BF16)
        return mm_nt(R.dh1[rows(b)], R.we1[0])

    def dec_step(i):
        m = jnp.where(i < 2, i, 5 - i)

        @pl.when(i == 1)
        def _():
            arrived(R.n5.at[rows(sc)], K.n5, 0)

        @pl.when(i == 2)
        def _():
            arrived(R.n5.at[rows(sy)], K.n5, 1)
            row_copy(R.n5, sy, K.n5, core, 2).start()
            arrived(R.n5.at[rows(around(3))], K.n5, 2)
            arrived(R.b5.at[rows(around(3))], K.b5, 2)

        y = dec_block(m)

        @pl.when(i == 0)
        def _():
            R.part[1] = y

        @pl.when((i == 1) | (i == 2))
        def _():
            R.es6[i - 1] = y.astype(BF16)
            send(R.es6.at[i - 1], R.er6.at[i - 1], K.rs6, core, i - 1).start()

        @pl.when(i == 3)
        def _():
            arrived(R.er6.at[1], K.rs6, 1)
            R.es6[2] = (y + R.er6[1].astype(F32)).astype(BF16)
            send(R.es6.at[2], R.er6.at[2], K.rs6, ypeer, 2).start()

    loop(4, dec_step)

    def dec_forward(i):
        m = 3 - i
        y = mm_nt(R.g1[rows(around(m))], R.we1[1])

        @pl.when(m == 0)
        def _():
            R.last[...] = y

        @pl.when((m == 1) | (m == 3))
        def _():
            at = lax.div(m, 2)
            R.es[at] = y.astype(BF16)
            send(R.es.at[at], R.er.at[at], K.rs5, core, at).start()

        @pl.when(m == 2)
        def _():
            arrived(R.er.at[1], K.rs5, 1)
            R.es[2] = (y + R.er[1].astype(F32)).astype(BF16)
            send(R.es.at[2], R.er.at[2], K.rs5, ypeer, 2).start()

    loop(4, dec_forward)

    def dp_x(a, p):
        at = rows(lax.div(p, 2), cw)
        return send(R.qA.at[a, :, rows(p, cw), :], R.pA.at[a, :, at, :], K.gd_x, (pair, s), a * nb + p)

    def dp_a(a, p):
        return send(
            R.qA.at[a, :, rows(p, cw), :], R.dpA.at[a, lax.div(me, 2)], K.gd_a, (p, s), a * nb + p, a * nb + me
        )

    def dp_e(l, p):
        return send(R.qE.at[l, :, rows(p, cw), :], R.dpE.at[l, me], K.gd_e, (p, s), l * nb + p, l * nb + me)

    def here(src, dst, i):
        return pltpu.make_async_copy(src, dst, R.ss.at[K.here + i])

    def here_a(a):
        return here(R.qA.at[a, :, rows(me, cw), :], R.dpA.at[a, lax.div(me, 2)], a)

    def here_e(l):
        return here(R.qE.at[l, :, rows(me, cw), :], R.dpE.at[l, me], 3 + l)

    def owners(piece, start):
        if inside:

            def one(i):
                p = piece * (nb // 2) + lax.rem(to_peer(i), nb // 2)

                @pl.when(p != me)
                def _():
                    start(p)

            loop(nb // 2, one)

    def dp_a_start(a, piece):
        if inside:

            def one(i):
                dp_x(a, piece * (nb // 2) + 2 * i + lax.rem(pair, 2)).start()

            loop(nb // 4, one)

    def dp_a_pass(a, piece):
        if inside:

            def one(i):
                p = piece * (nb // 2) + 2 * i + lax.rem(me, 2)
                at = rows(lax.div(p, 2), cw)
                arrived(R.pA.at[a, :, at, :], K.gd_x, a * nb + p)
                for m in range(4):
                    total = R.qA[a, m, rows(p, cw)].astype(F32) + R.pA[a, m, at].astype(F32)
                    R.qA[a, m, rows(p, cw)] = total.astype(BF16)

                @pl.when(p != me)
                def _():
                    dp_a(a, p).start()

            loop(nb // 4, one)

    def dp_e_start(l, piece):
        owners(piece, lambda p: dp_e(l, p).start())

    def keep_a(a):
        if inside:
            here_a(a).start()

    def keep_e(l):
        if inside:
            here_e(l).start()

    half_d = 2 * LANES

    def dec_grads(i):
        at, to = lanes(i, 2 * LANES), rows(i, 2 * LANES)
        R.qE[1, 0, to] = mm_tn(R.n5[:, at], R.dh1[...]).astype(BF16)
        R.qE[1, 1, to] = mm_tn(R.b5[:, at], R.g1[...]).astype(BF16)
        dp_e_start(1, i)

    loop(D // (2 * LANES), dec_grads)
    keep_e(1)

    def add_norm(i, dgain, dbias):
        R.acc[pl.ds(i, 1), :] += dgain
        R.acc[pl.ds(5 + i, 1), :] += dbias

    arrived(R.er6.at[0], K.rs6, 0)
    arrived(R.er6.at[2], K.rs6, 2)
    up = R.part[1] + R.er6[0].astype(F32) + R.er6[2].astype(F32)
    back, dgain, dbias = norm_back(R.t2[...], gain(4), up)
    g4 = R.cot[...].astype(F32) + back
    R.g4[...] = g4
    R.b4c[rows(c)] = g4.astype(BF16)
    row_copy(R.b4c, c, K.b4, core).start()
    add_norm(4, dgain, dbias)


    arrived(R.b4c.at[rows(cp)], K.b4)

    def cross_first(i, b):
        return mm(R.b4c[rows(b)], R.wx[3]).astype(BF16)

    def cross_bias(b):
        set_bias(R.biasT, (2 * h + b) * B, tgt_len, src_len, None, 1)

    for t in range(2):
        back_half(
            t, 2, lambda i: i, cross_first if t == 0 else None, R.q2, R.o2, R.lse2T, R.k2, R.v2, cross_bias
        )

    def memory_sum(j):
        arrived(R.cr.at[j], K.rs7m, j)
        y = R.dmem[j] + R.cr[j].astype(F32)
        R.dmem[j] = y
        sent(R.ms.at[j], K.m_y, j)
        R.ms[j] = y.astype(BF16)
        send(R.ms.at[j], R.dmr.at[j], K.dm, ypeer, j).start()

    def memory_back(i):
        j = lax.div(i, 2)
        first = lax.rem(i, 2) == 0
        b = jnp.where(first, cp, c) + 2 * j
        y = mm_nt(R.dkb[rows(b)], R.wx[1]) + mm_nt(R.dvb[rows(b)], R.wx[2])

        @pl.when(first)
        def _():
            sent(R.cs.at[j], K.rs2, j)
            R.cs[j] = y.astype(BF16)
            send(R.cs.at[j], R.cr.at[j], K.rs7m, core, j).start()

        @pl.when(jnp.logical_not(first))
        def _():
            R.dmem[j] = y

        @pl.when(i == 2)
        def _():
            memory_sum(0)

    loop(4, memory_back)

    def cross_dx(i):
        b = jnp.where(i < 1, cp, c)
        y = mm_nt(R.dq[rows(b)], R.wx[0])

        @pl.when(i < 1)
        def _():
            sent(R.ds, K.rs4)
            R.ds[...] = y.astype(BF16)
            send(R.ds, R.dr.at[1], K.rs7q, core).start()

        @pl.when(i >= 1)
        def _():
            R.part[0] = y

    loop(2, cross_dx)

    memory_sum(1)

    arrived(R.dr.at[1], K.rs7q)
    back, dgain, dbias = norm_back(R.t1[...], gain(3), R.part[0] + R.dr[1].astype(F32))
    g3 = R.g4[...] + back
    R.g3[...] = g3

    add_norm(3, dgain, dbias)

    arrived(R.er.at[0], K.rs5, 0)
    arrived(R.er.at[2], K.rs5, 2)
    branch5 = R.last[...] + R.er[0].astype(F32) + R.er[2].astype(F32)
    tally(25, branch5 * branch5)
    R.dec[...] = R.t2[...] + branch5

    def cross_grads(t):
        half_grads(t, R.n4c, R.mrow, R.dq.at[0:2 * B], R.o2, R.b4c)

    def y_grad_x():
        return send(R.gA.at[:, :, lanes(1 - h)], R.ylX, K.gy_x, ypeer)

    def y_grad_s(i):
        at = rows(i, half_d)
        return send(R.gA.at[:, at, lanes(1 - h)], R.qA.at[h, :, at, :], K.gy_s, ypeer, i)

    cross_grads(1 - h)
    cross_grads(h)

    def join_x():
        arrived(R.ylX, K.gy_x)
        for m in range(4):
            total = R.gA[m, :, lanes(h)].astype(F32) + R.ylX[m].astype(F32)
            R.qA[2, m] = total.astype(BF16)
        for piece in range(2):
            dp_a_start(2, piece)

    def pass_a(a):
        for piece in range(2):
            dp_a_pass(a, piece)
        keep_a(a)

    if inside:

        def chosen_sent(i):
            for l in range(2):
                sent(wblock(R.gE, 0, l, FQ), (K.we0, K.we1)[l], to_peer(i))

        loop(nb, chosen_sent, 1)

    @pl.when(is_a)
    def _():
        R.fs[...] = R.g3[...].astype(BF16)

    def enc_back_sum(j):
        arrived(R.cr.at[j], K.rs8, j)
        y = R.part[j] + R.cr[j].astype(F32)
        R.part[j] = y

        @pl.when(is_b)
        def _():
            sent(R.ms.at[j], K.dm, j)
            R.ms[j] = y.astype(BF16)
            send(R.ms.at[j], R.dxr.at[j], K.dx, ypeer, j).start()

    def enc_back(i):
        j = lax.div(i, 2)
        own = lax.rem(i, 2) == 0
        b = jnp.where(own, c, cp) + 2 * j

        @pl.when(own)
        def _():
            arrived(R.dmr.at[j], K.dm, j)
            x = R.dmem[j] + R.dmr[j].astype(F32)
            R.dmem[j] = x
            R.be[rows(b)] = x.astype(BF16)
            row_copy(R.be, b, K.be, core, j).start()

        @pl.when(jnp.logical_not(own))
        def _():
            arrived(R.be.at[rows(b)], K.be, j)

        dact = mm(R.be[rows(b)], R.we0[1])
        R.gp0[rows(b)] = (dact * R.gp0[rows(b)].astype(F32)).astype(BF16)
        y = mm_nt(R.gp0[rows(b)], R.we0[0])

        @pl.when(own)
        def _():
            R.part[j] = y

        @pl.when(jnp.logical_not(own))
        def _():
            sent(R.cs.at[j], K.rs7m, j)
            R.cs[j] = y.astype(BF16)
            send(R.cs.at[j], R.cr.at[j], K.rs8, core, j).start()

        @pl.when(i == 2)
        def _():
            enc_back_sum(0)

        @pl.when((i == 2) & is_a)
        def _():
            send(R.fs, R.brow.at[rows(c)], K.g3, ypeer).start()

    loop(4, enc_back)
    enc_back_sum(1)

    @pl.when(is_a)
    def _():
        y_grad_x().start()

    def enc_grads(i):
        at, to = lanes(i, 2 * LANES), rows(i, 2 * LANES)
        R.qE[0, 0, to] = mm_tn(R.n2row[:, at], R.gp0[...]).astype(BF16)
        R.qE[0, 1, to] = mm_tn(R.be[:, at], R.g0[...]).astype(BF16)
        dp_e_start(0, i)

    loop(D // (2 * LANES), enc_grads)
    keep_e(0)

    def enc_end(j):
        arrived(R.dxr.at[j], K.dx, j)
        up = R.part[j] + R.dxr[j].astype(F32)
        back, dgain, dbias = norm_back(R.mid[j], gain(1), up)
        add_norm(1, dgain, dbias)
        g = R.dmem[j] + back
        R.dmem[j] = g
        R.brow[rows(blk(j))] = g.astype(BF16)
        row_copy(R.brow, blk(j), K.brow, core, j).start()

    @pl.when(is_b)
    def _():
        R.brow[rows(blk(1))] = R.g3[...].astype(BF16)
        arrived(R.brow.at[rows(blk(0))], K.g3)
        for j in range(2):
            row_copy(R.brow, blk(j), K.brow, core, j).start()

    def self_block_of(i):
        return jnp.where(lax.rem(i, 2) == 0, c, cp) + 2 * lax.div(i, 2)

    def self_first(i, b):
        j = lax.div(i, 2)

        @pl.when(is_a & (lax.rem(i, 2) == 0))
        def _():
            enc_end(j)

        @pl.when(lax.rem(i, 2) == 1)
        def _():
            arrived(R.brow.at[rows(b)], K.brow, j)

        return mm(R.brow[rows(b)], R.wself[h, 3]).astype(BF16)

    def self_bias(b):
        set_bias(R.biasT, b * B, self_len, self_len, is_b, 1)

    def self_half(t, first_pass, hook=None):
        back_half(t, 4, self_block_of, first_pass, R.q, R.o, R.lseT, R.k, R.v, self_bias, hook)

    @pl.when(is_b)
    def _():
        for j in range(2):
            sent(R.ms.at[j], K.dx, j)
        y_grad_x().start()

    self_half(1 - h, self_first)

    y_grad_x().wait_send()

    half_grads(1 - h, R.nrow, R.nrow, R.dq, R.o, R.brow, lambda i: y_grad_s(i).start())

    def second_hook(i):
        @pl.when(i == 2)
        def _():
            join_x()

    self_half(h, None, second_hook)

    def own_piece(i):
        at = rows(i, half_d)
        for m in range(4):
            R.qA[h, m, at] = R.gA[m, at, lanes(h)]
        dp_a_start(h, i)

    half_grads(h, R.nrow, R.nrow, R.dq, R.o, R.brow, own_piece)

    def other_pieces():
        for piece in range(2):
            at = rows(piece, half_d)
            arrived(R.qA.at[1 - h, :, at, :], K.gy_s, piece)
            dp_a_start(1 - h, piece)

    def self_dx(i):
        j = lax.rem(i, 2)
        b = jnp.where(i < 2, cp, c) + 2 * j
        y = mm_nt(R.dq[rows(b)], R.wself[h, 0])
        y = y + mm_nt(R.dkb[rows(b)], R.wself[h, 1])
        y = y + mm_nt(R.dvb[rows(b)], R.wself[h, 2])

        @pl.when(i < 2)
        def _():
            sent(R.cs.at[j], K.rs8, j)
            R.cs[j] = y.astype(BF16)
            send(R.cs.at[j], R.cr.at[j], K.rs9, core, j).start()

        @pl.when(i >= 2)
        def _():
            R.part[j] = y

    loop(4, self_dx)
    pass_a(2)

    def self_final(i):
        j = jnp.where(is_a, 1 - i, i)
        arrived(R.cr.at[j], K.rs9, j)
        x = R.xrow[rows(blk(j))].astype(F32)
        back, dgain, dbias = norm_back(x, gain(2 * h), R.part[j] + R.cr[j].astype(F32))
        add_norm(2 * h, dgain, dbias)

        @pl.when(is_a & (j == 0))
        def _():
            R.sgrad[...] = R.dmem[0] + back

        @pl.when(is_a & (j == 1))
        def _():
            sent(R.fs, K.g3)
            R.fs[...] = (R.dmem[1] + back).astype(BF16)

        @pl.when(is_b & (j == 0))
        def _():
            sent(R.fs, K.br3)
            R.fs[...] = back.astype(BF16)

        @pl.when(is_b & (j == 1))
        def _():
            R.tgrad[...] = R.g3[...] + back

    loop(2, self_final)

    send(R.acc, R.accc, K.accc, core).start()

    other_pieces()
    arrived(R.accc, K.accc)
    R.acc1[...] = R.acc[...] + R.accc[...]
    send(R.acc1, R.accy, K.accy, ypeer).start()
    send(R.fs, R.fr, K.fin, ypeer).start()
    pass_a(h)
    arrived(R.accy, K.accy)
    R.acc2[...] = R.acc1[...] + R.accy[...]
    R.stats[...] = R.acc2[16:32, :]

    if inside:

        def tile_of(p):
            return lanes(lax.div(p * cw, LANES))

        def acc_copy(p):
            return send(R.acc2.at[0:16, tile_of(p)], R.accd.at[me], K.accd, (p, s), p, me)

        loop(nb, lambda i: acc_copy(to_peer(i)).start(), 1)
        R.picks[...] = R.smallr[...]

    pass_a(1 - h)
    arrived(R.fr, K.fin)

    @pl.when(is_a)
    def _():
        R.tgrad[...] = R.g3[...] + R.fr[...].astype(F32)

    @pl.when(is_b)
    def _():
        R.sgrad[...] = R.fr[...].astype(F32)

    if inside:
        loop(nb, lambda i: arrived(R.accd.at[0], K.accd, from_peer(i)), 1)
        R.ggb[...] = R.acc2[0:16, tile_of(me)]

        def more(i):
            R.ggb[...] += R.accd[from_peer(i)]

        loop(nb, more, 1)
        for l in range(2):
            loop(nb, lambda i, l=l: arrived(R.dpE.at[l, 0], K.gd_e, l * nb + from_peer(i)), 1)
            here_e(l).wait()
        for a in range(3):
            loop(nb // 2, lambda i, a=a: arrived(R.dpA.at[a, 0], K.gd_a, a * nb + same_side(i)), 1)
            here_a(a).wait()
    else:
        R.gacc[...] = R.acc2[0:16, :]

    for name in (K.in_y, K.n4, K.b4, K.rs7q, K.fin):
        sent(R.oth, name)
    for name in (K.in_c, K.m_c, K.brow, K.rs9, K.n2, K.be):
        for j in range(2):
            sent(R.oth, name, j)
    for name in (K.b5, K.n5, K.rs5, K.rs6):
        for j in range(3):
            sent(R.oth, name, j)
    y_sent(other, K.wy_self, LANES)
    y_sent(R.wx, K.wy_x, LANES)
    for piece in range(2):
        y_grad_s(piece).wait_send()
    sent(R.acc, K.accc)
    sent(R.acc1, K.accy)

    @pl.when(is_a)
    def _():
        for name in (K.n2y, K.dm):
            for j in range(2):
                sent(R.oth, name, j)

    if inside:

        def drain_side(i):
            for a in range(3):
                sent(R.sendA.at[0], K.wa, a * nb + same_side(i))
                sent(R.sendA.at[0], K.wr, a * nb + same_side(i))
                sent(R.sendA.at[0], K.gd_a, a * nb + same_side(i))
                sent(R.sendA.at[0], K.gd_x, a * nb + far_side(i))

        for a in range(3):
            sent(R.sendA.at[0], K.wa, a * nb + pair)
            sent(R.sendA.at[0], K.gd_x, a * nb + pair)
        loop(nb // 2, drain_side, 1)

        def drain(i):
            p = to_peer(i)
            sent(R.small, K.small, p)
            for l in range(2):
                sent(R.qE.at[l, :, rows(0, cw), :], K.gd_e, l * nb + p)
            sent(R.accd.at[0], K.accd, p)

        loop(nb, drain, 1)


def close_kernel(cfg, names, *refs):
    nb, cw, B, D, FQ, E, _ = cfg
    R = SimpleNamespace(**dict(zip(names, refs, strict=True)))
    dp = lax.axis_index("dp")

    def copy(src, dst, i):
        return pltpu.make_async_copy(src, dst, R.sem.at[i])

    plain = [(R.dec, R.o_dec), (R.sgrad, R.o_sgrad), (R.tgrad, R.o_tgrad)]
    for i, (src, _) in enumerate(plain):
        copy(src, R.vp.at[i], i).start()
    for l in range(2):
        copy(R.dpE.at[l], R.ve.at[l], 3 + l).start()
    for a in range(3):
        copy(R.dpA.at[a], R.va.at[a], 5 + a).start()

    stats = jnp.sum(R.stats[...], -1, keepdims=True) * (1.0 / (4 * B * D))
    root = jnp.broadcast_to(jnp.sqrt(stats), (16, LANES))
    place = lax.broadcasted_iota(jnp.int32, (16, LANES), 0) - lax.broadcasted_iota(jnp.int32, (16, LANES), 1)
    for k in range(2):
        line = jnp.sum(jnp.where(place == 5 * k, root, 0.0), 0, keepdims=True)
        R.o_rms[0, k:k + 1, :] = line[:, 0:5]
    for k in range(LANES // cw):

        @pl.when(lax.rem(dp, LANES // cw) == k)
        def _(k=k):
            R.o_gain[...] = R.ggb[0:5, k * cw:(k + 1) * cw]
            R.o_bias[...] = R.ggb[5:10, k * cw:(k + 1) * cw]

    for i, (src, dst) in enumerate(plain):
        copy(src, R.vp.at[i], i).wait()
        copy(R.vp.at[i], dst, i).start()
    for l in range(2):
        copy(R.dpE.at[l], R.ve.at[l], 3 + l).wait()
        R.w_up[l] = jnp.zeros((E, cw, FQ), F32)
        R.w_dn[l] = jnp.zeros((E, cw, FQ), F32)
        for p in range(nb):
            e = jnp.max(R.picks[p, 10 + l:11 + l, :]).astype(jnp.int32)
            R.w_up[l, pl.ds(e, 1)] += R.ve[l, p, 0].astype(F32)[None]
            R.w_dn[l, pl.ds(e, 1)] += R.ve[l, p, 1].astype(F32)[None]
        copy(R.w_up.at[l], R.o_up.at[l], 8 + l).start()
        copy(R.w_dn.at[l], R.o_dn.at[l], 10 + l).start()
    for a in range(3):
        copy(R.dpA.at[a], R.va.at[a], 5 + a).wait()
        for m in range(4):
            total = R.va[a, 0, m].astype(F32)
            for p in range(1, nb // 2):
                total = total + R.va[a, p, m].astype(F32)
            if m < 3:
                R.w_qkv[a, m] = total
            else:
                R.w_out[a] = total
    copy(R.w_qkv, R.o_qkv, 12).start()
    copy(R.w_out, R.o_out, 13).start()
    for i, (_, dst) in enumerate(plain):
        copy(R.vp.at[i], dst, i).wait()
    for l in range(2):
        copy(R.w_up.at[l], R.o_up.at[l], 8 + l).wait()
        copy(R.w_dn.at[l], R.o_dn.at[l], 10 + l).wait()
    copy(R.w_qkv, R.o_qkv, 12).wait()
    copy(R.w_out, R.o_out, 13).wait()


def on_device(
    src_input,
    tgt_input,
    out_cotangent,
    src_lengths,
    tgt_lengths,
    enc_expert,
    dec_expert,
    norm_gains,
    norm_biases,
    qkv_weight,
    out_weight,
    expert_up,
    expert_down,
):
    n = lax.axis_size("dp")
    B, D = src_input.shape[1:]
    cw = norm_gains.shape[1]
    FQ = expert_up.shape[3]
    E = expert_up.shape[1]
    inside = cw % 16 == 0 and LANES % cw == 0 and n % 4 == 0 and n & (n - 1) == 0
    wot = jnp.swapaxes(out_weight, 1, 2)
    dnt = jnp.swapaxes(expert_down, 2, 3)
    vmem = pl.BlockSpec(memory_space=pltpu.VMEM)
    smem = pl.BlockSpec(memory_space=pltpu.SMEM)
    anywhere = pl.BlockSpec(memory_space=pl.ANY)

    def f32(*shape):
        return jax.ShapeDtypeStruct(shape, F32)

    def bf16(*shape):
        return jax.ShapeDtypeStruct(shape, BF16)

    scalars = dict(slen=src_lengths, tlen=tgt_lengths)
    operands = dict(src=src_input[0], tgt=tgt_input[0], cot=out_cotangent[0])
    results = dict(dec=f32(B, D), sgrad=f32(B, D), tgrad=f32(B, D), stats=f32(16, D))
    far = {}
    if inside:
        nb, rowsize = n, cw
        scalars.update(epick=enc_expert, dpick=dec_expert)
        operands.update(gains=norm_gains, biases=norm_biases, qkv=qkv_weight, wot=wot, up=expert_up, dnt=dnt)
        results.update(ggb=f32(16, LANES), picks=f32(n, 16, LANES))
        far = dict(dpA=bf16(3, n // 2, 4, cw, LANES), dpE=bf16(2, n, 2, cw, FQ))
    else:
        nb, rowsize = 1, D
        gb = jnp.concatenate([norm_gains, norm_biases], 0).astype(F32)
        small = lax.all_gather(gb, "dp", axis=1, tiled=True)
        small = jnp.concatenate([small, jnp.zeros((6, D), F32)], 0)
        wa = jnp.concatenate([qkv_weight, wot[:, None]], 1)
        wa = lax.all_gather(wa, "dp", axis=2, tiled=True)
        picks = jnp.stack([enc_expert[0, 0], dec_expert[0, 0]])
        we = jnp.stack([expert_up, dnt], 2)
        we = lax.all_gather(we, "dp", axis=3, tiled=True)
        we = jnp.stack([jnp.take(we[l], picks[l], axis=0) for l in range(2)])
        operands.update(small=small, wa=wa, we=we)
        results.update(qA=bf16(3, 4, D, LANES), qE=bf16(2, 2, D, FQ), gacc=f32(16, D))
    cfg = (nb, rowsize, B, D, FQ, E, inside)
    scratch = scratch_list(nb, rowsize, B, D, FQ, inside)
    count = sem_list(nb)[1]
    scratch.update(ss=pltpu.SemaphoreType.DMA((count,)), rs=pltpu.SemaphoreType.DMA((count,)))
    names = tuple(scalars) + tuple(operands) + tuple(results) + tuple(far) + tuple(scratch)
    outs = pl.pallas_call(
        functools.partial(step_kernel, cfg, names),
        name="step",
        out_shape=tuple(results.values()) + tuple(far.values()),
        in_specs=[smem] * len(scalars) + [vmem] * len(operands),
        out_specs=[vmem] * len(results) + [anywhere] * len(far),
        scratch_shapes=list(scratch.values()),
        compiler_params=pltpu.CompilerParams(
            collective_id=1, has_side_effects=True, vmem_limit_bytes=63 << 20
        ),
        cost_estimate=pl.CostEstimate(flops=17 << 30, bytes_accessed=8 << 20, transcendentals=16 << 20),
    )(*scalars.values(), *operands.values())
    made = dict(zip(tuple(results) + tuple(far), outs, strict=True))
    if inside:
        near = dict(stats=vmem, ggb=vmem, picks=vmem, dec=anywhere, sgrad=anywhere, tgrad=anywhere)
        near.update(dpA=anywhere, dpE=anywhere)
        last = dict(
            o_dec=f32(B, D),
            o_sgrad=f32(B, D),
            o_tgrad=f32(B, D),
            o_gain=f32(5, cw),
            o_bias=f32(5, cw),
            o_qkv=f32(3, 3, cw, LANES),
            o_out=f32(3, cw, LANES),
            o_up=f32(2, E, cw, FQ),
            o_dn=f32(2, E, cw, FQ),
            o_rms=f32(1, 2, 5),
        )
        held = dict(
            vp=pltpu.VMEM((3, B, D), F32),
            ve=pltpu.VMEM((2, n, 2, cw, FQ), BF16),
            va=pltpu.VMEM((3, n // 2, 4, cw, LANES), BF16),
            w_up=pltpu.VMEM((2, E, cw, FQ), F32),
            w_dn=pltpu.VMEM((2, E, cw, FQ), F32),
            w_qkv=pltpu.VMEM((3, 3, cw, LANES), F32),
            w_out=pltpu.VMEM((3, cw, LANES), F32),
            sem=pltpu.SemaphoreType.DMA((14,)),
        )
        small_outs = [k in (3, 4, 9) for k in range(len(last))]
        dec, sgrad, tgrad, gains, biases, gqkv, gout, gup, gdn, rms = pl.pallas_call(
            functools.partial(close_kernel, cfg, tuple(near) + tuple(last) + tuple(held)),
            name="close",
            out_shape=tuple(last.values()),
            in_specs=list(near.values()),
            out_specs=[vmem if near_by else anywhere for near_by in small_outs],
            scratch_shapes=list(held.values()),
            compiler_params=pltpu.CompilerParams(vmem_limit_bytes=63 << 20),
            cost_estimate=pl.CostEstimate(flops=16 << 20, bytes_accessed=10 << 20, transcendentals=0),
        )(*[made[name] for name in near])
    else:
        dec, sgrad, tgrad, stats, ga, ge, gacc = outs

        def total(x, axis):
            return lax.psum_scatter(x, "dp", scatter_dimension=axis, tiled=True)

        gains, biases = total(gacc[0:5], 1), total(gacc[5:10], 1)
        ga = total(ga.astype(F32), 2)
        gqkv, gout = ga[:, :3], ga[:, 3]
        match = (picks[:, None] == jnp.arange(E, dtype=jnp.int32)[None]).astype(F32)
        ge = ge.astype(F32)[:, None] * match[:, :, None, None, None]
        ge = total(ge, 3)
        gup, gdn = ge[:, :, 0], ge[:, :, 1]
        length = B * lax.axis_size("seq")
        rms = jnp.sqrt(jnp.sum(stats[:10], 1) / (length * D)).reshape(1, 2, 5)
    return (
        dec[None],
        sgrad[None],
        tgrad[None],
        gains,
        biases,
        gqkv,
        jnp.swapaxes(gout, 1, 2),
        gup,
        jnp.swapaxes(gdn, 2, 3),
        rms,
    )


def solution(mesh):
    placed = (
        P("dp", "seq", None),
        P("dp", "seq", None),
        P("dp", "seq", None),
        P("dp", None),
        P("dp", None),
        P("dp", None),
        P("dp", None),
        P(None, "dp"),
        P(None, "dp"),
        P(None, None, "dp", "seq"),
        P(None, "seq", "dp"),
        P(None, None, "dp", "seq"),
        P(None, None, "seq", "dp"),
    )
    return jax.shard_map(
        on_device,
        mesh=mesh,
        in_specs=placed,
        out_specs=(
            P("dp", "seq", None),
            P("dp", "seq", None),
            P("dp", "seq", None),
            P(None, "dp"),
            P(None, "dp"),
            P(None, None, "dp", "seq"),
            P(None, "seq", "dp"),
            P(None, None, "dp", "seq"),
            P(None, None, "seq", "dp"),
            P("dp", None, None),
        ),
        check_vma=False,
    )
```

```python
import functools
import math
from types import SimpleNamespace

import jax
import jax.numpy as jnp
from jax import lax
from jax.experimental import pallas as pl
from jax.experimental.pallas import tpu as pltpu
from jax.sharding import PartitionSpec as P

HEAD_DIM = 64
EPSILON = 1e-05
MASKED = -1e30
LANES = 128
F32 = jnp.float32
BF16 = jnp.bfloat16
MESH = pl.DeviceIdType.MESH
GELU_A = math.sqrt(2.0 / math.pi)
GELU_B = 0.044715


def mm(a, b):
    return lax.dot_general(a, b, (((1,), (0,)), ((), ())), preferred_element_type=F32)


def mm_nt(a, b):
    return lax.dot_general(a, b, (((1,), (1,)), ((), ())), preferred_element_type=F32)


def mm_tn(a, b):
    return lax.dot_general(a, b, (((0,), (0,)), ((), ())), preferred_element_type=F32)


def centre(x):
    mean = jnp.mean(x, -1, keepdims=True)
    xc = x - mean
    var = jnp.mean(xc * xc, -1, keepdims=True)
    scale = lax.rsqrt(var + EPSILON)
    return xc * scale, scale


def norm(x, gain, shift):
    return centre(x)[0] * gain + shift


def norm_back(x, gain, up):
    xh, scale = centre(x)
    dgain = jnp.sum(up * xh, 0, keepdims=True)
    dbias = jnp.sum(up, 0, keepdims=True)
    dxh = up * gain
    m1 = jnp.mean(dxh, -1, keepdims=True)
    m2 = jnp.mean(dxh * xh, -1, keepdims=True)
    return scale * (dxh - m1 - xh * m2), dgain, dbias


def gelu_pair(x):
    square = x * x
    t = jnp.tanh(x * (GELU_A + (GELU_A * GELU_B) * square))
    half = 0.5 + 0.5 * t
    slope = half + (0.5 * x) * (1.0 - t * t) * (GELU_A + (3.0 * GELU_A * GELU_B) * square)
    return x * half, slope


def scratch_list(nb, cw, B, D, FQ, inside):
    L, F2, KW = 4 * B, 2 * FQ, 2 * LANES

    def b(*shape):
        return pltpu.VMEM(shape, BF16)

    def f(*shape):
        return pltpu.VMEM(shape, F32)

    out = dict(
        xrow=b(L, D),
        oth=b(B, D),
        nrow=b(L, D),
        wself=b(2, 4, D, KW),
        wx=b(4, D, KW),
        we0=b(2, D, FQ),
        we1=b(2, D, FQ),
        gtab=f(16, D),
        q=b(L, KW),
        k=b(L, KW),
        v=b(L, KW),
        o=b(L, KW),
        do=b(L, KW),
        lseT=f(8, L),
        drowT=f(16, L),
        bias=f(B, L),
        biasT=f(L, B),
        part=f(2, B, D),
        cs=b(2, B, D),
        cr=b(2, B, D),
        mid=f(2, B, D),
        n2row=b(L, D),
        g0=b(L, FQ),
        gp0=b(L, FQ),
        ms=b(2, B, D),
        dxr=b(2, B, D),
        mrow=b(L, D),
        fs=b(B, D),
        fr=b(B, D),
        t1=f(B, D),
        n4c=b(2 * B, D),
        q2=b(2 * B, KW),
        k2=b(L, KW),
        v2=b(L, KW),
        o2=b(2 * B, KW),
        lse2T=f(8, 2 * B),
        ds=b(B, D),
        dr=b(2, B, D),
        t2=f(B, D),
        n5=b(L, D),
        b5=b(L, D),
        g1=b(L, FQ),
        dh1=b(L, FQ),
        es=b(3, B, D),
        er=b(3, B, D),
        es6=b(3, B, D),
        er6=b(3, B, D),
        g4=f(B, D),
        last=f(B, D),
        b4c=b(2 * B, D),
        dkf=f(L, LANES),
        dvf=f(L, LANES),
        dkb=b(L, KW),
        dvb=b(L, KW),
        dmr=b(2, B, D),
        g3=f(B, D),
        brow=b(L, D),
        dmem=f(2, B, D),
        be=b(L, D),
        dq=b(L, KW),
        gA=b(4, D, KW),
        gX=b(4, D, KW),
        ylX=b(4, D, LANES),
        acc=f(32, D),
        acc1=f(32, D),
        acc2=f(32, D),
        accc=f(32, D),
        accy=f(32, D),
        dec=f(B, D),
        sgrad=f(B, D),
        tgrad=f(B, D),
        stats=f(16, D),
        ggb=f(16, LANES),
    )
    if inside:
        out.update(
            small=f(16, LANES),
            smallr=f(nb, 16, LANES),
            sendA=b(3, 4, cw, LANES),
            gE=b(2, D, F2),
            qA=b(3, 4, D, LANES),
            pA=b(3, 4, D // 2, LANES),
            qE=b(2, 2, D, FQ),
            accd=f(nb, 16, LANES),
        )
    return out


def sem_list(nb):
    counts = dict(
        in_y=1,
        in_c=2,
        b5=3,
        small=1,
        wa=3 * (nb // 2),
        wr=3 * (nb // 2),
        we0=1,
        we1=1,
        wy_self=1,
        wy_x=1,
        rs1=2,
        n2=2,
        rs2=2,
        br3=1,
        m_y=2,
        m_c=2,
        n4=1,
        rs4=1,
        n5=3,
        rs5=3,
        rs6=3,
        b4=1,
        rs7q=1,
        rs7m=2,
        dm=2,
        g3=1,
        brow=2,
        be=2,
        rs8=2,
        rs9=2,
        fin=1,
        gy_s=2,
        gy_x=1,
        dx=2,
        n2y=2,
        gd_a=3,
        gd_x=6,
        gd_e=2,
        accc=1,
        accy=1,
        accd=1,
        here=5,
        put=6,
    )
    base, at = {}, 0
    for name, number in counts.items():
        base[name] = at
        at = at + number
    return SimpleNamespace(**base), at


def step_kernel(cfg, names, *refs):
    nb, cw, B, D, FQ, E, inside = cfg
    L, F2, KW = 4 * B, 2 * FQ, 2 * LANES
    R = SimpleNamespace(**dict(zip(names, refs, strict=True)))
    K, _ = sem_list(nb)

    dp = lax.axis_index("dp")
    me = dp if inside else 0
    s = lax.axis_index("seq")
    h = lax.div(s, 2)
    c = lax.rem(s, 2)
    cp = 1 - c
    sc = s + 1 - 2 * c
    sy = s + 2 - 4 * h
    core, ypeer = (dp, sc), (dp, sy)
    is_a, is_b = h == 0, h == 1

    def rows(i, size=B):
        return pl.ds(pl.multiple_of(i * size, size), size)

    def lanes(i, size=LANES):
        return pl.ds(pl.multiple_of(i * size, size), size)

    def send(src, dst, name, to, i=0, j=None):
        return pltpu.make_async_remote_copy(
            src_ref=src,
            dst_ref=dst,
            send_sem=R.ss.at[name + i],
            recv_sem=R.rs.at[name + (i if j is None else j)],
            device_id=to,
            device_id_type=MESH,
        )

    def arrived(dst, name, i=0):
        send(dst, dst, name, core, i).wait_recv()

    def sent(src, name, i=0):
        send(src, src, name, core, i).wait_send()

    def loop(count, body, start=0):
        def step(i, carry):
            body(i)
            return carry

        lax.fori_loop(start, count, step, 0)

    def flip(a, m):
        out, bit = a, 1
        while bit < nb:
            out = out + bit * lax.rem(lax.div(m, bit), 2) * (1 - 2 * lax.rem(lax.div(a, bit), 2))
            bit = 2 * bit
        return out

    def to_peer(i):
        return flip(me, i)

    from_peer = to_peer
    pair = me + 1 - 2 * lax.rem(me, 2)

    barrier = pltpu.get_barrier_semaphore()
    for to in (core, ypeer):
        pl.semaphore_signal(barrier, inc=1, device_id=to, device_id_type=MESH)

    def greet(i):
        pl.semaphore_signal(barrier, inc=1, device_id=(to_peer(i), s), device_id_type=MESH)

    loop(nb, greet, 1)

    if inside:
        R.small[...] = jnp.zeros((16, LANES), F32)
        for k in range(LANES // cw):

            @pl.when(lax.rem(dp, LANES // cw) == k)
            def _(k=k):
                R.small[0:5, k * cw:(k + 1) * cw] = R.gains[...].astype(F32)
                R.small[5:10, k * cw:(k + 1) * cw] = R.biases[...].astype(F32)

        R.small[10:11, :] = jnp.broadcast_to(R.epick[0, 0].astype(F32), (1, LANES))
        R.small[11:12, :] = jnp.broadcast_to(R.dpick[0, 0].astype(F32), (1, LANES))

    @pl.when(is_a)
    def _():
        R.xrow[rows(s)] = R.src[...]
        R.oth[...] = R.tgt[...]

    @pl.when(is_b)
    def _():
        R.xrow[rows(s)] = R.tgt[...]
        R.oth[...] = R.src[...]

    R.b5[rows(s)] = R.cot[...]
    for a in range(3):
        if inside:
            for j in range(3):
                R.sendA[a, j] = R.qkv[a, j]
            R.sendA[a, 3] = R.wot[a]
        buf = R.wself.at[a] if a < 2 else R.wx
        piece = R.sendA if inside else R.wa
        for j in range(4):
            buf[j, rows(me, cw), lanes(h)] = piece[a, j]
    pl.semaphore_wait(barrier, nb + 1)

    def small_copy(p):
        return send(R.small, R.smallr.at[me], K.small, (p, s))

    def wblock(buf, p, half, width):
        return buf.at[:, rows(p, cw), lanes(half, width)]

    def held(a):
        return R.wself.at[a] if a < 2 else R.wx

    def a_copy(a, i):
        p = jnp.where(i == 0, pair, same_side(i))
        return send(R.sendA.at[a], wblock(held(a), me, h, LANES), K.wa, (p, s), a * (nb // 2) + i)

    def a_relay(a, i):
        at = wblock(held(a), same_side(i), h, LANES)
        return send(at, at, K.wr, (pair, s), a * (nb // 2) + i)

    def y_block(buf, p, name, width):
        at = wblock(buf, p, h, width)
        return send(at, at, name, ypeer)

    def same_side(i):
        return flip(me, 2 * i)

    def far_side(i):
        return flip(pair, 2 * i)

    def e_copy(l, p):
        at = (R.we0, R.we1)[l].at[:, rows(me, cw), :]
        return send(wblock(R.gE, p, l, FQ), at, (K.we0, K.we1)[l], (p, s))

    def row_copy(buf, block, name, to, i=0):
        at = buf.at[rows(block)]
        return send(at, at, name, to, i)

    if inside:
        loop(nb, lambda i: small_copy(to_peer(i)).start(), 1)
    send(R.oth, R.xrow.at[rows(s)], K.in_y, ypeer).start()
    row_copy(R.xrow, s, K.in_c, core, 0).start()
    if inside:

        def spread_self(i):
            for a in range(2):
                a_copy(a, i).start()

        loop(nb // 2, spread_self, 1)
        for a in range(2):
            a_copy(a, 0).start()
    other = R.wself.at[1 - h]
    y_block(other, me, K.wy_self, LANES).start()

    if inside:
        arrived(R.smallr.at[pl.ds(0, nb - 1)], K.small)
        R.smallr[pl.ds(me, 1)] = R.small[...][None]
        per = LANES // cw
        for t in range(D // LANES):
            tile = R.smallr[t * per]
            for k in range(1, per):
                tile = tile + R.smallr[t * per + k]
            R.gtab[:, t * LANES:(t + 1) * LANES] = tile

        def chosen(l, p):
            row = R.smallr[p, pl.ds(10 + l, 1), :]
            for m, shard in enumerate((R.up, R.dnt)):
                total = None
                for e in range(E):
                    hit = jnp.where(row == float(e), 1.0, 0.0)
                    hit = jnp.concatenate([hit] * (FQ // LANES), axis=1)
                    term = shard[l, e].astype(F32) * hit
                    total = term if total is None else total + term
                R.gE[m, rows(p, cw), lanes(l, FQ)] = total.astype(BF16)

        loop(nb, lambda p: chosen(0, p))
        loop(nb // 2, lambda i: a_copy(2, i).start(), 1)
        a_copy(2, 0).start()
        for m in range(2):
            R.we0[m, rows(me, cw), :] = R.gE[m, rows(me, cw), lanes(0, FQ)]

    arrived(R.xrow.at[rows(sy)], K.in_y)
    row_copy(R.xrow, sy, K.in_c, core, 1).start()

    def gain(i):
        return R.gtab[pl.ds(i, 1), :]

    def shift(i):
        return R.gtab[pl.ds(5 + i, 1), :]

    def blk(j):
        return c + 2 * j

    def pblk(j):
        return cp + 2 * j

    def self_norms():
        loop(2, lambda j: arrived(R.xrow.at[rows(pblk(j))], K.in_c, lax.rem(j + h, 2)))

        def one(i):
            x = R.xrow[rows(i)].astype(F32)
            R.nrow[rows(i)] = norm(x, gain(2 * h), shift(2 * h)).astype(BF16)

        loop(4, one)

    if inside:

        def near(i):
            p = same_side(i)
            for a in range(2):
                arrived(wblock(held(a), p, h, LANES), K.wa, a * (nb // 2) + i)
                a_relay(a, i).start()
            y_block(other, p, K.wy_self, LANES).start()

        def far(i):
            p = far_side(i)
            for a in range(2):
                arrived(wblock(held(a), p, h, LANES), K.wr, a * (nb // 2) + i)
            y_block(other, p, K.wy_self, LANES).start()

        for a in range(2):
            arrived(wblock(held(a), pair, h, LANES), K.wa, a * (nb // 2))
        y_block(other, pair, K.wy_self, LANES).start()
        loop(nb // 2, near, 1)
        e_copy(0, pair).start()
        loop(nb // 2, lambda i: e_copy(0, same_side(i)).start(), 1)
        self_norms()
        loop(nb // 2, far, 1)
        loop(nb, lambda p: chosen(1, p))
        for m in range(2):
            R.we1[m, rows(me, cw), :] = R.gE[m, rows(me, cw), lanes(1, FQ)]
    else:
        R.gtab[...] = R.small[...]
        self_norms()
        for m in range(2):
            R.we0[m, rows(me, cw), :] = R.we[0, m]
            R.we1[m, rows(me, cw), :] = R.we[1, m]

    def near_x():
        def one(i):
            arrived(wblock(R.wx, 0, h, LANES), K.wa, 2 * (nb // 2) + i)
            a_relay(2, i).start()

        if inside:
            loop(nb // 2, one, 1)

    def send_e1():
        if inside:
            loop(nb, lambda i: e_copy(1, to_peer(i)).start(), 1)

    def finish_x():
        if inside:
            arrived(wblock(R.wx, pair, h, LANES), K.wa, 2 * (nb // 2))
            loop(nb // 2, lambda i: arrived(wblock(R.wx, 0, h, LANES), K.wr, 2 * (nb // 2) + i), 1)
        loop(nb, lambda i: y_block(R.wx, to_peer(i), K.wy_x, LANES).start())

    def y_arrived(buf, name, width):
        arrived(buf.at[:, :, lanes(1 - h, width)], name)

    def y_sent(buf, name, width):
        sent(buf.at[:, :, lanes(h, width)], name)

    near_x()
    y_arrived(R.wself.at[h], K.wy_self, LANES)

    R.acc[...] = jnp.zeros((32, D), F32)

    def tally(row, x):
        R.acc[pl.ds(row, 1), :] += jnp.sum(x, 0, keepdims=True)

    def src_len(k):
        return R.slen[0, k]

    def tgt_len(k):
        return R.tlen[0, k]

    def self_len(k):
        return jnp.where(is_a, R.slen[0, k], R.tlen[0, k])

    docs = R.slen.shape[1]

    def set_bias(buf, q_start, q_len, k_len, causal, q_axis):
        shape = (B, L) if q_axis == 0 else (L, B)
        q_pos = lax.broadcasted_iota(jnp.int32, (B, 1) if q_axis == 0 else (1, B), q_axis) + q_start
        k_pos = lax.broadcasted_iota(jnp.int32, shape, 1 - q_axis)
        first = jnp.zeros(q_pos.shape, jnp.int32)
        last = jnp.zeros(q_pos.shape, jnp.int32) + k_len(0)
        edge = 0
        for k in range(docs):
            edge = edge + q_len(k)
            passed = q_pos >= edge
            first = first + jnp.where(passed, k_len(k), 0)
            if k + 1 < docs:
                last = last + jnp.where(passed, k_len(k + 1), 0)
        if causal is not None:
            last = jnp.minimum(last, q_pos + jnp.where(causal, 1, L))
        buf[...] = jnp.where((k_pos >= first) & (k_pos < last), 0.0, MASKED)

    lane_head = lax.div(lax.broadcasted_iota(jnp.int32, (1, KW), 1), HEAD_DIM)
    heads = KW // HEAD_DIM

    def attend(q_blk, k_ref, v_ref):
        lane = lax.broadcasted_iota(jnp.int32, (1, LANES), 1)
        out = jnp.zeros((B, KW), F32)
        lse = jnp.zeros((B, LANES), F32)
        for hd in range(heads):
            hrow = jnp.where(lane_head == hd, 1.0, 0.0)
            scores = mm_nt(q_blk * hrow.astype(BF16), k_ref[...]) + R.bias[...]
            top = jnp.max(scores, -1, keepdims=True)
            expos = jnp.exp(scores - top)
            total = jnp.sum(expos, -1, keepdims=True)
            out = out + mm(expos.astype(BF16), v_ref[...]) * (hrow / total)
            lse = lse + jnp.where(lane == hd, top + jnp.log(total), 0.0)
        return out.astype(BF16), jnp.transpose(lse)[0:8, :]

    scale = HEAD_DIM ** (-0.5)

    def row_sums(o_blk, do_blk):
        prod = do_blk.astype(F32) * o_blk.astype(F32)
        high = prod.astype(BF16)
        low = (prod - high.astype(F32)).astype(BF16)
        pick = lax.broadcasted_iota(jnp.int32, (16, KW), 0) == jnp.broadcast_to(lane_head, (16, KW))
        pick = jnp.where(pick, 1.0, 0.0).astype(BF16)
        return mm_nt(pick, high) + mm_nt(pick, low)

    half_head = lax.div(lax.broadcasted_iota(jnp.int32, (1, LANES), 1), HEAD_DIM)

    def back_half(t, count, block_of, first_pass, q_ref, o_ref, lse_ref, k_ref, v_ref, bias_of, hook=None):
        lt = lanes(t)
        R.dkf[...] = jnp.zeros((L, LANES), F32)
        R.dvf[...] = jnp.zeros((L, LANES), F32)

        def block(i):
            b = block_of(i)
            if hook is not None:
                hook(i)
            if first_pass is not None:
                do = first_pass(i, b)
                R.do[rows(b)] = do
                R.drowT[:, rows(b)] = row_sums(o_ref[rows(b)], do)
            bias_of(b)
            q_blk, do_blk = q_ref[rows(b), lt], R.do[rows(b), lt]
            pairs = range(LANES // HEAD_DIM)
            masks = [jnp.where(half_head == u, 1.0, 0.0) for u in pairs]
            lse = jnp.concatenate([lse_ref[pl.ds(2 * t + u, 1), rows(b)] for u in pairs], 1)
            inner = jnp.concatenate([R.drowT[pl.ds(2 * t + u, 1), rows(b)] for u in pairs], 1)
            bias = jnp.concatenate([R.biasT[...] for u in pairs], 1)
            qm = jnp.concatenate([q_blk * mask.astype(BF16) for mask in masks], 0)
            dom = jnp.concatenate([do_blk * mask.astype(BF16) for mask in masks], 0)
            probs = jnp.exp(mm_nt(k_ref[:, lt], qm) + bias - lse)
            change = (probs * (mm_nt(v_ref[:, lt], dom) - inner)).astype(BF16)
            R.dvf[...] += mm(probs.astype(BF16), dom)
            R.dkf[...] += mm(change, qm)
            dq = mm_tn(change, k_ref[:, lt])
            total = sum(dq[u * B:(u + 1) * B] * masks[u] for u in pairs)
            R.dq[rows(b), lt] = (total * scale).astype(BF16)

        loop(count, block)
        R.dkb[:, lt] = R.dkf[...].astype(BF16)
        R.dvb[:, lt] = R.dvf[...].astype(BF16)

    def half_grads(to_ref, t, xq_ref, xk_ref, dq_ref, o_ref, b_ref, after=None):
        lt = lanes(t)

        def part(i):
            at, to = lanes(i, 2 * LANES), rows(i, 2 * LANES)
            to_ref[0, to, lt] = mm_tn(xq_ref[:, at], dq_ref[:, lt]).astype(BF16)
            to_ref[1, to, lt] = mm_tn(xk_ref[:, at], R.dkb[:, lt]).astype(BF16)
            to_ref[2, to, lt] = mm_tn(xk_ref[:, at], R.dvb[:, lt]).astype(BF16)
            to_ref[3, to, lt] = mm_tn(b_ref[:, at], o_ref[:, lt]).astype(BF16)
            if after is not None:
                after(i)

        loop(D // (2 * LANES), part)

    def self_project(i):
        y = R.nrow[rows(i)]
        R.q[rows(i)] = mm(y, R.wself[h, 0]).astype(BF16) * jnp.asarray(scale, BF16)
        R.k[rows(i)] = mm(y, R.wself[h, 1]).astype(BF16)
        R.v[rows(i)] = mm(y, R.wself[h, 2]).astype(BF16)

    if inside:
        loop(nb // 2, lambda i: e_copy(0, far_side(i)).start(), 1)
    loop(4, self_project)

    def self_block(i):
        j = lax.rem(i, 2)
        b = jnp.where(i < 2, cp, c) + 2 * j
        set_bias(R.bias, b * B, self_len, self_len, is_b, 0)
        o, lse = attend(R.q[rows(b)], R.k, R.v)
        R.o[rows(b)] = o
        R.lseT[:, rows(b)] = lse
        y = mm_nt(o, R.wself[h, 3])

        @pl.when(i < 2)
        def _():
            R.cs[j] = y.astype(BF16)
            send(R.cs.at[j], R.cr.at[j], K.rs1, core, j).start()

        @pl.when(i >= 2)
        def _():
            R.part[j] = y

        @pl.when(i == 0)
        def _():
            finish_x()

    loop(4, self_block)

    def self_end(j):
        arrived(R.cr.at[j], K.rs1, j)
        branch = R.part[j] + R.cr[j].astype(F32)
        x = R.xrow[rows(blk(j))].astype(F32)
        y = x + branch
        R.mid[j] = y
        tally(16 + 2 * h, x * x)
        tally(21 + 2 * h, branch * branch)

        @pl.when(is_a)
        def _():
            R.n2row[rows(blk(j))] = norm(y, gain(1), shift(1)).astype(BF16)
            row_copy(R.n2row, blk(j), K.n2y, ypeer, j).start()
            row_copy(R.n2row, blk(j), K.n2, core, j).start()
            tally(17, y * y)

        @pl.when(is_b & (j == 0))
        def _():
            R.fs[...] = branch.astype(BF16)
            send(R.fs, R.fr, K.br3, ypeer).start()

    loop(2, self_end)

    if inside:
        arrived(R.we0.at[:, pl.ds(0, (nb - 1) * cw), :], K.we0)
    send_e1()

    def enc_sum(j):
        arrived(R.cr.at[j], K.rs2, j)
        y = R.part[j] + R.cr[j].astype(F32)
        R.part[j] = y

        @pl.when(is_a)
        def _():
            sent(R.n2row.at[rows(blk(j))], K.n2y, j)
            R.ms[j] = (R.mid[j] + y).astype(BF16)

        @pl.when(is_b)
        def _():
            R.ms[j] = y.astype(BF16)

        send(R.ms.at[j], R.dmr.at[j], K.m_y, ypeer, j).start()

    def enc_block(i):
        j = lax.div(i, 2)
        own = lax.rem(i, 2) == 0
        b = jnp.where(own, c, cp) + 2 * j

        @pl.when(own & is_b)
        def _():
            arrived(R.n2row.at[rows(b)], K.n2y, j)
            row_copy(R.n2row, b, K.n2, core, j).start()

        @pl.when(jnp.logical_not(own))
        def _():
            arrived(R.n2row.at[rows(b)], K.n2, j)

        hid = mm(R.n2row[rows(b)], R.we0[0])
        act, slope = gelu_pair(hid)
        R.g0[rows(b)] = act.astype(BF16)
        R.gp0[rows(b)] = slope.astype(BF16)
        y = mm_nt(R.g0[rows(b)], R.we0[1])

        @pl.when(own)
        def _():
            R.part[j] = y

        @pl.when(jnp.logical_not(own))
        def _():
            sent(R.cs.at[j], K.rs1, j)
            R.cs[j] = y.astype(BF16)
            send(R.cs.at[j], R.cr.at[j], K.rs2, core, j).start()

        @pl.when(i == 2)
        def _():
            enc_sum(0)

    loop(4, enc_block)
    enc_sum(1)

    @pl.when(is_a)
    def _():
        arrived(R.fr, K.br3)
        R.t1[...] = R.tgt[...].astype(F32) + R.fr[...].astype(F32)

    @pl.when(is_b)
    def _():
        R.t1[...] = R.mid[1]

    one = R.t1[...]
    tally(19, one * one)
    R.n4c[rows(c)] = norm(one, gain(3), shift(3)).astype(BF16)
    row_copy(R.n4c, c, K.n4, core).start()
    y_arrived(R.wx, K.wy_x, LANES)

    arrived(R.n4c.at[rows(cp)], K.n4)
    row_copy(R.b5, s, K.b5, core, 0).start()
    row_copy(R.b5, s, K.b5, ypeer, 1).start()

    def cross_query(i):
        R.q2[rows(i)] = mm(R.n4c[rows(i)], R.wx[0]).astype(BF16) * jnp.asarray(scale, BF16)

    loop(2, cross_query)

    def memory_block(i):
        j = lax.rem(i, 2)
        b = jnp.where(i < 2, c, cp) + 2 * j

        @pl.when(i < 2)
        def _():
            arrived(R.dmr.at[j], K.m_y, j)
            branch = R.part[j] + R.dmr[j].astype(F32)

            @pl.when(is_a)
            def _():
                tally(22, branch * branch)
                R.mrow[rows(b)] = (R.mid[j] + branch).astype(BF16)

            @pl.when(is_b)
            def _():
                R.mrow[rows(b)] = branch.astype(BF16)

            row_copy(R.mrow, b, K.m_c, core, j).start()

        @pl.when(i >= 2)
        def _():
            arrived(R.mrow.at[rows(b)], K.m_c, j)

        y = R.mrow[rows(b)]
        R.k2[rows(b)] = mm(y, R.wx[1]).astype(BF16)
        R.v2[rows(b)] = mm(y, R.wx[2]).astype(BF16)

    loop(4, memory_block)

    def cross_block(i):
        b = jnp.where(i < 1, cp, c)
        set_bias(R.bias, (2 * h + b) * B, tgt_len, src_len, None, 0)
        o, lse = attend(R.q2[rows(b)], R.k2, R.v2)
        R.o2[rows(b)] = o
        R.lse2T[:, rows(b)] = lse
        y = mm_nt(o, R.wx[3])

        @pl.when(i < 1)
        def _():
            R.ds[...] = y.astype(BF16)
            send(R.ds, R.dr.at[0], K.rs4, core).start()

        @pl.when(i >= 1)
        def _():
            R.part[0] = y

    loop(2, cross_block)
    arrived(R.dr.at[0], K.rs4)
    branch4 = R.part[0] + R.dr[0].astype(F32)
    two = R.t1[...] + branch4
    R.t2[...] = two
    R.n5[rows(s)] = norm(two, gain(4), shift(4)).astype(BF16)
    row_copy(R.n5, s, K.n5, ypeer, 1).start()
    row_copy(R.n5, s, K.n5, core, 0).start()
    tally(24, branch4 * branch4)
    tally(20, two * two)

    if inside:
        arrived(R.we1.at[:, pl.ds(0, (nb - 1) * cw), :], K.we1)
    arrived(R.b5.at[rows(sc)], K.b5, 0)
    arrived(R.b5.at[rows(sy)], K.b5, 1)
    row_copy(R.b5, sy, K.b5, core, 2).start()

    def around(m):
        return 2 * lax.rem(h + lax.div(m, 2), 2) + lax.rem(c + lax.rem(m, 2), 2)

    def dec_block(m):
        b = around(m)
        hid = mm(R.n5[rows(b)], R.we1[0])
        act, slope = gelu_pair(hid)
        R.g1[rows(b)] = act.astype(BF16)
        dact = mm(R.b5[rows(b)], R.we1[1])
        R.dh1[rows(b)] = (dact * slope).astype(BF16)
        return mm_nt(R.dh1[rows(b)], R.we1[0])

    def dec_step(i):
        m = jnp.where(i < 2, i, 5 - i)

        @pl.when(i == 1)
        def _():
            arrived(R.n5.at[rows(sc)], K.n5, 0)

        @pl.when(i == 2)
        def _():
            arrived(R.n5.at[rows(sy)], K.n5, 1)
            row_copy(R.n5, sy, K.n5, core, 2).start()
            arrived(R.n5.at[rows(around(3))], K.n5, 2)
            arrived(R.b5.at[rows(around(3))], K.b5, 2)

        y = dec_block(m)

        @pl.when(i == 0)
        def _():
            R.part[1] = y

        @pl.when((i == 1) | (i == 2))
        def _():
            R.es6[i - 1] = y.astype(BF16)
            send(R.es6.at[i - 1], R.er6.at[i - 1], K.rs6, core, i - 1).start()

        @pl.when(i == 3)
        def _():
            arrived(R.er6.at[1], K.rs6, 1)
            R.es6[2] = (y + R.er6[1].astype(F32)).astype(BF16)
            send(R.es6.at[2], R.er6.at[2], K.rs6, ypeer, 2).start()

    loop(4, dec_step)

    def dec_forward(i):
        m = 3 - i
        y = mm_nt(R.g1[rows(around(m))], R.we1[1])

        @pl.when(m == 0)
        def _():
            R.last[...] = y

        @pl.when((m == 1) | (m == 3))
        def _():
            at = lax.div(m, 2)
            R.es[at] = y.astype(BF16)
            send(R.es.at[at], R.er.at[at], K.rs5, core, at).start()

        @pl.when(m == 2)
        def _():
            arrived(R.er.at[1], K.rs5, 1)
            R.es[2] = (y + R.er[1].astype(F32)).astype(BF16)
            send(R.es.at[2], R.er.at[2], K.rs5, ypeer, 2).start()

    loop(4, dec_forward)

    def dp_x(a, p):
        at = rows(lax.div(p, 2), cw)
        return send(R.qA.at[a, :, rows(p, cw), :], R.pA.at[a, :, at, :], K.gd_x, (pair, s), 2 * a + lax.div(p, nb // 2))

    def dp_a(a, p):
        return send(
            R.qA.at[a, :, rows(p, cw), :], R.dpA.at[a, lax.div(me, 2)], K.gd_a, (p, s), a
        )

    def dp_e(l, p):
        return send(R.qE.at[l, :, rows(p, cw), :], R.dpE.at[l, me], K.gd_e, (p, s), l)

    def here(src, dst, i):
        return pltpu.make_async_copy(src, dst, R.ss.at[K.here + i])

    def put_dec():
        return here(R.dec, R.z_dec, 5)

    def put_sgrad():
        return here(R.sgrad, R.z_sgrad, 6)

    def put_tgrad():
        return here(R.tgrad, R.z_tgrad, 7)

    def put_stats():
        return here(R.stats, R.z_stats, 8)

    def put_ggb():
        return here(R.ggb, R.z_ggb, 9)

    def put_picks():
        return here(R.smallr, R.z_picks, 10)

    def here_a(a):
        return here(R.qA.at[a, :, rows(me, cw), :], R.dpA.at[a, lax.div(me, 2)], a)

    def here_e(l):
        return here(R.qE.at[l, :, rows(me, cw), :], R.dpE.at[l, me], 3 + l)

    def owners(piece, start):
        if inside:

            def one(i):
                p = piece * (nb // 2) + lax.rem(to_peer(i), nb // 2)

                @pl.when(p != me)
                def _():
                    start(p)

            loop(nb // 2, one)

    def dp_a_start(a, piece):
        if inside:

            def one(i):
                dp_x(a, piece * (nb // 2) + 2 * i + lax.rem(pair, 2)).start()

            loop(nb // 4, one)

    def x_part(a, piece):
        return R.pA.at[a, :, rows(piece, nb // 4 * cw), :]

    def dp_a_pass(a, piece):
        if inside:
            arrived(x_part(a, piece), K.gd_x, 2 * a + piece)

            def one(i):
                p = piece * (nb // 2) + 2 * i + lax.rem(me, 2)
                at = rows(lax.div(p, 2), cw)
                for m in range(4):
                    total = R.qA[a, m, rows(p, cw)].astype(F32) + R.pA[a, m, at].astype(F32)
                    R.qA[a, m, rows(p, cw)] = total.astype(BF16)

                @pl.when(p != me)
                def _():
                    dp_a(a, p).start()

            loop(nb // 4, one)

    def dp_e_start(l, piece):
        owners(piece, lambda p: dp_e(l, p).start())

    def keep_a(a):
        if inside:
            here_a(a).start()

    def keep_e(l):
        if inside:
            here_e(l).start()

    half_d = 2 * LANES

    def dec_grads(i):
        at, to = lanes(i, 2 * LANES), rows(i, 2 * LANES)
        R.qE[1, 0, to] = mm_tn(R.n5[:, at], R.dh1[...]).astype(BF16)
        R.qE[1, 1, to] = mm_tn(R.b5[:, at], R.g1[...]).astype(BF16)
        dp_e_start(1, i)

    loop(D // (2 * LANES), dec_grads)
    keep_e(1)

    def add_norm(i, dgain, dbias):
        R.acc[pl.ds(i, 1), :] += dgain
        R.acc[pl.ds(5 + i, 1), :] += dbias

    arrived(R.er6.at[0], K.rs6, 0)
    arrived(R.er6.at[2], K.rs6, 2)
    up = R.part[1] + R.er6[0].astype(F32) + R.er6[2].astype(F32)
    back, dgain, dbias = norm_back(R.t2[...], gain(4), up)
    g4 = R.cot[...].astype(F32) + back
    R.g4[...] = g4
    R.b4c[rows(c)] = g4.astype(BF16)
    row_copy(R.b4c, c, K.b4, core).start()
    add_norm(4, dgain, dbias)


    arrived(R.b4c.at[rows(cp)], K.b4)

    def cross_first(i, b):
        return mm(R.b4c[rows(b)], R.wx[3]).astype(BF16)

    def cross_bias(b):
        set_bias(R.biasT, (2 * h + b) * B, tgt_len, src_len, None, 1)

    for t in range(2):
        back_half(
            t, 2, lambda i: i, cross_first if t == 0 else None, R.q2, R.o2, R.lse2T, R.k2, R.v2, cross_bias
        )

    def memory_sum(j):
        arrived(R.cr.at[j], K.rs7m, j)
        y = R.dmem[j] + R.cr[j].astype(F32)
        R.dmem[j] = y
        sent(R.ms.at[j], K.m_y, j)
        R.ms[j] = y.astype(BF16)
        send(R.ms.at[j], R.dmr.at[j], K.dm, ypeer, j).start()

    def memory_back(i):
        j = lax.div(i, 2)
        first = lax.rem(i, 2) == 0
        b = jnp.where(first, cp, c) + 2 * j
        y = mm_nt(R.dkb[rows(b)], R.wx[1]) + mm_nt(R.dvb[rows(b)], R.wx[2])

        @pl.when(first)
        def _():
            sent(R.cs.at[j], K.rs2, j)
            R.cs[j] = y.astype(BF16)
            send(R.cs.at[j], R.cr.at[j], K.rs7m, core, j).start()

        @pl.when(jnp.logical_not(first))
        def _():
            R.dmem[j] = y

        @pl.when(i == 2)
        def _():
            memory_sum(0)

    loop(4, memory_back)

    def cross_dx(i):
        b = jnp.where(i < 1, cp, c)
        y = mm_nt(R.dq[rows(b)], R.wx[0])

        @pl.when(i < 1)
        def _():
            sent(R.ds, K.rs4)
            R.ds[...] = y.astype(BF16)
            send(R.ds, R.dr.at[1], K.rs7q, core).start()

        @pl.when(i >= 1)
        def _():
            R.part[0] = y

    loop(2, cross_dx)

    memory_sum(1)

    arrived(R.dr.at[1], K.rs7q)
    back, dgain, dbias = norm_back(R.t1[...], gain(3), R.part[0] + R.dr[1].astype(F32))
    g3 = R.g4[...] + back
    R.g3[...] = g3

    add_norm(3, dgain, dbias)

    arrived(R.er.at[0], K.rs5, 0)
    arrived(R.er.at[2], K.rs5, 2)
    branch5 = R.last[...] + R.er[0].astype(F32) + R.er[2].astype(F32)
    tally(25, branch5 * branch5)
    R.dec[...] = R.t2[...] + branch5
    put_dec().start()
    if inside:
        put_picks().start()

    def cross_grads(t):
        half_grads(R.gX, t, R.n4c, R.mrow, R.dq.at[0:2 * B], R.o2, R.b4c)

    def y_grad_x():
        return send(R.gX.at[:, :, lanes(1 - h)], R.ylX, K.gy_x, ypeer)

    def y_grad_s(i):
        at = rows(i, half_d)
        return send(R.gA.at[:, at, lanes(1 - h)], R.qA.at[h, :, at, :], K.gy_s, ypeer, i)

    cross_grads(1 - h)
    cross_grads(h)

    def join_x():
        arrived(R.ylX, K.gy_x)
        for m in range(4):
            total = R.gX[m, :, lanes(h)].astype(F32) + R.ylX[m].astype(F32)
            R.qA[2, m] = total.astype(BF16)
        for piece in range(2):
            dp_a_start(2, piece)

    def pass_a(a):
        for piece in range(2):
            dp_a_pass(a, piece)
        keep_a(a)

    if inside:

        for l in range(2):
            sent((R.we0, R.we1)[l].at[:, pl.ds(0, (nb - 1) * cw), :], (K.we0, K.we1)[l])

    @pl.when(is_a)
    def _():
        R.fs[...] = R.g3[...].astype(BF16)

    def enc_back_sum(j):
        arrived(R.cr.at[j], K.rs8, j)
        y = R.part[j] + R.cr[j].astype(F32)
        R.part[j] = y

        @pl.when(is_b)
        def _():
            sent(R.ms.at[j], K.dm, j)
            R.ms[j] = y.astype(BF16)
            send(R.ms.at[j], R.dxr.at[j], K.dx, ypeer, j).start()

    def enc_back(i):
        j = lax.div(i, 2)
        own = lax.rem(i, 2) == 0
        b = jnp.where(own, c, cp) + 2 * j

        @pl.when(own)
        def _():
            arrived(R.dmr.at[j], K.dm, j)
            x = R.dmem[j] + R.dmr[j].astype(F32)
            R.dmem[j] = x
            R.be[rows(b)] = x.astype(BF16)
            row_copy(R.be, b, K.be, core, j).start()

        @pl.when(jnp.logical_not(own))
        def _():
            arrived(R.be.at[rows(b)], K.be, j)

        dact = mm(R.be[rows(b)], R.we0[1])
        R.gp0[rows(b)] = (dact * R.gp0[rows(b)].astype(F32)).astype(BF16)
        y = mm_nt(R.gp0[rows(b)], R.we0[0])

        @pl.when(own)
        def _():
            R.part[j] = y

        @pl.when(jnp.logical_not(own))
        def _():
            sent(R.cs.at[j], K.rs7m, j)
            R.cs[j] = y.astype(BF16)
            send(R.cs.at[j], R.cr.at[j], K.rs8, core, j).start()

        @pl.when(i == 2)
        def _():
            enc_back_sum(0)

        @pl.when((i == 2) & is_a)
        def _():
            send(R.fs, R.brow.at[rows(c)], K.g3, ypeer).start()

    loop(4, enc_back)
    enc_back_sum(1)

    @pl.when(is_a)
    def _():
        y_grad_x().start()

    def enc_grads(i):
        at, to = lanes(i, 2 * LANES), rows(i, 2 * LANES)
        R.qE[0, 0, to] = mm_tn(R.n2row[:, at], R.gp0[...]).astype(BF16)
        R.qE[0, 1, to] = mm_tn(R.be[:, at], R.g0[...]).astype(BF16)
        dp_e_start(0, i)

    loop(D // (2 * LANES), enc_grads)
    keep_e(0)

    def enc_end(j):
        arrived(R.dxr.at[j], K.dx, j)
        up = R.part[j] + R.dxr[j].astype(F32)
        back, dgain, dbias = norm_back(R.mid[j], gain(1), up)
        add_norm(1, dgain, dbias)
        g = R.dmem[j] + back
        R.dmem[j] = g
        R.brow[rows(blk(j))] = g.astype(BF16)
        row_copy(R.brow, blk(j), K.brow, core, j).start()

    @pl.when(is_b)
    def _():
        R.brow[rows(blk(1))] = R.g3[...].astype(BF16)
        arrived(R.brow.at[rows(blk(0))], K.g3)
        for j in range(2):
            row_copy(R.brow, blk(j), K.brow, core, j).start()

    def self_block_of(i):
        return jnp.where(lax.rem(i, 2) == 0, c, cp) + 2 * lax.div(i, 2)

    def self_first(i, b):
        j = lax.div(i, 2)

        @pl.when(is_a & (lax.rem(i, 2) == 0))
        def _():
            enc_end(j)

        @pl.when(lax.rem(i, 2) == 1)
        def _():
            arrived(R.brow.at[rows(b)], K.brow, j)

        return mm(R.brow[rows(b)], R.wself[h, 3]).astype(BF16)

    def self_bias(b):
        set_bias(R.biasT, b * B, self_len, self_len, is_b, 1)

    def self_half(t, first_pass, hook=None):
        back_half(t, 4, self_block_of, first_pass, R.q, R.o, R.lseT, R.k, R.v, self_bias, hook)

    @pl.when(is_b)
    def _():
        for j in range(2):
            sent(R.ms.at[j], K.dx, j)
        y_grad_x().start()

    self_half(1 - h, self_first)


    half_grads(R.gA, 1 - h, R.nrow, R.nrow, R.dq, R.o, R.brow, lambda i: y_grad_s(i).start())

    def second_hook(i):
        @pl.when(i == 3)
        def _():
            join_x()

    self_half(h, None, second_hook)

    def own_piece(i):
        at = rows(i, half_d)
        for m in range(4):
            R.qA[h, m, at] = R.gA[m, at, lanes(h)]
        dp_a_start(h, i)

    half_grads(R.gA, h, R.nrow, R.nrow, R.dq, R.o, R.brow, own_piece)

    def other_pieces():
        for piece in range(2):
            at = rows(piece, half_d)
            arrived(R.qA.at[1 - h, :, at, :], K.gy_s, piece)
            dp_a_start(1 - h, piece)

    def self_dx(i):
        j = lax.rem(i, 2)
        b = jnp.where(i < 2, cp, c) + 2 * j
        y = mm_nt(R.dq[rows(b)], R.wself[h, 0])
        y = y + mm_nt(R.dkb[rows(b)], R.wself[h, 1])
        y = y + mm_nt(R.dvb[rows(b)], R.wself[h, 2])

        @pl.when(i < 2)
        def _():
            sent(R.cs.at[j], K.rs8, j)
            R.cs[j] = y.astype(BF16)
            send(R.cs.at[j], R.cr.at[j], K.rs9, core, j).start()

        @pl.when(i >= 2)
        def _():
            R.part[j] = y

    loop(4, self_dx)
    pass_a(2)

    def self_final(i):
        j = jnp.where(is_a, 1 - i, i)
        arrived(R.cr.at[j], K.rs9, j)
        x = R.xrow[rows(blk(j))].astype(F32)
        back, dgain, dbias = norm_back(x, gain(2 * h), R.part[j] + R.cr[j].astype(F32))
        add_norm(2 * h, dgain, dbias)

        @pl.when(is_a & (j == 0))
        def _():
            R.sgrad[...] = R.dmem[0] + back
            put_sgrad().start()

        @pl.when(is_a & (j == 1))
        def _():
            sent(R.fs, K.g3)
            R.fs[...] = (R.dmem[1] + back).astype(BF16)

        @pl.when(is_b & (j == 0))
        def _():
            sent(R.fs, K.br3)
            R.fs[...] = back.astype(BF16)

        @pl.when(is_b & (j == 1))
        def _():
            R.tgrad[...] = R.g3[...] + back
            put_tgrad().start()

    loop(2, self_final)

    send(R.acc, R.accc, K.accc, core).start()

    other_pieces()
    arrived(R.accc, K.accc)
    R.acc1[...] = R.acc[...] + R.accc[...]
    send(R.acc1, R.accy, K.accy, ypeer).start()
    send(R.fs, R.fr, K.fin, ypeer).start()
    pass_a(h)
    arrived(R.accy, K.accy)
    R.acc2[...] = R.acc1[...] + R.accy[...]
    R.stats[...] = R.acc2[16:32, :]
    put_stats().start()

    if inside:

        def tile_of(p):
            return lanes(lax.div(p * cw, LANES))

        def acc_copy(p):
            return send(R.acc2.at[0:16, tile_of(p)], R.accd.at[me], K.accd, (p, s))

        loop(nb, lambda i: acc_copy(to_peer(i)).start(), 1)
    pass_a(1 - h)
    arrived(R.fr, K.fin)

    @pl.when(is_a)
    def _():
        R.tgrad[...] = R.g3[...] + R.fr[...].astype(F32)
        put_tgrad().start()

    @pl.when(is_b)
    def _():
        R.sgrad[...] = R.fr[...].astype(F32)
        put_sgrad().start()

    if inside:
        arrived(R.accd.at[pl.ds(0, nb - 1)], K.accd)
        R.ggb[...] = R.acc2[0:16, tile_of(me)]

        def more(i):
            R.ggb[...] += R.accd[from_peer(i)]

        loop(nb, more, 1)
        put_ggb().start()
        for l in range(2):
            arrived(R.dpE.at[l, pl.ds(0, nb - 1)], K.gd_e, l)
            here_e(l).wait()
        for a in range(3):
            arrived(R.dpA.at[a, pl.ds(0, nb // 2 - 1)], K.gd_a, a)
            here_a(a).wait()
    else:
        R.gacc[...] = R.acc2[0:16, :]

    for copy in (put_dec, put_sgrad, put_tgrad, put_stats):
        copy().wait()
    if inside:
        put_ggb().wait()
        put_picks().wait()
    for name in (K.in_y, K.n4, K.b4, K.rs7q, K.fin):
        sent(R.oth, name)
    for name in (K.in_c, K.m_c, K.brow, K.rs9, K.n2, K.be):
        for j in range(2):
            sent(R.oth, name, j)
    for name in (K.b5, K.n5, K.rs5, K.rs6):
        for j in range(3):
            sent(R.oth, name, j)
    y_sent(other, K.wy_self, LANES)
    y_sent(R.wx, K.wy_x, LANES)
    y_grad_x().wait_send()
    for piece in range(2):
        y_grad_s(piece).wait_send()
    sent(R.acc, K.accc)
    sent(R.acc1, K.accy)

    @pl.when(is_a)
    def _():
        for j in range(2):
            sent(R.oth, K.dm, j)

    if inside:

        def drain_side(i):
            for a in range(3):
                sent(R.sendA.at[0], K.wa, a * (nb // 2) + i)
                sent(R.sendA.at[0], K.wr, a * (nb // 2) + i)

        loop(nb // 2, drain_side, 1)
        for a in range(3):
            sent(R.sendA.at[0], K.wa, a * (nb // 2))
            sent(R.dpA.at[a, pl.ds(0, nb // 2 - 1)], K.gd_a, a)
            for piece in range(2):
                sent(x_part(a, piece), K.gd_x, 2 * a + piece)
        for l in range(2):
            sent(R.dpE.at[l, pl.ds(0, nb - 1)], K.gd_e, l)
        sent(R.smallr.at[pl.ds(0, nb - 1)], K.small)
        sent(R.accd.at[pl.ds(0, nb - 1)], K.accd)


def close_kernel(cfg, names, *refs):
    nb, cw, B, D, FQ, E, _ = cfg
    R = SimpleNamespace(**dict(zip(names, refs, strict=True)))
    dp = lax.axis_index("dp")

    def copy(src, dst, i):
        return pltpu.make_async_copy(src, dst, R.sem.at[i])

    plain = [(R.z_dec, R.o_dec), (R.z_sgrad, R.o_sgrad), (R.z_tgrad, R.o_tgrad)]
    for i, (src, _) in enumerate(plain):
        copy(src, R.vp.at[i], i).start()
    for l in range(2):
        copy(R.dpE.at[l], R.ve.at[l], 3 + l).start()
    for a in range(3):
        copy(R.dpA.at[a], R.va.at[a], 5 + a).start()

    stats = jnp.sum(R.z_stats[...], -1, keepdims=True) * (1.0 / (4 * B * D))
    root = jnp.broadcast_to(jnp.sqrt(stats), (16, LANES))
    place = lax.broadcasted_iota(jnp.int32, (16, LANES), 0) - lax.broadcasted_iota(jnp.int32, (16, LANES), 1)
    for k in range(2):
        line = jnp.sum(jnp.where(place == 5 * k, root, 0.0), 0, keepdims=True)
        R.o_rms[0, k:k + 1, :] = line[:, 0:5]
    for k in range(LANES // cw):

        @pl.when(lax.rem(dp, LANES // cw) == k)
        def _(k=k):
            R.o_gain[...] = R.z_ggb[0:5, k * cw:(k + 1) * cw]
            R.o_bias[...] = R.z_ggb[5:10, k * cw:(k + 1) * cw]

    for i, (src, dst) in enumerate(plain):
        copy(src, R.vp.at[i], i).wait()
        copy(R.vp.at[i], dst, i).start()
    for l in range(2):
        copy(R.dpE.at[l], R.ve.at[l], 3 + l).wait()
        R.w_up[l] = jnp.zeros((E, cw, FQ), F32)
        R.w_dn[l] = jnp.zeros((E, cw, FQ), F32)
        for p in range(nb):
            e = jnp.max(R.z_picks[p, 10 + l:11 + l, :]).astype(jnp.int32)
            R.w_up[l, pl.ds(e, 1)] += R.ve[l, p, 0].astype(F32)[None]
            R.w_dn[l, pl.ds(e, 1)] += R.ve[l, p, 1].astype(F32)[None]
        copy(R.w_up.at[l], R.o_up.at[l], 8 + l).start()
        copy(R.w_dn.at[l], R.o_dn.at[l], 10 + l).start()
    for a in range(3):
        copy(R.dpA.at[a], R.va.at[a], 5 + a).wait()
        for m in range(4):
            total = R.va[a, 0, m].astype(F32)
            for p in range(1, nb // 2):
                total = total + R.va[a, p, m].astype(F32)
            if m < 3:
                R.w_qkv[a, m] = total
            else:
                R.w_out[a] = total
    copy(R.w_qkv, R.o_qkv, 12).start()
    copy(R.w_out, R.o_out, 13).start()
    for i, (_, dst) in enumerate(plain):
        copy(R.vp.at[i], dst, i).wait()
    for l in range(2):
        copy(R.w_up.at[l], R.o_up.at[l], 8 + l).wait()
        copy(R.w_dn.at[l], R.o_dn.at[l], 10 + l).wait()
    copy(R.w_qkv, R.o_qkv, 12).wait()
    copy(R.w_out, R.o_out, 13).wait()


def on_device(
    src_input,
    tgt_input,
    out_cotangent,
    src_lengths,
    tgt_lengths,
    enc_expert,
    dec_expert,
    norm_gains,
    norm_biases,
    qkv_weight,
    out_weight,
    expert_up,
    expert_down,
):
    n = lax.axis_size("dp")
    B, D = src_input.shape[1:]
    cw = norm_gains.shape[1]
    FQ = expert_up.shape[3]
    E = expert_up.shape[1]
    inside = cw % 16 == 0 and LANES % cw == 0 and n % 4 == 0 and n & (n - 1) == 0
    wot = jnp.swapaxes(out_weight, 1, 2)
    dnt = jnp.swapaxes(expert_down, 2, 3)
    vmem = pl.BlockSpec(memory_space=pltpu.VMEM)
    smem = pl.BlockSpec(memory_space=pltpu.SMEM)
    anywhere = pl.BlockSpec(memory_space=pl.ANY)

    def f32(*shape):
        return jax.ShapeDtypeStruct(shape, F32)

    def bf16(*shape):
        return jax.ShapeDtypeStruct(shape, BF16)

    scalars = dict(slen=src_lengths, tlen=tgt_lengths)
    operands = dict(src=src_input[0], tgt=tgt_input[0], cot=out_cotangent[0])
    results = {}
    far = dict(z_dec=f32(B, D), z_sgrad=f32(B, D), z_tgrad=f32(B, D), z_stats=f32(16, D))
    if inside:
        nb, rowsize = n, cw
        scalars.update(epick=enc_expert, dpick=dec_expert)
        operands.update(gains=norm_gains, biases=norm_biases, qkv=qkv_weight, wot=wot, up=expert_up, dnt=dnt)
        far.update(z_ggb=f32(16, LANES), z_picks=f32(n, 16, LANES))
        far.update(dpA=bf16(3, n // 2, 4, cw, LANES), dpE=bf16(2, n, 2, cw, FQ))
    else:
        nb, rowsize = 1, D
        gb = jnp.concatenate([norm_gains, norm_biases], 0).astype(F32)
        small = lax.all_gather(gb, "dp", axis=1, tiled=True)
        small = jnp.concatenate([small, jnp.zeros((6, D), F32)], 0)
        wa = jnp.concatenate([qkv_weight, wot[:, None]], 1)
        wa = lax.all_gather(wa, "dp", axis=2, tiled=True)
        picks = jnp.stack([enc_expert[0, 0], dec_expert[0, 0]])
        we = jnp.stack([expert_up, dnt], 2)
        we = lax.all_gather(we, "dp", axis=3, tiled=True)
        we = jnp.stack([jnp.take(we[l], picks[l], axis=0) for l in range(2)])
        operands.update(small=small, wa=wa, we=we)
        results.update(qA=bf16(3, 4, D, LANES), qE=bf16(2, 2, D, FQ), gacc=f32(16, D))
    cfg = (nb, rowsize, B, D, FQ, E, inside)
    scratch = scratch_list(nb, rowsize, B, D, FQ, inside)
    count = sem_list(nb)[1]
    scratch.update(ss=pltpu.SemaphoreType.DMA((count,)), rs=pltpu.SemaphoreType.DMA((count,)))
    names = tuple(scalars) + tuple(operands) + tuple(results) + tuple(far) + tuple(scratch)
    outs = pl.pallas_call(
        functools.partial(step_kernel, cfg, names),
        name="step",
        out_shape=tuple(results.values()) + tuple(far.values()),
        in_specs=[smem] * len(scalars) + [vmem] * len(operands),
        out_specs=[vmem] * len(results) + [anywhere] * len(far),
        scratch_shapes=list(scratch.values()),
        compiler_params=pltpu.CompilerParams(
            collective_id=1, has_side_effects=True, vmem_limit_bytes=63 << 20
        ),
        cost_estimate=pl.CostEstimate(flops=17 << 30, bytes_accessed=8 << 20, transcendentals=16 << 20),
    )(*scalars.values(), *operands.values())
    made = dict(zip(tuple(results) + tuple(far), outs, strict=True))
    if inside:
        near = dict(z_stats=vmem, z_ggb=vmem, z_picks=vmem, z_dec=anywhere, z_sgrad=anywhere, z_tgrad=anywhere)
        near.update(dpA=anywhere, dpE=anywhere)
        last = dict(
            o_dec=f32(B, D),
            o_sgrad=f32(B, D),
            o_tgrad=f32(B, D),
            o_gain=f32(5, cw),
            o_bias=f32(5, cw),
            o_qkv=f32(3, 3, cw, LANES),
            o_out=f32(3, cw, LANES),
            o_up=f32(2, E, cw, FQ),
            o_dn=f32(2, E, cw, FQ),
            o_rms=f32(1, 2, 5),
        )
        held = dict(
            vp=pltpu.VMEM((3, B, D), F32),
            ve=pltpu.VMEM((2, n, 2, cw, FQ), BF16),
            va=pltpu.VMEM((3, n // 2, 4, cw, LANES), BF16),
            w_up=pltpu.VMEM((2, E, cw, FQ), F32),
            w_dn=pltpu.VMEM((2, E, cw, FQ), F32),
            w_qkv=pltpu.VMEM((3, 3, cw, LANES), F32),
            w_out=pltpu.VMEM((3, cw, LANES), F32),
            sem=pltpu.SemaphoreType.DMA((14,)),
        )
        small_outs = [k in (3, 4, 9) for k in range(len(last))]
        dec, sgrad, tgrad, gains, biases, gqkv, gout, gup, gdn, rms = pl.pallas_call(
            functools.partial(close_kernel, cfg, tuple(near) + tuple(last) + tuple(held)),
            name="close",
            out_shape=tuple(last.values()),
            in_specs=list(near.values()),
            out_specs=[vmem if near_by else anywhere for near_by in small_outs],
            scratch_shapes=list(held.values()),
            compiler_params=pltpu.CompilerParams(vmem_limit_bytes=63 << 20),
            cost_estimate=pl.CostEstimate(flops=16 << 20, bytes_accessed=10 << 20, transcendentals=0),
        )(*[made[name] for name in near])
    else:
        ga, ge, gacc, dec, sgrad, tgrad, stats = outs

        def total(x, axis):
            return lax.psum_scatter(x, "dp", scatter_dimension=axis, tiled=True)

        gains, biases = total(gacc[0:5], 1), total(gacc[5:10], 1)
        ga = total(ga.astype(F32), 2)
        gqkv, gout = ga[:, :3], ga[:, 3]
        match = (picks[:, None] == jnp.arange(E, dtype=jnp.int32)[None]).astype(F32)
        ge = ge.astype(F32)[:, None] * match[:, :, None, None, None]
        ge = total(ge, 3)
        gup, gdn = ge[:, :, 0], ge[:, :, 1]
        length = B * lax.axis_size("seq")
        rms = jnp.sqrt(jnp.sum(stats[:10], 1) / (length * D)).reshape(1, 2, 5)
    return (
        dec[None],
        sgrad[None],
        tgrad[None],
        gains,
        biases,
        gqkv,
        jnp.swapaxes(gout, 1, 2),
        gup,
        jnp.swapaxes(gdn, 2, 3),
        rms,
    )


def solution(mesh):
    placed = (
        P("dp", "seq", None),
        P("dp", "seq", None),
        P("dp", "seq", None),
        P("dp", None),
        P("dp", None),
        P("dp", None),
        P("dp", None),
        P(None, "dp"),
        P(None, "dp"),
        P(None, None, "dp", "seq"),
        P(None, "seq", "dp"),
        P(None, None, "dp", "seq"),
        P(None, None, "seq", "dp"),
    )
    return jax.shard_map(
        on_device,
        mesh=mesh,
        in_specs=placed,
        out_specs=(
            P("dp", "seq", None),
            P("dp", "seq", None),
            P("dp", "seq", None),
            P(None, "dp"),
            P(None, "dp"),
            P(None, None, "dp", "seq"),
            P(None, "seq", "dp"),
            P(None, None, "dp", "seq"),
            P(None, None, "seq", "dp"),
            P("dp", None, None),
        ),
        check_vma=False,
    )
```
